32 devices in a mesh: ctx: 4 (over y, x), ch: 8 (over z, core).
Axes of the slice: x: 2, y: 2, z: 4, core: 2. Of those that a mesh axis runs over, the one named last changes fastest.
Arguments:
- hidden_in: bfloat16 [4096, 1024], P(('ctx', 'ch')), may hold values from -6 to 6
- norm_gain: float32 [1024], replicated, may hold values from 0.1 to 1.9
- in_weight: bfloat16 [1024, 4096], P('ch'), may hold values from -0.1875 to 0.1875
- conv_weight: float32 [2048, 4], replicated, may hold values from -2 to 2
- conv_bias: float32 [2048], replicated, may hold values from -2 to 2
- x_weight: bfloat16 [2048, 96], replicated, may hold values from -0.25 to 0.25
- dt_weight: bfloat16 [64, 2048], P(None, 'ch'), may hold values from -0.75 to 0.75
- dt_bias: float32 [2048], P('ch'), may hold values from -8.5 to -2.5
- a_log: float32 [2048, 16], P('ch'), may hold values from 0 to 2.77
- skip: float32 [2048], P('ch'), may hold values from 0.5 to 1.5
- out_weight: bfloat16 [2048, 1024], P('ch'), may hold values from -0.25 to 0.25
- lengths: int32 [4, 4], P('ctx'), may hold values from 1 to 1021, as said below
- resets: int32 [4096], P('ctx'), may hold values from 0 to 1, as said below
- out_grad: bfloat16 [4096, 1024], P(('ctx', 'ch')), may hold values from -6 to 6
Outputs:
- output: bfloat16 [4096, 1024], P(('ctx', 'ch'))
- d_hidden: bfloat16 [4096, 1024], P(('ctx', 'ch'))
- d_norm_gain: float32 [1024], P('ch')
- d_in_weight: float32 [1024, 4096], P('ch')
- d_conv_weight: float32 [2048, 4], P('ch')
- d_conv_bias: float32 [2048], P('ch')
- d_x_weight: float32 [2048, 96], P('ch')
- d_dt_weight: float32 [64, 2048], P(None, 'ch')
- d_dt_bias: float32 [2048], P('ch')
- d_a_log: float32 [2048, 16], P('ch')
- d_skip: float32 [2048], P('ch')
- d_out_weight: float32 [2048, 1024], P('ch')
The draws below stay inside these ranges and needn't reach their ends.
Inputs may be any that keep to these rules, and one draw needn't show every extreme that they name: Each row lists the context lengths of one group in order and sums to 1024; the second context of a group is its longest. `resets`: 1 marks a token where the scan state is zeroed.
All inputs are finite; a program needn't handle non-finite values.
Results may differ from the reference program's by a relative error of at most 0.012.
The reference program's roundings to bfloat16 on the way count: a program that leaves them out, or rounds other values in their place, can miss the bound.
Values may be sent and summed in bfloat16 or wider, within the bound.
No kernel may reach another device: no remote copies, remote signals or barrier semaphores. Data moves between devices by JAX's collectives and lax.ppermute only.
A program may use at most 256 MiB of HBM per device.

```python
import math
import jax
import jax.numpy as jnp
from jax import lax

D = 1024
E = 2048
N = 16
K = 4
R = 64
TOK_DEV = 128
GROUP_TOK = 1024
TOKENS = 4096
N_CTX = 4


def draw_lengths(key, part):
    key = jax.random.fold_in(key, 7)
    upper = max(2, TOK_DEV // 6) + 1
    short = jax.random.randint(key, (N_CTX, 3), 1, upper, dtype=jnp.int32)
    chosen = jax.random.randint(jax.random.fold_in(key, 11), (), 0, N_CTX, dtype=jnp.int32)
    rows = jnp.arange(N_CTX, dtype=jnp.int32)[:, None]
    short = jnp.where(rows == chosen, jnp.ones_like(short), short).astype(jnp.int32)
    longest = GROUP_TOK - jnp.sum(short, axis=1, keepdims=True)
    return jnp.concatenate([short[:, :1], longest, short[:, 1:]], axis=1).astype(jnp.int32)


def draw_resets(key, part):
    key = jax.random.fold_in(key, 13)
    marks = jax.random.randint(key, (N_CTX, 4, 1), 1, GROUP_TOK, dtype=jnp.int32)
    places = jnp.arange(GROUP_TOK, dtype=jnp.int32)[None, None, :]
    hits = jnp.max(jnp.where(marks == places, 1, 0), axis=1)
    return hits.reshape(TOKENS).astype(jnp.int32)


def levels(stream_key, extent, shards, low, largest):
    def one(position, blocks):
        draws = jax.random.uniform(jax.random.fold_in(jax.random.fold_in(stream_key, 6), position), (blocks,), jnp.float32, low / len(shards), largest / len(shards))
        return jnp.repeat(jnp.exp(draws), extent[position] // blocks).reshape((-1,) + (1,) * (len(extent) - position - 1))

    level = one(*shards[0])
    for cut in shards[1:]:
        level = level * one(*cut)
    return level


def scatter_about(own_key, shape, width, most, shards=(), kind=jnp.bfloat16):
    level = levels(own_key, shape, shards, -0.22, 0.18) if shards else 1.0
    array = jax.random.normal(own_key, shape, jnp.float32) * width * level
    return jnp.minimum(jnp.maximum(array, -most), most).astype(kind)


def setup_inputs(seed: int = 0) -> dict:
    keys = jax.random.split(jax.random.key(seed), 15)
    hidden_in = scatter_about(keys[0], (TOKENS, D), 1.0, 6.0, ((0, 32),))
    norm_gain = jnp.clip(1.0 + 0.18 * jax.random.normal(keys[1], (D,), jnp.float32), 0.1, 1.9)
    in_weight = scatter_about(keys[2], (D, 2 * E), D ** -0.5, 0.1875, ((0, 8),))
    conv_weight = scatter_about(keys[3], (E, K), 0.5, 2.0, (), jnp.float32)
    conv_bias = scatter_about(keys[4], (E,), 0.5, 2.0, (), jnp.float32)
    x_weight = scatter_about(keys[5], (E, R + 2 * N), (E // 4) ** -0.5, 0.25)
    dt_weight = scatter_about(keys[6], (R, E), R ** -0.5, 0.75, ((1, 8),))
    dt_bias = jnp.clip(-8.5 + 6.0 * jax.random.uniform(keys[7], (E,), jnp.float32) ** levels(keys[7], (E,), ((0, 8),), -0.2, 0.2), -8.5, -2.5)
    a_log = jnp.clip(2.77 * jax.random.uniform(keys[8], (E, N), jnp.float32) ** levels(keys[8], (E, N), ((0, 8),), -0.2, 0.2), 0.0, 2.77)
    skip = jnp.clip(0.5 + 1.0 * jax.random.uniform(keys[9], (E,), jnp.float32) ** levels(keys[9], (E,), ((0, 8),), -0.2, 0.2), 0.5, 1.5)
    out_weight = scatter_about(keys[10], (E, D), (E // 4) ** -0.5, 0.25, ((0, 8),))
    lengths = draw_lengths(jax.random.fold_in(keys[14], 71), 0)
    resets = draw_resets(jax.random.fold_in(keys[14], 71), 0)
    out_grad = scatter_about(keys[13], (TOKENS, D), 1.0, 6.0, ((0, 32),))
    return {"hidden_in": hidden_in, "norm_gain": norm_gain, "in_weight": in_weight, "conv_weight": conv_weight, "conv_bias": conv_bias, "x_weight": x_weight, "dt_weight": dt_weight, "dt_bias": dt_bias, "a_log": a_log, "skip": skip, "out_weight": out_weight, "lengths": lengths, "resets": resets, "out_grad": out_grad}


HIGH = lax.Precision.HIGHEST
eps = 1e-05

@jax.custom_vjp
def low(v):
    return lax.optimization_barrier(v.astype(jnp.bfloat16)).astype(jnp.float32)

@jax.custom_vjp
def low_back(v):
    return v

def low_keep(v):
    return (low(v), None)

def low_pass(kept, grad):
    return (grad,)

def back_keep(v):
    return (v, None)

def back_low(kept, grad):
    return (low(grad),)
low.defvjp(low_keep, low_pass)
low_back.defvjp(back_keep, back_low)

def silu(v):
    return v * jax.nn.sigmoid(v)

def context_pos(lengths, total):
    offsets = (jnp.cumsum(lengths) - lengths).astype(jnp.int32)
    places = jnp.arange(total, dtype=jnp.int32)
    begins = lax.optimization_barrier(jnp.max(jnp.where(offsets[:, None] <= places[None, :], offsets[:, None], 0), axis=0)).astype(jnp.int32)
    return places - begins

def delay_rows(v, steps):
    if steps == 0:
        return v
    return jnp.concatenate([jnp.zeros((steps,) + v.shape[1:], v.dtype), v[:v.shape[0] - steps]], axis=0)

def run_scan(delta, values, b_in, c_out, keep, rates):
    total = delta.shape[0]
    size = math.gcd(total, 1024)
    count = total // size

    def token_step(state, item):
        d_t, v_t, b_t, c_t, k_t = item
        state = jnp.exp(d_t[:, None] * rates) * k_t * state + (d_t * v_t)[:, None] * b_t[None, :]
        return (state, lax.optimization_barrier(jnp.sum(state * c_t[None, :], axis=1)))

    @jax.checkpoint
    def block_step(state, items):
        return lax.scan(token_step, state, items)
    items = tuple((a.reshape((count, size) + a.shape[1:]) for a in (delta, values, b_in, c_out, keep)))
    start = jnp.zeros((delta.shape[1], b_in.shape[1]), delta.dtype)
    _, outputs = lax.scan(block_step, start, items)
    return outputs.reshape(total, delta.shape[1])

def group_forward(params, hidden, lengths, resets):
    gain, in_weight, conv_weight, conv_bias, x_weight, dt_weight, dt_bias, a_log, skip, out_weight = params
    scale = lax.rsqrt(lax.optimization_barrier(jnp.mean(hidden * hidden, axis=1, keepdims=True)) + eps)
    normed = low(hidden * scale * gain[None, :])
    mixed = jnp.dot(normed, in_weight, precision=HIGH)
    inner = in_weight.shape[1] // 2
    x_in = low_back(low(mixed[:, :inner]))
    gate = low_back(low(mixed[:, inner:]))
    total = hidden.shape[0]
    where_in = context_pos(lengths, total)
    taps = conv_weight.shape[1]
    pre = conv_bias[None, :] + jnp.zeros_like(x_in)
    for k in range(taps):
        lag = taps - 1 - k
        valid = (where_in >= lag).astype(hidden.dtype)
        pre = pre + conv_weight[:, k][None, :] * delay_rows(x_in, lag) * valid[:, None]
    values = low(silu(pre))
    proj = low_back(low(jnp.dot(values, x_weight, precision=HIGH)))
    rank = dt_weight.shape[0]
    states_n = a_log.shape[1]
    dt_low = proj[:, :rank]
    b_in = proj[:, rank:rank + states_n]
    c_out = proj[:, rank + states_n:]
    delta = jax.nn.softplus(jnp.dot(dt_low, dt_weight, precision=HIGH) + dt_bias[None, :])
    rates = -jnp.exp(a_log)
    keep = jnp.where((where_in == 0) | (resets == 1), 0.0, 1.0).astype(hidden.dtype)
    scanned = run_scan(delta, values, b_in, c_out, keep, rates) + skip[None, :] * values
    gated = low_back(low(scanned * silu(gate)))
    return hidden + jnp.dot(gated, out_weight, precision=HIGH)

def reference(hidden_in, norm_gain, in_weight, conv_weight, conv_bias, x_weight, dt_weight, dt_bias, a_log, skip, out_weight, lengths, resets, out_grad):
    params = tuple((p.astype(jnp.float32) for p in (norm_gain, in_weight, conv_weight, conv_bias, x_weight, dt_weight, dt_bias, a_log, skip, out_weight)))
    hidden = hidden_in.astype(jnp.float32).reshape(N_CTX, GROUP_TOK, D)
    marks = resets.reshape(N_CTX, GROUP_TOK)

    def forward(weights, inputs):

        def one_group(item):
            rows, sizes, flags = item
            return jax.checkpoint(group_forward)(weights, rows, sizes, flags)
        return lax.map(one_group, (inputs, lengths, marks))
    result, pullback = jax.vjp(forward, params, hidden)
    grads, d_input = pullback(out_grad.astype(jnp.float32).reshape(N_CTX, GROUP_TOK, D))
    return (result.reshape(TOKENS, D).astype(jnp.bfloat16), d_input.reshape(TOKENS, D).astype(jnp.bfloat16), grads[0], grads[1], grads[2], grads[3], grads[4], grads[5], grads[6], grads[7], grads[8], grads[9])
```

```python
import functools
import math

import jax
import jax.numpy as jnp
from jax import lax
from jax.experimental import pallas as pl
from jax.experimental.pallas import tpu as pltpu
from jax.sharding import PartitionSpec as P

HIGH = lax.Precision.HIGHEST
f32 = jnp.float32
bf16 = jnp.bfloat16
eps = 1e-05
LOG2E = 1.4426950408889634
CUT = 1e30
SEGS = 8
MIB = 1 << 20


def silu(v):
    return v * jax.nn.sigmoid(v)


def silu_slope(v):
    sig = jax.nn.sigmoid(v)
    return sig * (1.0 + v * (1.0 - sig))


def context_place(offsets, places):
    begins = jnp.max(jnp.where(offsets[:, None] <= places[None, :], offsets[:, None], 0), axis=0)
    return places - begins


def dot(a, b, dims, precision=None):
    return lax.dot_general(a, b, ((dims[:1], dims[1:]), ((), ())), precision=precision, preferred_element_type=f32)


def lane_groups(chans):
    width = 128 if chans % 128 == 0 else chans
    return chans // width, width


def softplus(v):
    small = jnp.exp(-jnp.abs(v))
    series = small * (1.0 - small * (0.5 - small * (1.0 / 3.0)))
    return jnp.maximum(v, 0.0) + jnp.where(small < 0.01, series, jnp.log(1.0 + small))


def by_rows(total, body):
    size = math.gcd(total, 256)

    def step(k, carry):
        body(pl.ds(pl.multiple_of(k * size, size), size))
        return carry

    lax.fori_loop(0, total // size, step, 0)


def step_params(proj_ref, dtw_ref, dtb_ref, rank, rows):
    return dot(proj_ref[rows, :rank], dtw_ref[...], (1, 0)) + dtb_ref[...]


def put(ref, rows, value, groups, width):
    for g in range(groups):
        ref[g, rows, :] = value[:, g * width : (g + 1) * width]


def take(ref, rows, groups):
    return jnp.concatenate([ref[g, rows, :] for g in range(groups)], axis=1) if groups > 1 else ref[0, rows, :]


def rows_at(ref, g, i, steps):
    return ref[g, pl.ds(i, SEGS, stride=steps), :]


def forward_kernel(
    rank, states, span, proj_ref, val_ref, gate_ref, dg_ref, dtw_ref, dtb_ref, alog_ref, skip_ref,
    gated_ref, dgate_ref, hist_ref, dc_ref, dskip_ref,
    s_cut, s_dx, s_dy, s_bc, s_rate, s_state,
):
    total, chans = val_ref.shape
    steps = total // SEGS
    groups, width = lane_groups(chans)
    pairs = [(n, g) for n in range(states) for g in range(groups)]
    b_at, c_at = rank, rank + states
    turn = pl.program_id(0)

    def rate(n, g):
        return s_rate[n : n + 1, g * width : (g + 1) * width]

    @pl.when(turn == 0)
    def _():
        s_rate[...] = -jnp.exp(alog_ref[...]) * LOG2E

        def fill(rows):
            delta = softplus(step_params(proj_ref, dtw_ref, dtb_ref, rank, rows))
            wide = proj_ref[rows, :].astype(f32)
            s_bc[0, rows, :] = wide
            cut = wide[:, rank + 2 * states : rank + 2 * states + 1] * CUT
            put(s_cut, rows, delta + cut, groups, width)
            put(s_dx, rows, delta * val_ref[rows, :].astype(f32), groups, width)
            d_scan = dg_ref[rows, :].astype(f32) * silu(gate_ref[rows, :].astype(f32))
            put(s_dy, rows, d_scan, groups, width)

        by_rows(total, fill)

        def sweep(i, carry):
            held, span_sum = carry
            cuts = [rows_at(s_cut, g, i, steps) for g in range(groups)]
            dxs = [rows_at(s_dx, g, i, steps) for g in range(groups)]
            bc = rows_at(s_bc, 0, i, steps)
            out = []
            for n, g in pairs:
                push = dxs[g] * bc[:, b_at + n : b_at + n + 1]
                out.append(jnp.exp2(cuts[g] * rate(n, g)) * held[n * groups + g] + push)
            return tuple(out), tuple(span_sum[g] + cuts[g] for g in range(groups))

        zero = jnp.zeros((SEGS, width), f32)
        ends, sums = lax.fori_loop(0, steps, sweep, ((zero,) * len(pairs), (zero,) * groups))
        first = lax.broadcasted_iota(jnp.int32, (SEGS, width), 0) == 0
        for n, g in pairs:
            gain = jnp.exp2(sums[g] * rate(n, g))
            end = ends[n * groups + g]
            start = zero
            for _ in range(SEGS - 1):
                start = jnp.where(first, 0.0, pltpu.roll(gain * start + end, 1, 0))
            s_state[n * groups + g] = start

    lane = lax.broadcasted_iota(jnp.int32, (SEGS, dc_ref.shape[1]), 1)

    def sweep(k, held):
        i = turn * span + k
        cuts = [rows_at(s_cut, g, i, steps) for g in range(groups)]
        dxs = [rows_at(s_dx, g, i, steps) for g in range(groups)]
        dys = [rows_at(s_dy, g, i, steps) for g in range(groups)]
        bc = rows_at(s_bc, 0, i, steps)
        ys = [jnp.zeros((SEGS, width), f32) for _ in range(groups)]
        dc_row = jnp.zeros(lane.shape, f32)
        out = []
        for n in range(states):
            b_n = bc[:, b_at + n : b_at + n + 1]
            c_n = bc[:, c_at + n : c_at + n + 1]
            mix = None
            for g in range(groups):
                old = held[n * groups + g]
                hist_ref[k, n * groups + g] = old
                new = jnp.exp2(cuts[g] * rate(n, g)) * old + dxs[g] * b_n
                out.append(new)
                ys[g] = ys[g] + new * c_n
                term = dys[g] * new
                mix = term if mix is None else mix + term
            dc_row = jnp.where(lane == c_at + n, jnp.sum(mix, axis=1, keepdims=True), dc_row)
        for g in range(groups):
            s_dx[g, pl.ds(i, SEGS, stride=steps), :] = ys[g]
        dc_ref[pl.ds(i, SEGS, stride=steps), :] = dc_row
        return tuple(out)

    held = lax.fori_loop(0, span, sweep, tuple(s_state[j] for j in range(len(pairs))))
    for j in range(len(pairs)):
        s_state[j] = held[j]

    @pl.when(turn == pl.num_programs(0) - 1)
    def _():
        dskip_ref[...] = jnp.zeros_like(dskip_ref)

        def finish(rows):
            vals = val_ref[rows, :].astype(f32)
            gate = gate_ref[rows, :].astype(f32)
            scanned = take(s_dx, rows, groups) + skip_ref[...] * vals
            gated_ref[rows, :] = (scanned * silu(gate)).astype(bf16)
            dgate_ref[rows, :] = (dg_ref[rows, :].astype(f32) * scanned * silu_slope(gate)).astype(bf16)
            dskip_ref[...] += jnp.sum(take(s_dy, rows, groups) * vals, axis=0, keepdims=True)

        by_rows(total, finish)


def backward_kernel(
    rank, states, span, proj_ref, val_ref, gate_ref, dg_ref, dtw_ref, dtwt_ref, dtb_ref, alog_ref, skip_ref, hist_ref,
    dc_ref, part_ref, dval_ref, ddtw_ref, ddtb_ref, dalog_ref,
    s_cut, s_delta, s_val, s_dy, s_bc, s_rate, s_state, s_drate,
):
    total, chans = val_ref.shape
    steps = total // SEGS
    groups, width = lane_groups(chans)
    pairs = [(n, g) for n in range(states) for g in range(groups)]
    b_at, c_at = rank, rank + states
    turn = pl.program_id(0)
    turns = pl.num_programs(0)

    def rate(n, g):
        return s_rate[n : n + 1, g * width : (g + 1) * width]

    @pl.when(turn == 0)
    def _():
        s_rate[...] = -jnp.exp(alog_ref[...]) * LOG2E
        s_drate[...] = jnp.zeros_like(s_drate)

        def fill(rows):
            delta = softplus(step_params(proj_ref, dtw_ref, dtb_ref, rank, rows))
            wide = proj_ref[rows, :].astype(f32)
            s_bc[0, rows, :] = wide
            cut = wide[:, rank + 2 * states : rank + 2 * states + 1] * CUT
            put(s_cut, rows, delta + cut, groups, width)
            put(s_delta, rows, delta, groups, width)
            put(s_val, rows, val_ref[rows, :].astype(f32), groups, width)
            d_scan = dg_ref[rows, :].astype(f32) * silu(gate_ref[rows, :].astype(f32))
            put(s_dy, rows, d_scan, groups, width)

        by_rows(total, fill)

        def sweep(k, carry):
            i = steps - 1 - k
            held, span_sum = carry
            cuts = [rows_at(s_cut, g, i, steps) for g in range(groups)]
            dys = [rows_at(s_dy, g, i, steps) for g in range(groups)]
            bc = rows_at(s_bc, 0, i, steps)
            out = []
            for n, g in pairs:
                lam = dys[g] * bc[:, c_at + n : c_at + n + 1] + held[n * groups + g]
                out.append(jnp.exp2(cuts[g] * rate(n, g)) * lam)
            return tuple(out), tuple(span_sum[g] + cuts[g] for g in range(groups))

        zero = jnp.zeros((SEGS, width), f32)
        ends, sums = lax.fori_loop(0, steps, sweep, ((zero,) * len(pairs), (zero,) * groups))
        last = lax.broadcasted_iota(jnp.int32, (SEGS, width), 0) == SEGS - 1
        for n, g in pairs:
            gain = jnp.exp2(sums[g] * rate(n, g))
            end = ends[n * groups + g]
            start = zero
            for _ in range(SEGS - 1):
                start = jnp.where(last, 0.0, pltpu.roll(gain * start + end, SEGS - 1, 0))
            s_state[n * groups + g] = start

    lane = lax.broadcasted_iota(jnp.int32, (SEGS, part_ref.shape[1]), 1)

    def sweep(back, held):
        k = span - 1 - back
        i = (turns - 1 - turn) * span + k
        cuts = [rows_at(s_cut, g, i, steps) for g in range(groups)]
        deltas = [rows_at(s_delta, g, i, steps) for g in range(groups)]
        vals = [rows_at(s_val, g, i, steps) for g in range(groups)]
        dys = [rows_at(s_dy, g, i, steps) for g in range(groups)]
        dxs = [deltas[g] * vals[g] for g in range(groups)]
        bc = rows_at(s_bc, 0, i, steps)
        zero = jnp.zeros((SEGS, width), f32)
        by_rate = [zero] * groups
        by_b = [zero] * groups
        db_row = jnp.zeros(lane.shape, f32)
        out = []
        for n in range(states):
            b_n = bc[:, b_at + n : b_at + n + 1]
            c_n = bc[:, c_at + n : c_at + n + 1]
            mix = None
            for g in range(groups):
                j = n * groups + g
                lam = dys[g] * c_n + held[j]
                onward = jnp.exp2(cuts[g] * rate(n, g)) * lam
                out.append(onward)
                through = onward * hist_ref[k, j]
                by_rate[g] = by_rate[g] + through * rate(n, g)
                by_b[g] = by_b[g] + lam * b_n
                s_drate[j] = s_drate[j] + through * deltas[g]
                term = lam * dxs[g]
                mix = term if mix is None else mix + term
            db_row = jnp.where(lane == b_at + n, jnp.sum(mix, axis=1, keepdims=True), db_row)
        for g in range(groups):
            skip = skip_ref[:, g * width : (g + 1) * width]
            here = pl.ds(i, SEGS, stride=steps)
            s_delta[g, here, :] = by_rate[g] * (1.0 / LOG2E) + by_b[g] * vals[g]
            dval_ref[g, here, :] = by_b[g] * deltas[g] + dys[g] * skip
        part_ref[pl.ds(i, SEGS, stride=steps), :] = db_row
        return tuple(out)

    held = lax.fori_loop(0, span, sweep, tuple(s_state[j] for j in range(len(pairs))))
    for j in range(len(pairs)):
        s_state[j] = held[j]

    @pl.when(turn == turns - 1)
    def _():
        ddtb_ref[...] = jnp.zeros_like(ddtb_ref)
        ddtw_ref[...] = jnp.zeros_like(ddtw_ref)

        def finish(rows):
            pre = step_params(proj_ref, dtw_ref, dtb_ref, rank, rows)
            d_pre = take(s_delta, rows, groups) * jax.nn.sigmoid(pre)
            ddtb_ref[...] += jnp.sum(d_pre, axis=0, keepdims=True)
            ddtw_ref[...] += dot(proj_ref[rows, :rank].astype(f32), d_pre, (0, 0), HIGH)
            part_ref[rows, :] += dot(d_pre, dtwt_ref[...].astype(f32), (1, 0), HIGH) + dc_ref[rows, :]

        by_rows(total, finish)
        sums = [jnp.sum(s_drate[j], axis=0, keepdims=True) for j in range(len(pairs))]
        rows = [jnp.concatenate(sums[n * groups : (n + 1) * groups], axis=1) for n in range(states)]
        dalog_ref[...] = jnp.concatenate(rows, axis=0) * s_rate[...] * (1.0 / LOG2E)


def padded(rows, lanes, size):
    return -(-rows // 16) * 16 * (-(-lanes // 128) * 128) * size


def scan_span(steps):
    return math.gcd(steps, 32)


def run_forward(proj, values, gate, d_gated, dt_weight, dt_bias, a_log_t, skip, states):
    total, chans = values.shape
    rank = dt_weight.shape[0]
    steps = total // SEGS
    span = scan_span(steps)
    groups, width = lane_groups(chans)
    count = states * groups
    whole = lambda *shape: pl.BlockSpec(shape, lambda t: (0,) * len(shape))
    lanes = proj.shape[1]
    need = 5 * padded(total, chans, 2) + 3 * padded(total, chans, 4) + 3 * padded(total, lanes, 4)
    need += 2 * span * count * 32 * 128 + 8 * MIB
    return pl.pallas_call(
        functools.partial(forward_kernel, rank, states, span),
        grid=(steps // span,),
        in_specs=[
            whole(total, lanes), whole(total, chans), whole(total, chans), whole(total, chans),
            whole(rank, chans), whole(1, chans), whole(states, chans), whole(1, chans),
        ],
        out_specs=[
            whole(total, chans), whole(total, chans),
            pl.BlockSpec((span, count, SEGS, width), lambda t: (t, 0, 0, 0)),
            whole(total, lanes), whole(1, chans),
        ],
        out_shape=[
            jax.ShapeDtypeStruct((total, chans), bf16), jax.ShapeDtypeStruct((total, chans), bf16),
            jax.ShapeDtypeStruct((steps, count, SEGS, width), f32),
            jax.ShapeDtypeStruct((total, lanes), f32), jax.ShapeDtypeStruct((1, chans), f32),
        ],
        scratch_shapes=[
            pltpu.VMEM((groups, total, width), f32), pltpu.VMEM((groups, total, width), f32),
            pltpu.VMEM((groups, total, width), f32), pltpu.VMEM((1, total, lanes), f32),
            pltpu.VMEM((states, chans), f32), pltpu.VMEM((count, SEGS, width), f32),
        ],
        compiler_params=pltpu.CompilerParams(vmem_limit_bytes=need),
        name="scan_forward",
    )(proj, values, gate, d_gated, dt_weight, dt_bias, a_log_t, skip)


def run_backward(proj, values, gate, d_gated, dt_weight, dt_weight_t, dt_bias, a_log_t, skip, hist, dc, states):
    total, chans = values.shape
    rank = dt_weight.shape[0]
    steps = total // SEGS
    span = scan_span(steps)
    groups, width = lane_groups(chans)
    count = states * groups
    whole = lambda *shape: pl.BlockSpec(shape, lambda t: (0,) * len(shape))
    lanes = proj.shape[1]
    turns = steps // span
    need = 3 * padded(total, chans, 2) + 5 * padded(total, chans, 4) + 4 * padded(total, lanes, 4)
    need += 2 * span * count * 32 * 128 + 8 * MIB
    return pl.pallas_call(
        functools.partial(backward_kernel, rank, states, span),
        grid=(turns,),
        in_specs=[
            whole(total, lanes), whole(total, chans), whole(total, chans), whole(total, chans),
            whole(rank, chans), whole(chans, lanes), whole(1, chans), whole(states, chans), whole(1, chans),
            pl.BlockSpec((span, count, SEGS, width), lambda t: (turns - 1 - t, 0, 0, 0)),
            whole(total, lanes),
        ],
        out_specs=[
            whole(total, lanes), whole(groups, total, width), whole(rank, chans), whole(1, chans), whole(states, chans),
        ],
        out_shape=[
            jax.ShapeDtypeStruct((total, lanes), f32), jax.ShapeDtypeStruct((groups, total, width), f32),
            jax.ShapeDtypeStruct((rank, chans), f32), jax.ShapeDtypeStruct((1, chans), f32),
            jax.ShapeDtypeStruct((states, chans), f32),
        ],
        scratch_shapes=[
            pltpu.VMEM((groups, total, width), f32), pltpu.VMEM((groups, total, width), f32),
            pltpu.VMEM((groups, total, width), f32), pltpu.VMEM((groups, total, width), f32),
            pltpu.VMEM((1, total, lanes), f32), pltpu.VMEM((states, chans), f32),
            pltpu.VMEM((count, SEGS, width), f32), pltpu.VMEM((count, SEGS, width), f32),
        ],
        compiler_params=pltpu.CompilerParams(vmem_limit_bytes=need),
        name="scan_backward",
    )(proj, values, gate, d_gated, dt_weight, dt_weight_t, dt_bias, a_log_t, skip, hist, dc)


def shifted(array, steps):
    if steps == 0:
        return array
    zeros = jnp.zeros((abs(steps), array.shape[1]), array.dtype)
    if steps > 0:
        return jnp.concatenate([zeros, array[:-steps]], axis=0)
    return jnp.concatenate([array[-steps:], zeros], axis=0)


def sum_parts(array, axes, lead):
    got = lax.all_to_all(array, axes, split_axis=0, concat_axis=0, tiled=True)
    got = got.reshape((lead, got.shape[0] // lead) + got.shape[1:])
    return got.astype(f32).sum(axis=0)


def on_device(
    hidden_in, norm_gain, in_weight, conv_weight, conv_bias, x_weight, dt_weight, dt_bias, a_log, skip, out_weight,
    lengths, resets, out_grad,
):
    peers = lax.axis_size("ch")
    packs = lax.axis_size("ctx")
    me = lax.axis_index("ch")
    rows, width = hidden_in.shape
    chans = out_weight.shape[0]
    inner = chans * peers
    taps = conv_weight.shape[1]
    rank, states = dt_weight.shape[0], a_log.shape[1]
    total = rows * peers

    hidden_all = lax.all_gather(hidden_in, "ch", axis=0, tiled=True)
    in_rows = in_weight.shape[0]
    pieces = jnp.moveaxis(in_weight.reshape(in_rows, 2, peers, chans), 2, 0)
    my_cols = lax.all_to_all(pieces, "ch", split_axis=0, concat_axis=0, tiled=True).reshape(width, 2 * chans)
    grad_all = lax.all_gather(out_grad, "ch", axis=0, tiled=True)

    wide = hidden_all.astype(f32)
    scale_all = lax.rsqrt(jnp.mean(wide * wide, axis=1, keepdims=True) + eps)
    unit_all = wide * scale_all
    normed = (unit_all * norm_gain[None, :]).astype(bf16)
    mixed = dot(normed, my_cols, (1, 0)).astype(bf16)
    x_in, gate = mixed[:, :chans], mixed[:, chans:]

    sizes = lengths[0]
    offsets = jnp.cumsum(sizes) - sizes
    where_in = context_place(offsets, jnp.arange(total, dtype=jnp.int32))
    masks = [(where_in >= taps - 1 - k).astype(f32)[:, None] for k in range(taps)]
    cut = ((where_in == 0) | (resets == 1)).astype(bf16)[:, None]
    conv_w = lax.dynamic_slice_in_dim(conv_weight, me * chans, chans, 0)
    conv_b = lax.dynamic_slice_in_dim(conv_bias, me * chans, chans, 0)
    x_w = lax.dynamic_slice_in_dim(x_weight, me * chans, chans, 0)
    x_f = x_in.astype(f32)
    delayed = [shifted(x_f, taps - 1 - k) * masks[k] for k in range(taps)]
    pre = conv_b[None, :] + sum(conv_w[:, k][None, :] * delayed[k] for k in range(taps))
    values = silu(pre).astype(bf16)

    proj_part = dot(values, x_w, (1, 0)).astype(bf16)
    proj_own = sum_parts(proj_part, "ch", peers).astype(bf16)
    proj = lax.all_gather(proj_own, "ch", axis=0, tiled=True)
    low_cols = rank + 2 * states
    lanes = -(-(low_cols + 1) // 128) * 128
    proj_ext = jnp.concatenate([proj, cut, jnp.zeros((total, lanes - low_cols - 1), bf16)], axis=1)

    d_gated = dot(grad_all, out_weight, (1, 1)).astype(bf16)
    a_log_t = a_log.T
    dt_b, skip_row = dt_bias[None, :], skip[None, :]
    gated, d_gate, hist, dc, d_skip = run_forward(
        proj_ext, values, gate, d_gated, dt_weight, dt_b, a_log_t, skip_row, states
    )
    branch_part = dot(gated, out_weight, (1, 0)).astype(bf16)
    branch = lax.psum_scatter(branch_part, "ch", scatter_dimension=0, tiled=True)
    output = (hidden_in.astype(f32) + branch.astype(f32)).astype(bf16)
    d_out_weight = dot(gated, grad_all, (0, 0))

    dt_w_t = jnp.pad(dt_weight.T, ((0, 0), (0, lanes - rank)))
    d_part, value_part, d_dt_weight, d_dt_bias, d_a_log_t = run_backward(
        proj_ext, values, gate, d_gated, dt_weight, dt_w_t, dt_b, a_log_t, skip_row, hist, dc, states
    )
    d_proj_own = sum_parts(d_part[:, :low_cols].astype(bf16), "ch", peers).astype(bf16)
    d_proj = lax.all_gather(d_proj_own, "ch", axis=0, tiled=True)

    value_part = jnp.moveaxis(value_part, 0, 1).reshape(total, chans)
    d_values = value_part + dot(d_proj, x_w, (1, 1))
    d_x_weight = dot(values, d_proj, (0, 0))
    d_pre = d_values * silu_slope(pre)
    d_conv_bias = jnp.sum(d_pre, axis=0)
    d_conv_weight = jnp.stack([jnp.sum(d_pre * delayed[k], axis=0) for k in range(taps)], axis=1)
    d_x = sum(conv_w[:, k][None, :] * shifted(d_pre * masks[k], k + 1 - taps) for k in range(taps))
    d_mixed = jnp.concatenate([d_x.astype(bf16), d_gate], axis=1)

    d_normed_part = dot(d_mixed, my_cols, (1, 1))
    d_normed = lax.psum_scatter(d_normed_part.astype(bf16), "ch", scatter_dimension=0, tiled=True).astype(f32)
    d_gain = jnp.sum(d_normed_part * unit_all, axis=0)
    d_in = dot(normed, d_mixed, (0, 0)).astype(bf16)

    hidden = hidden_in.astype(f32)
    scale = lax.rsqrt(jnp.mean(hidden * hidden, axis=1, keepdims=True) + eps)
    unit = hidden * scale
    d_unit = d_normed * norm_gain[None, :]
    d_hidden = (
        out_grad.astype(f32) + scale * (d_unit - unit * jnp.mean(d_unit * unit, axis=1, keepdims=True))
    ).astype(bf16)

    in_parts = jnp.moveaxis(d_in.reshape(peers, packs, in_rows // packs, 2 * chans), 1, 0)
    in_parts = in_parts.reshape(packs * peers, in_rows // packs, 2 * chans)
    in_own = sum_parts(in_parts, ("ctx", "ch"), packs).astype(bf16)
    in_own = jnp.transpose(in_own.reshape(peers, in_rows // packs, 2, chans), (1, 2, 0, 3))
    in_own = in_own.reshape(in_rows // packs, 2 * inner)
    in_sum = lax.all_gather(in_own, "ctx", axis=0, tiled=True).astype(f32)

    out_own = sum_parts(d_out_weight.astype(bf16), "ctx", packs).astype(bf16)
    out_sum = lax.all_gather(out_own, "ctx", axis=0, tiled=True).astype(f32)

    gain_own = sum_parts(d_gain.astype(bf16), "ch", peers)
    small = [
        gain_own, d_conv_weight, d_conv_bias, d_x_weight, d_dt_weight, d_dt_bias[0], d_a_log_t.T, d_skip[0],
    ]
    flat = jnp.concatenate([a.reshape(-1) for a in small]).astype(bf16)
    every = lax.all_gather(flat, "ctx", axis=0, tiled=False).astype(f32).sum(axis=0)
    sums = []
    at = 0
    for a in small:
        sums.append(every[at : at + a.size].reshape(a.shape))
        at += a.size
    gain_sum, conv_w_sum, conv_b_sum, x_w_sum, dt_w_sum, dt_b_sum, a_log_sum, skip_sum = sums
    return (
        output, d_hidden, gain_sum, in_sum, conv_w_sum, conv_b_sum, x_w_sum, dt_w_sum, dt_b_sum, a_log_sum,
        skip_sum, out_sum,
    )


def solution(mesh):
    return jax.shard_map(
        on_device,
        mesh=mesh,
        in_specs=(
            P(("ctx", "ch"), None), P(), P("ch", None), P(), P(), P(), P(None, "ch"), P("ch"), P("ch", None),
            P("ch"), P("ch", None), P("ctx", None), P("ctx"), P(("ctx", "ch"), None),
        ),
        out_specs=(
            P(("ctx", "ch"), None), P(("ctx", "ch"), None), P("ch"), P("ch", None), P("ch", None), P("ch"),
            P("ch", None), P(None, "ch"), P("ch"), P("ch", None), P("ch"), P("ch", None),
        ),
        check_vma=False,
    )
```

```python
import functools
import math

import jax
import jax.numpy as jnp
from jax import lax
from jax.experimental import pallas as pl
from jax.experimental.pallas import tpu as pltpu
from jax.sharding import PartitionSpec as P

f32 = jnp.float32
bf16 = jnp.bfloat16
eps = 1e-05
LOG2E = 1.4426950408889634
CUT = 1e30
SEGS = 8
UNROLL_FIRST = 4
UNROLL_SECOND = 4
MIB = 1 << 20
ROOM = 56 * MIB


def silu(v):
    return v * jax.nn.sigmoid(v)


def silu_slope(v):
    sig = jax.nn.sigmoid(v)
    return sig * (1.0 + v * (1.0 - sig))


def context_place(offsets, places):
    begins = jnp.max(jnp.where(offsets[:, None] <= places[None, :], offsets[:, None], 0), axis=0)
    return places - begins


def dot(a, b, dims, precision=None):
    return lax.dot_general(a, b, ((dims[:1], dims[1:]), ((), ())), precision=precision, preferred_element_type=f32)


def lane_groups(chans):
    width = 128 if chans % 128 == 0 else chans
    return chans // width, width


def softplus(v):
    small = jnp.exp(-jnp.abs(v))
    series = small * (1.0 - small * (0.5 - small * (1.0 / 3.0)))
    return jnp.maximum(v, 0.0) + jnp.where(small < 0.01, series, jnp.log(1.0 + small))


def mixing(span, back):
    size = span * SEGS
    row = lax.broadcasted_iota(jnp.int32, (size, size), 0)
    column = lax.broadcasted_iota(jnp.int32, (size, size), 1)
    if back:
        hit = (row % span) * SEGS + row // span == column
    else:
        hit = (row % SEGS) * span + row // SEGS == column
    return hit.astype(f32).astype(bf16)


def context_positions(starts_ref, first_row, rows, steps, chans):
    groups, width = lane_groups(chans)
    row = lax.broadcasted_iota(jnp.int32, (rows, width), 0) + first_row
    token = jnp.bitwise_and(row, SEGS - 1) * steps + jnp.right_shift(row, SEGS.bit_length() - 1)
    begin = jnp.zeros((rows, width), jnp.int32)
    for c in range(starts_ref.shape[1]):
        begin = jnp.where(starts_ref[0, c] <= token, starts_ref[0, c], begin)
    place = token - begin
    return jnp.concatenate([place] * groups, axis=1) if groups > 1 else place


def split_dot(wide, narrow, dims, swapped=False):
    high = wide.astype(bf16)
    low = (wide - high.astype(f32)).astype(bf16)
    if swapped:
        return dot(narrow, high, dims) + dot(narrow, low, dims)
    return dot(high, narrow, dims) + dot(low, narrow, dims)


def put(ref, rows, value, groups, width):
    for g in range(groups):
        ref[g, rows, :] = value[:, g * width : (g + 1) * width]


def take(ref, rows, groups):
    return jnp.concatenate([ref[g, rows, :] for g in range(groups)], axis=1) if groups > 1 else ref[0, rows, :]


def block_rows(t, size):
    return pl.ds(pl.multiple_of(t * size, size), size)


def entry_kernel(
    span, taps, rank_cols, starts_ref, hid_ref, w_ref, gain_ref, cw_ref, cb_ref, xw_ref,
    normed_ref, scale_ref, x_ref, gate_ref, val_ref, pre_ref, proj_ref, s_x, s_mixing,
):
    turn = pl.program_id(0)
    turns = pl.num_programs(0)
    chans = x_ref.shape[1]
    size = span * SEGS
    steps = span * turns
    halo = (taps - 1) * SEGS

    @pl.when(turn == 0)
    def _():
        s_mixing[...] = mixing(span, False)

    wide = hid_ref[...].astype(f32).reshape(size, hid_ref.shape[2])
    scale = lax.rsqrt(jnp.mean(wide * wide, axis=1, keepdims=True) + eps)
    normed = (wide * scale * gain_ref[...]).astype(bf16)
    normed_ref[...] = normed.reshape(normed_ref.shape)
    scale_ref[...] = scale.reshape(scale_ref.shape)
    mixed = dot(normed, w_ref[...], (1, 0)).astype(bf16)
    mixed = dot(s_mixing[...], mixed, (1, 0))
    rows = block_rows(turn, size)
    x_ref[rows, :] = mixed[:, :chans].astype(bf16)
    gate_ref[rows, :] = mixed[:, chans:].astype(bf16)
    s_x[pl.ds(pl.multiple_of(turn * size + halo, SEGS), size), :] = mixed[:, :chans]

    @pl.when(turn == turns - 1)
    def _():
        first = lax.broadcasted_iota(jnp.int32, (SEGS, chans), 0) == 0
        for j in range(taps - 1):
            last = s_x[steps * SEGS + j * SEGS : steps * SEGS + (j + 1) * SEGS, :]
            s_x[j * SEGS : (j + 1) * SEGS, :] = jnp.where(first, 0.0, pltpu.roll(last, 1, 0))

        def step(t, carry):
            place = context_positions(starts_ref, t * size, size, steps, chans)
            pre = cb_ref[...] + jnp.zeros((size, chans), f32)
            for k in range(taps):
                lag = taps - 1 - k
                at = pl.ds(pl.multiple_of(t * size + halo - lag * SEGS, SEGS), size)
                pre = pre + cw_ref[k : k + 1, :] * jnp.where(place >= lag, s_x[at, :], 0.0)
            rows = block_rows(t, size)
            pre_ref[rows, :] = pre
            values = silu(pre).astype(bf16)
            val_ref[rows, :] = values
            proj_ref[rows, :] = dot(values, xw_ref[...], (1, 0)).astype(bf16)
            return carry

        lax.fori_loop(0, turns, step, 0)


def gate_kernel(
    span, grad_ref, w_ref, gate_ref, val_ref, y_ref, skip_ref,
    branch_ref, gated_ref, dy_ref, dgate_ref, dskip_ref, s_in, s_out,
):
    turn = pl.program_id(0)
    size = span * SEGS

    @pl.when(turn == 0)
    def _():
        s_in[...] = mixing(span, False)
        s_out[...] = mixing(span, True)
        dskip_ref[...] = jnp.zeros_like(dskip_ref)

    vals = val_ref[...].astype(f32)
    gate = gate_ref[...].astype(f32)
    sig = jax.nn.sigmoid(gate)
    act = gate * sig
    scanned = y_ref[...] + skip_ref[...] * vals
    gated = dot(s_out[...], (scanned * act).astype(bf16), (1, 0)).astype(bf16)
    gated_ref[...] = gated.reshape(gated_ref.shape)
    branch_ref[...] = dot(gated, w_ref[...], (1, 0)).astype(bf16).reshape(branch_ref.shape)
    grad = grad_ref[...].reshape(size, grad_ref.shape[2])
    d_gated = dot(s_in[...], dot(grad, w_ref[...], (1, 1)).astype(bf16), (1, 0))
    dy = d_gated * act
    dy_ref[...] = dy
    d_gate = (d_gated * scanned * (sig * (1.0 + gate * (1.0 - sig)))).astype(bf16)
    d_gate = dot(s_out[...], d_gate, (1, 0)).astype(bf16)
    dgate_ref[...] = d_gate.reshape(dgate_ref.shape)
    dskip_ref[...] += jnp.sum(dy * vals, axis=0, keepdims=True)


def exit_kernel(
    span, taps, low_cols, starts_ref, dproj_ref, part_ref, pre_ref, x_ref, val_ref, cw_ref, xw_ref, dgate_ref, w_ref,
    hid_ref, scale_ref, gain_ref, ddtw_ref, dalog_ref, ddtb_ref, dskip_ref,
    dn_ref, din_ref, small_ref, dgain_ref, s_pre, s_dx, s_din,
):
    total, chans = x_ref.shape
    size = span * SEGS
    steps = total // SEGS
    turns = steps // span
    halo = (taps - 1) * SEGS
    turn = pl.program_id(0)

    @pl.when(turn == 0)
    def _():

        def first(t, carry):
            rows = block_rows(t, size)
            d_proj = dproj_ref[rows, :]
            d_values = part_ref[rows, :] + dot(d_proj, xw_ref[...], (1, 1))
            d_pre = d_values * silu_slope(pre_ref[rows, :])
            s_pre[rows, :] = d_pre
            d_bias, d_xw = carry
            return d_bias + jnp.sum(d_pre, axis=0, keepdims=True), d_xw + dot(d_proj, val_ref[rows, :], (0, 0))

        begin = (jnp.zeros((1, chans), f32), jnp.zeros((dproj_ref.shape[1], chans), f32))
        d_bias, d_xw = lax.fori_loop(0, turns, first, begin)
        last = lax.broadcasted_iota(jnp.int32, (SEGS, chans), 0) == SEGS - 1
        for j in range(taps - 1):
            head = s_pre[j * SEGS : (j + 1) * SEGS, :]
            s_pre[total + j * SEGS : total + (j + 1) * SEGS, :] = jnp.where(last, 0.0, pltpu.roll(head, SEGS - 1, 0))
        back = mixing(span, True)

        def second(t, sums):
            rows = block_rows(t, size)
            x = x_ref[rows, :].astype(f32)
            d_x = jnp.zeros((size, chans), f32)
            out = []
            for k in range(taps):
                lag = taps - 1 - k
                place = context_positions(starts_ref, t * size + lag * SEGS, size, steps, chans)
                later = s_pre[pl.ds(pl.multiple_of(t * size + lag * SEGS, SEGS), size), :]
                later = jnp.where(place >= lag, later, 0.0)
                d_x = d_x + cw_ref[k : k + 1, :] * later
                out.append(sums[k] + jnp.sum(later * x, axis=0, keepdims=True))
            natural = dot(back, d_x.astype(bf16), (1, 0)).astype(bf16).reshape(SEGS, span, chans)
            s_dx[:, block_rows(t, span), :] = natural
            return tuple(out)

        sums = lax.fori_loop(0, turns, second, (jnp.zeros((1, chans), f32),) * taps)
        s_din[...] = jnp.zeros_like(s_din)
        dgain_ref[...] = jnp.zeros_like(dgain_ref)
        rest = [*sums, d_bias, ddtb_ref[...], dskip_ref[...]]
        pad = small_ref.shape[0] - low_cols - ddtw_ref.shape[0] - dalog_ref.shape[0] - len(rest)
        small = [d_xw[:low_cols], ddtw_ref[...], dalog_ref[...], *rest, jnp.zeros((pad, chans), f32)]
        small_ref[...] = jnp.concatenate(small, axis=0).astype(bf16)

    @pl.when(turn > 0)
    def _():
        rows = hid_ref.shape[0]
        per_segment = steps // rows if rows <= steps else 1
        if rows <= steps:
            here = pl.ds(pl.multiple_of((turn - 1) % per_segment * rows, rows), rows)
            d_x = s_dx[(turn - 1) // per_segment, here, :]
        else:
            d_x = s_dx[pl.ds((turn - 1) * (rows // steps), rows // steps)].reshape(rows, chans)
        both = jnp.concatenate([d_x, dgate_ref[...]], axis=1)
        d_normed = dot(both, w_ref[...], (1, 1)).astype(bf16)
        dn_ref[...] = d_normed
        unit = hid_ref[...].astype(f32) * scale_ref[...]
        dgain_ref[...] += jnp.sum(d_normed.astype(f32) * unit, axis=0, keepdims=True)
        s_din[...] += dot(d_x, (unit * gain_ref[...]).astype(bf16), (0, 0))

    @pl.when(turn == pl.num_programs(0) - 1)
    def _():
        din_ref[...] = s_din[...].T.astype(bf16)


def prepare_spread(hot_ref, rank, states):
    row = lax.broadcasted_iota(jnp.int32, (hot_ref.shape[0], 128), 0)
    for n in range(2 * states):
        hot_ref[:, n * 128 : (n + 1) * 128] = (row == rank + n).astype(f32).astype(bf16)


def spread_columns(out_ref, slot, hot_ref, proj_ref, rows, states):
    block = proj_ref[rows, :]
    for n in range(0, 2 * states, 2):
        both = dot(block, hot_ref[:, n * 128 : (n + 2) * 128], (1, 0))
        out_ref[slot, n] = both[:, :128]
        out_ref[slot, n + 1] = both[:, 128:]


def prepare_sums(pick_ref, rank):
    column = lax.broadcasted_iota(jnp.int32, (128, pick_ref.shape[1]), 1)
    for n in range(pick_ref.shape[0] // 128):
        pick_ref[n * 128 : (n + 1) * 128, :] = (column == rank + n).astype(f32).astype(bf16)


def sum_lanes(mix_ref, pick_ref):
    total = None
    for first in range(0, mix_ref.shape[1], 512):
        part = dot(mix_ref[:, first : first + 512].astype(bf16), pick_ref[first : first + 512, :], (1, 0))
        total = part if total is None else total + part
    return total


def forward_kernel(
    rank, states, span, proj_ref, val_ref, cut_ref, dtw_ref, dtb_ref, alog_ref,
    y_ref, hist_ref, delta_ref, s_cut, s_dx, s_rate, s_state, s_wide, s_hot,
):
    total, chans = val_ref.shape
    steps = total // SEGS
    size = span * SEGS
    groups, width = lane_groups(chans)
    pairs = [(n, g) for n in range(states) for g in range(groups)]
    turn = pl.program_id(0)
    turns = steps // span
    slots = s_wide.shape[0]

    def rate(n, g):
        return s_rate[n : n + 1, g * width : (g + 1) * width]

    @pl.when(turn == 0)
    def _():
        s_rate[...] = -jnp.exp(alog_ref[...]) * LOG2E
        prepare_spread(s_hot, rank, states)

        def block(t, carry):
            rows = block_rows(t, size)
            slot = t if slots > 1 else 0
            spread_columns(s_wide, slot, s_hot, proj_ref, rows, states)
            delta = softplus(dot(proj_ref[rows, :rank], dtw_ref[...], (1, 0)) + dtb_ref[...])
            put(delta_ref, rows, delta, groups, width)
            put(s_cut, rows, delta + cut_ref[rows, :] * CUT, groups, width)
            put(s_dx, rows, delta * val_ref[rows, :].astype(f32), groups, width)

            def sweep(k, carry):
                held, span_sum = carry
                at = block_rows(t * span + k, SEGS)
                here = block_rows(k, SEGS)
                cuts = [s_cut[g, at, :] for g in range(groups)]
                dxs = [s_dx[g, at, :] for g in range(groups)]
                out = []
                for n, g in pairs:
                    push = dxs[g] * s_wide[slot, n, here, :width]
                    out.append(jnp.exp2(cuts[g] * rate(n, g)) * held[n * groups + g] + push)
                return tuple(out), tuple(span_sum[g] + cuts[g] for g in range(groups))

            return lax.fori_loop(0, span, sweep, carry, unroll=UNROLL_FIRST)

        zero = jnp.zeros((SEGS, width), f32)
        ends, sums = lax.fori_loop(0, turns, block, ((zero,) * len(pairs), (zero,) * groups))
        first = lax.broadcasted_iota(jnp.int32, (SEGS, width), 0) == 0
        for n, g in pairs:
            gain = jnp.exp2(sums[g] * rate(n, g))
            end = ends[n * groups + g]
            start = zero
            for _ in range(SEGS - 1):
                start = jnp.where(first, 0.0, pltpu.roll(gain * start + end, 1, 0))
            s_state[n * groups + g] = start

    slot = turn if slots > 1 else 0
    if slots == 1:
        spread_columns(s_wide, slot, s_hot, proj_ref, block_rows(turn, size), states)

    def sweep(k, held):
        at = block_rows(turn * span + k, SEGS)
        here = block_rows(k, SEGS)
        cuts = [s_cut[g, at, :] for g in range(groups)]
        dxs = [s_dx[g, at, :] for g in range(groups)]
        ys = [jnp.zeros((SEGS, width), f32) for _ in range(groups)]
        out = []
        for n in range(states):
            b_n = s_wide[slot, n, here, :width]
            c_n = s_wide[slot, states + n, here, :width]
            for g in range(groups):
                old = held[n * groups + g]
                hist_ref[0, k, n * groups + g] = old
                new = jnp.exp2(cuts[g] * rate(n, g)) * old + dxs[g] * b_n
                out.append(new)
                ys[g] = ys[g] + new * c_n
        for g in range(groups):
            y_ref[at, g * width : (g + 1) * width] = ys[g]
        return tuple(out)

    held = lax.fori_loop(0, span, sweep, tuple(s_state[j] for j in range(len(pairs))), unroll=UNROLL_SECOND)
    for j in range(len(pairs)):
        s_state[j] = held[j]
        hist_ref[0, span, j] = held[j]


def backward_kernel(
    rank, states, span, proj_ref, val_ref, cut_ref, dy_ref, delta_ref, dtw_ref, dtwt_ref, dtb_ref, alog_ref, skip_ref,
    hist_ref, part_ref, dval_ref, ddtw_ref, ddtb_ref, dalog_ref,
    s_cut, s_val, s_dy, s_dd, s_rate, s_state, s_drate, s_wide, s_mix, s_hot, s_pick,
):
    total, chans = val_ref.shape
    steps = total // SEGS
    size = span * SEGS
    groups, width = lane_groups(chans)
    pairs = [(n, g) for n in range(states) for g in range(groups)]
    turns = steps // span
    turn = pl.program_id(0)
    place = turns - 1 - turn
    slots = s_wide.shape[0]

    def rate(n, g):
        return s_rate[n : n + 1, g * width : (g + 1) * width]

    @pl.when(turn == 0)
    def _():
        s_rate[...] = -jnp.exp(alog_ref[...]) * LOG2E
        prepare_spread(s_hot, rank, states)
        prepare_sums(s_pick, rank)
        s_drate[...] = jnp.zeros_like(s_drate)
        s_mix[...] = jnp.zeros_like(s_mix)

        def block(turned, carry):
            t = turns - 1 - turned
            rows = block_rows(t, size)
            slot = t if slots > 1 else 0
            spread_columns(s_wide, slot, s_hot, proj_ref, rows, states)
            delta = take(delta_ref, rows, groups)
            put(s_cut, rows, delta + cut_ref[rows, :] * CUT, groups, width)
            put(s_val, rows, val_ref[rows, :].astype(f32), groups, width)
            put(s_dy, rows, dy_ref[rows, :], groups, width)

            def sweep(turned, carry):
                k = span - 1 - turned
                held, span_sum = carry
                at = block_rows(t * span + k, SEGS)
                here = block_rows(k, SEGS)
                cuts = [s_cut[g, at, :] for g in range(groups)]
                dys = [s_dy[g, at, :] for g in range(groups)]
                out = []
                for n, g in pairs:
                    lam = dys[g] * s_wide[slot, states + n, here, :width] + held[n * groups + g]
                    out.append(jnp.exp2(cuts[g] * rate(n, g)) * lam)
                return tuple(out), tuple(span_sum[g] + cuts[g] for g in range(groups))

            return lax.fori_loop(0, span, sweep, carry, unroll=UNROLL_FIRST)

        zero = jnp.zeros((SEGS, width), f32)
        ends, sums = lax.fori_loop(0, turns, block, ((zero,) * len(pairs), (zero,) * groups))
        last = lax.broadcasted_iota(jnp.int32, (SEGS, width), 0) == SEGS - 1
        for n, g in pairs:
            gain = jnp.exp2(sums[g] * rate(n, g))
            end = ends[n * groups + g]
            start = zero
            for _ in range(SEGS - 1):
                start = jnp.where(last, 0.0, pltpu.roll(gain * start + end, SEGS - 1, 0))
            s_state[n * groups + g] = start

    slot = place if slots > 1 else 0
    if slots == 1:
        spread_columns(s_wide, slot, s_hot, proj_ref, block_rows(place, size), states)

    def sweep(turned, held):
        k = span - 1 - turned
        at = block_rows(place * span + k, SEGS)
        here = block_rows(k, SEGS)
        cuts = [s_cut[g, at, :] for g in range(groups)]
        deltas = [delta_ref[g, at, :] for g in range(groups)]
        vals = [s_val[g, at, :] for g in range(groups)]
        dys = [s_dy[g, at, :] for g in range(groups)]
        dxs = [deltas[g] * vals[g] for g in range(groups)]
        zero = jnp.zeros((SEGS, width), f32)
        by_rate = [zero] * groups
        by_b = [zero] * groups
        out = []
        for n in range(states):
            b_n = s_wide[slot, n, here, :width]
            c_n = s_wide[slot, states + n, here, :width]
            mix = None
            mix_c = None
            for g in range(groups):
                j = n * groups + g
                lam = dys[g] * c_n + held[j]
                onward = jnp.exp2(cuts[g] * rate(n, g)) * lam
                out.append(onward)
                through = onward * hist_ref[0, k, j]
                by_rate[g] = by_rate[g] + through * rate(n, g)
                by_b[g] = by_b[g] + lam * b_n
                s_drate[j] = s_drate[j] + through * deltas[g]
                term = lam * dxs[g]
                mix = term if mix is None else mix + term
                term = dys[g] * hist_ref[0, k + 1, j]
                mix_c = term if mix_c is None else mix_c + term
            s_mix[here, n * 128 : n * 128 + width] = mix
            s_mix[here, (states + n) * 128 : (states + n) * 128 + width] = mix_c
        for g in range(groups):
            skip = skip_ref[:, g * width : (g + 1) * width]
            s_dd[g, at, :] = by_rate[g] * (1.0 / LOG2E) + by_b[g] * vals[g]
            dval_ref[at, g * width : (g + 1) * width] = by_b[g] * deltas[g] + dys[g] * skip
        return tuple(out)

    held = lax.fori_loop(0, span, sweep, tuple(s_state[j] for j in range(len(pairs))), unroll=UNROLL_SECOND)
    for j in range(len(pairs)):
        s_state[j] = held[j]
    rows = block_rows(place, size)
    pre = dot(proj_ref[rows, :rank], dtw_ref[...], (1, 0)) + dtb_ref[...]
    d_pre = take(s_dd, rows, groups) * jax.nn.sigmoid(pre)
    d_bias = jnp.sum(d_pre, axis=0, keepdims=True)
    d_dtw = split_dot(d_pre, proj_ref[rows, :rank], (0, 0), swapped=True)
    part = split_dot(d_pre, dtwt_ref[...], (1, 0))
    part_ref[rows, :] = (part + sum_lanes(s_mix, s_pick)).astype(bf16)

    @pl.when(turn == 0)
    def _():
        ddtb_ref[...] = d_bias
        ddtw_ref[...] = d_dtw

    @pl.when(turn > 0)
    def _():
        ddtb_ref[...] += d_bias
        ddtw_ref[...] += d_dtw

    @pl.when(turn == turns - 1)
    def _():
        sums = [jnp.sum(s_drate[j], axis=0, keepdims=True) for j in range(len(pairs))]
        rows = [jnp.concatenate(sums[n * groups : (n + 1) * groups], axis=1) for n in range(states)]
        dalog_ref[...] = jnp.concatenate(rows, axis=0) * s_rate[...] * (1.0 / LOG2E)


def scan_span(steps):
    return math.gcd(steps, 32)


def wide_slots(steps, span, states):
    turns = steps // span
    return turns if turns * 2 * states * span * SEGS * 128 * 4 <= 16 * MIB else 1


def whole(*shape):
    return pl.BlockSpec(shape, lambda *t: (0,) * len(shape))


def like(*shape, dtype=f32):
    return jax.ShapeDtypeStruct(shape, dtype)


def about(micros):
    return pl.CostEstimate(flops=int(micros * 1.1e9), bytes_accessed=1 << 20, transcendentals=0)


SCALARS = pl.BlockSpec(memory_space=pltpu.SMEM)


def run_entry(starts, hidden_all, weight, gain, conv_w, conv_b, x_w, span):
    total, width = hidden_all.shape
    taps, chans = conv_w.shape
    lanes = x_w.shape[1]
    steps = total // SEGS
    segments = pl.BlockSpec((SEGS, span, width), lambda t: (0, t, 0))
    normed, scale, *rest = pl.pallas_call(
        functools.partial(entry_kernel, span, taps, lanes),
        grid=(steps // span,),
        in_specs=[
            SCALARS, segments, whole(width, 2 * chans), whole(1, width), whole(taps, chans), whole(1, chans),
            whole(chans, lanes),
        ],
        out_specs=[segments, pl.BlockSpec((SEGS, span, 1), lambda t: (0, t, 0))]
        + [whole(total, chans)] * 4 + [whole(total, lanes)],
        out_shape=[like(SEGS, steps, width, dtype=bf16), like(SEGS, steps, 1)] + [like(total, chans, dtype=bf16)] * 3
        + [like(total, chans), like(total, lanes, dtype=bf16)],
        scratch_shapes=[
            pltpu.VMEM((total + (taps - 1) * SEGS, chans), f32), pltpu.VMEM((span * SEGS, span * SEGS), bf16),
        ],
        compiler_params=pltpu.CompilerParams(vmem_limit_bytes=ROOM),
        cost_estimate=about(6 * total * chans / 262144),
        name="entry",
    )(starts, hidden_all.reshape(SEGS, steps, width), weight, gain, conv_w, conv_b, x_w)
    return (normed, scale.reshape(total, 1), *rest)


def run_gate(grad_all, out_w, gate, values, y, skip, span):
    total, width = grad_all.shape
    chans = gate.shape[1]
    steps = total // SEGS
    rows = pl.BlockSpec((span * SEGS, chans), lambda t: (t, 0))
    part = pl.BlockSpec((SEGS, span, chans), lambda t: (0, t, 0))
    full = pl.BlockSpec((SEGS, span, width), lambda t: (0, t, 0))
    natural = like(SEGS, steps, chans, dtype=bf16)
    branch, gated, dy, d_gate, d_skip = pl.pallas_call(
        functools.partial(gate_kernel, span),
        grid=(steps // span,),
        in_specs=[full, whole(chans, width), rows, rows, rows, whole(1, chans)],
        out_specs=[full, part, rows, part, whole(1, chans)],
        out_shape=[like(SEGS, steps, width, dtype=bf16), natural, like(total, chans), natural, like(1, chans)],
        scratch_shapes=[pltpu.VMEM((span * SEGS, span * SEGS), bf16)] * 2,
        compiler_params=pltpu.CompilerParams(vmem_limit_bytes=ROOM),
        cost_estimate=about(6 * total * chans / 262144),
        name="gate",
    )(grad_all.reshape(SEGS, steps, width), out_w, gate, values, y, skip)
    return branch.reshape(total, width), gated.reshape(total, chans), dy, d_gate.reshape(total, chans), d_skip


def run_exit(
    starts, d_proj, value_part, pre, x_in, values, conv_w, x_w, d_gate, weight, hidden_all, scale, gain,
    d_dtw, d_alog_t, d_dtb, d_skip, low_cols, small_rows, span,
):
    total, chans = x_in.shape
    taps = conv_w.shape[0]
    lanes = x_w.shape[1]
    width = hidden_all.shape[1]
    steps = total // SEGS
    size = math.gcd(total, 256)

    def rows(lanes):
        return pl.BlockSpec((size, lanes), lambda t: (jnp.maximum(t - 1, 0), 0))

    return pl.pallas_call(
        functools.partial(exit_kernel, span, taps, low_cols),
        grid=(1 + total // size,),
        in_specs=[SCALARS, whole(total, lanes)] + [whole(total, chans)] * 4 + [
            whole(taps, chans), whole(chans, lanes), rows(chans), whole(width, 2 * chans), rows(width), rows(1),
            whole(1, width), whole(*d_dtw.shape), whole(*d_alog_t.shape), whole(1, chans), whole(1, chans),
        ],
        out_specs=[rows(width), whole(width, chans), whole(small_rows, chans), whole(1, width)],
        out_shape=[
            like(total, width, dtype=bf16), like(width, chans, dtype=bf16), like(small_rows, chans, dtype=bf16),
            like(1, width),
        ],
        scratch_shapes=[
            pltpu.VMEM((total + (taps - 1) * SEGS, chans), f32), pltpu.VMEM((SEGS, steps, chans), bf16),
            pltpu.VMEM((chans, width), f32),
        ],
        compiler_params=pltpu.CompilerParams(vmem_limit_bytes=ROOM),
        cost_estimate=about(10 * total * chans / 262144),
        name="exit",
    )(
        starts, d_proj, value_part, pre, x_in, values, conv_w, x_w, d_gate, weight, hidden_all, scale, gain,
        d_dtw, d_alog_t, d_dtb, d_skip,
    )


def run_forward(proj, values, cut, dt_weight, dt_bias, a_log_t, states, span):
    total, chans = values.shape
    rank = dt_weight.shape[0]
    steps = total // SEGS
    groups, width = lane_groups(chans)
    count = states * groups
    lanes = proj.shape[1]
    slots = wide_slots(steps, span, states)
    by_group = pltpu.VMEM((groups, total, width), f32)
    return pl.pallas_call(
        functools.partial(forward_kernel, rank, states, span),
        grid=(steps // span,),
        in_specs=[
            whole(total, lanes), whole(total, chans), whole(total, 1), whole(rank, chans), whole(1, chans),
            whole(states, chans),
        ],
        out_specs=[
            whole(total, chans), pl.BlockSpec((1, span + 1, count, SEGS, width), lambda t: (t, 0, 0, 0, 0)),
            whole(groups, total, width),
        ],
        out_shape=[
            like(total, chans), like(steps // span, span + 1, count, SEGS, width), like(groups, total, width),
        ],
        scratch_shapes=[
            by_group, by_group, pltpu.VMEM((states, chans), f32), pltpu.VMEM((count, SEGS, width), f32),
            pltpu.VMEM((slots, 2 * states, span * SEGS, 128), f32), pltpu.VMEM((lanes, 2 * states * 128), bf16),
        ],
        compiler_params=pltpu.CompilerParams(vmem_limit_bytes=ROOM),
        cost_estimate=about(18 * total * chans / 262144),
        name="scan_forward",
    )(proj, values, cut, dt_weight, dt_bias, a_log_t)


def run_backward(proj, values, cut, dy, delta, dt_weight, dt_weight_t, dt_bias, a_log_t, skip, hist, states, span):
    total, chans = values.shape
    rank = dt_weight.shape[0]
    steps = total // SEGS
    groups, width = lane_groups(chans)
    count = states * groups
    lanes = proj.shape[1]
    turns = steps // span
    slots = wide_slots(steps, span, states)
    by_group = pltpu.VMEM((groups, total, width), f32)
    return pl.pallas_call(
        functools.partial(backward_kernel, rank, states, span),
        grid=(turns,),
        in_specs=[
            whole(total, lanes), whole(total, chans), whole(total, 1), whole(total, chans), whole(groups, total, width),
            whole(rank, chans), whole(chans, lanes), whole(1, chans), whole(states, chans), whole(1, chans),
            pl.BlockSpec((1, span + 1, count, SEGS, width), lambda t: (turns - 1 - t, 0, 0, 0, 0)),
        ],
        out_specs=[
            whole(total, lanes), whole(total, chans), whole(rank, chans), whole(1, chans), whole(states, chans),
        ],
        out_shape=[
            like(total, lanes, dtype=bf16), like(total, chans), like(rank, chans), like(1, chans), like(states, chans),
        ],
        scratch_shapes=[
            by_group, by_group, by_group, by_group, pltpu.VMEM((states, chans), f32),
            pltpu.VMEM((count, SEGS, width), f32), pltpu.VMEM((count, SEGS, width), f32),
            pltpu.VMEM((slots, 2 * states, span * SEGS, 128), f32), pltpu.VMEM((span * SEGS, 2 * states * 128), f32),
            pltpu.VMEM((lanes, 2 * states * 128), bf16), pltpu.VMEM((2 * states * 128, lanes), bf16),
        ],
        compiler_params=pltpu.CompilerParams(vmem_limit_bytes=ROOM),
        cost_estimate=about(22 * total * chans / 262144),
        name="scan_backward",
    )(proj, values, cut, dy, delta, dt_weight, dt_weight_t, dt_bias, a_log_t, skip, hist)


def tree_sum(parts):
    parts = [p.astype(f32) for p in parts]
    while len(parts) > 1:
        parts = [parts[i] + parts[i + 1] for i in range(0, len(parts), 2)]
    return parts[0]


def swap(value, axis, mask):
    return lax.ppermute(value, axis, [(i, i ^ mask) for i in range(lax.axis_size(axis))])


def pick(blocks, index, dim=0):
    return lax.dynamic_index_in_dim(blocks, index, dim, keepdims=False)


def collected(pieces, me):
    out = jnp.zeros((len(pieces),) + pieces[0].shape, pieces[0].dtype)
    for d, piece in enumerate(pieces):
        out = lax.dynamic_update_index_in_dim(out, piece, me ^ d, 0)
    return out


def owned_parts(blocks, axis):
    me = lax.axis_index(axis)
    size = lax.axis_size(axis)
    return [pick(blocks, me)] + [swap(pick(blocks, me ^ d), axis, d) for d in range(1, size)]


def collect(value, axis):
    me = lax.axis_index(axis)
    return collected([value] + [swap(value, axis, d) for d in range(1, lax.axis_size(axis))], me)


def sum_over_peers(part):
    peers = lax.axis_size("ch")
    rows, lanes = part.shape
    if peers != 8:
        got = lax.all_to_all(part.reshape(peers, rows // peers, lanes), "ch", split_axis=0, concat_axis=0, tiled=True)
        return lax.all_gather(got.astype(f32).sum(axis=0).astype(bf16), "ch", axis=0, tiled=True)
    core, chip = lax.axis_index("ch") % 2, lax.axis_index("ch") // 2
    chips = peers // 2
    halves = part.reshape(2, chips, rows // peers, lanes)
    got = swap(pick(halves, 1 - core), "ch", 1)
    half = tree_sum([pick(halves, core), got]).astype(bf16)
    pieces = [pick(half, chip)] + [swap(pick(half, chip ^ d), "ch", 2 * d) for d in range(1, chips)]
    own = tree_sum(pieces).astype(bf16)
    half = collected([own] + [swap(own, "ch", 2 * d) for d in range(1, chips)], chip)
    return collected([half, swap(half, "ch", 1)], core).reshape(rows, lanes)


def to_peers(blocks):
    return lax.all_to_all(blocks, "ch", split_axis=0, concat_axis=0, tiled=True)


def finish_kernel(
    parts, me_ref, *refs,
):
    n = parts
    late, outs, (cross_ref, branch_ref, dn_ref, hid_ref, grad_ref, gain_ref) = refs[:n], refs[n : 2 * n], refs[2 * n : 2 * n + 6]
    (out_ref, dh_ref, dgain_ref, din_ref, dcw_ref, dcb_ref, dxw_ref, ddtw_ref, ddtb_ref, dalog_ref, dskip_ref,
     dout_ref, s_small) = refs[2 * n + 6 :]
    chans = dcb_ref.shape[1]
    inner = din_ref.shape[1] // 2
    share = din_ref.shape[0] // n
    peers = inner // chans
    low_cols, rank, states, taps = dxw_ref.shape[0], ddtw_ref.shape[0], dalog_ref.shape[0], dcw_ref.shape[0]
    for d in range(n):
        who = jnp.bitwise_xor(me_ref[0], d)
        rows = block_rows(who, share)
        for p in range(peers):
            block = late[d][p * 2 * share : (p + 1) * 2 * share, :].astype(f32)
            din_ref[rows, p * chans : (p + 1) * chans] = block[:share]
            din_ref[rows, inner + p * chans : inner + (p + 1) * chans] = block[share:]
        small = late[d][2 * share * peers :, :].astype(f32)
        s_small[block_rows(who, small.shape[0]), :] = small
        dout_ref[block_rows(who, outs[d].shape[0]), :] = outs[d][...].astype(f32)
    gain = jnp.sum(cross_ref[:, 2 * share :, :].astype(f32), axis=0)
    dgain_ref[...] = gain[:1, : dgain_ref.shape[1]]
    at = low_cols + rank
    ddtw_ref[...] = s_small[low_cols:at, :]
    dxw_ref[...] = s_small[:low_cols, :]
    tail = s_small[at:, :]
    dalog_ref[...] = tail[:states]
    dcw_ref[...] = tail[states : states + taps]
    at = states + taps
    dcb_ref[...] = tail[at : at + 1]
    ddtb_ref[...] = tail[at + 1 : at + 2]
    dskip_ref[...] = tail[at + 2 : at + 3]
    hidden = hid_ref[...].astype(f32)
    out_ref[...] = (hidden + branch_ref[...].astype(f32)).astype(bf16)
    scale = lax.rsqrt(jnp.mean(hidden * hidden, axis=1, keepdims=True) + eps)
    unit = hidden * scale
    d_unit = dn_ref[...].astype(f32) * gain_ref[...]
    mean = jnp.mean(d_unit * unit, axis=1, keepdims=True)
    dh_ref[...] = (grad_ref[...].astype(f32) + scale * (d_unit - unit * mean)).astype(bf16)


def run_finish(late, outs, cross, branch, d_normed, hidden, grad, gain, sizes, me):
    rows, width = hidden.shape
    low_cols, rank, states, taps, small_rows = sizes
    packs = len(late)
    chans = late[0].shape[1]
    in_rows = width // cross.shape[0]
    inner = chans * cross.shape[0]
    wide = [*late, *outs, cross, branch, d_normed, hidden, grad, gain]
    shapes = [
        like(rows, width, dtype=bf16), like(rows, width, dtype=bf16), like(1, in_rows), like(in_rows, 2 * inner),
        like(taps, chans), like(1, chans), like(low_cols, chans), like(rank, chans), like(1, chans),
        like(states, chans), like(1, chans), like(chans, width),
    ]
    return pl.pallas_call(
        functools.partial(finish_kernel, packs),
        grid=(1,),
        in_specs=[SCALARS] + [whole(*a.shape) for a in wide],
        out_specs=[whole(*a.shape) for a in shapes],
        out_shape=shapes,
        scratch_shapes=[pltpu.VMEM((small_rows, chans), f32)],
        compiler_params=pltpu.CompilerParams(vmem_limit_bytes=ROOM),
        cost_estimate=about(4),
        name="finish",
    )(me[None], *wide)


def finish_plain(late, outs, cross, branch, d_normed, hidden, grad, gain, sizes, me):
    low_cols, rank, states, taps, small_rows = sizes
    packs, peers, chans = len(late), cross.shape[0], late[0].shape[1]
    share = hidden.shape[1] // (peers * packs)
    late = collected(late, me).astype(f32)
    halves = late[:, : 2 * share * peers].reshape(packs, peers, 2, share, chans)
    d_in = jnp.transpose(halves, (0, 3, 2, 1, 4)).reshape(packs * share, 2 * peers * chans)
    small = late[:, 2 * share * peers :].reshape(small_rows, chans)
    parts = []
    at = 0
    for count in (low_cols, rank, states, taps, 1, 1, 1):
        parts.append(small[at : at + count])
        at += count
    d_xw, d_dtw, d_alog, d_cw, d_cb, d_dtb, d_skip = parts
    d_gain = cross[:, 2 * share :].astype(f32).sum(axis=0).reshape(1, -1)[:, : share * packs]
    hidden = hidden.astype(f32)
    output = (hidden + branch.astype(f32)).astype(bf16)
    scale = lax.rsqrt(jnp.mean(hidden * hidden, axis=1, keepdims=True) + eps)
    unit = hidden * scale
    d_unit = d_normed.astype(f32) * gain
    mean = jnp.mean(d_unit * unit, axis=1, keepdims=True)
    d_hidden = (grad.astype(f32) + scale * (d_unit - unit * mean)).astype(bf16)
    d_out = collected(outs, me).astype(f32).reshape(chans, -1)
    return output, d_hidden, d_gain, d_in, d_cw, d_cb, d_xw, d_dtw, d_dtb, d_alog, d_skip, d_out


def on_device(
    hidden_in, norm_gain, in_weight, conv_weight, conv_bias, x_weight, dt_weight, dt_bias, a_log, skip, out_weight,
    lengths, resets, out_grad,
):
    peers = lax.axis_size("ch")
    packs = lax.axis_size("ctx")
    me = lax.axis_index("ch")
    rows, width = hidden_in.shape
    chans = out_weight.shape[0]
    taps = conv_weight.shape[1]
    rank, states = dt_weight.shape[0], a_log.shape[1]
    total = rows * peers

    hidden_all = lax.all_gather(hidden_in, "ch", axis=0, tiled=True)
    in_rows = in_weight.shape[0]
    share = in_rows // packs
    my_share = lax.dynamic_slice_in_dim(in_weight, lax.axis_index("ctx") * share, share, 0)
    got = to_peers(jnp.moveaxis(my_share.reshape(share, 2, peers, chans), 2, 0))
    shares = collect(got.reshape(peers, share, 2 * chans), "ctx")
    my_cols = jnp.moveaxis(shares, 0, 1).reshape(width, 2 * chans)
    grad_all = lax.all_gather(out_grad, "ch", axis=0, tiled=True)

    steps = total // SEGS
    span = scan_span(steps)
    low_cols = rank + 2 * states
    lanes = -(-low_cols // 128) * 128
    sizes = lengths[0]
    offsets = jnp.cumsum(sizes) - sizes
    where_in = context_place(offsets, jnp.arange(total, dtype=jnp.int32))
    cut = ((where_in == 0) | (resets == 1)).astype(f32).reshape(SEGS, steps).T.reshape(total, 1)
    starts = offsets[None, :]
    conv_w = lax.dynamic_slice_in_dim(conv_weight, me * chans, chans, 0).T
    conv_b = lax.dynamic_slice_in_dim(conv_bias, me * chans, chans, 0)[None, :]
    x_w = lax.dynamic_slice_in_dim(x_weight, me * chans, chans, 0)
    x_w = jnp.pad(x_w, ((0, 0), (0, lanes - low_cols)))

    normed, scale_all, x_in, gate, values, pre, proj_part = run_entry(
        starts, hidden_all, my_cols, norm_gain[None, :], conv_w, conv_b, x_w, span
    )
    proj = sum_over_peers(proj_part)

    a_log_t = a_log.T
    dt_b, skip_row = dt_bias[None, :], skip[None, :]
    y, hist, delta = run_forward(proj, values, cut, dt_weight, dt_b, a_log_t, states, span)
    branch_part, gated, dy, d_gate, d_skip = run_gate(grad_all, out_weight, gate, values, y, skip_row, span)
    branch = lax.psum_scatter(branch_part, "ch", scatter_dimension=0, tiled=True)
    sides = width // chans
    out_share = chans // packs
    d_out = dot(gated, grad_all, (0, 0)).astype(bf16).reshape(packs, out_share, sides, chans)
    d_out = jnp.moveaxis(d_out, 2, 1).reshape(packs, out_share * sides, chans)
    d_in_gate = dot(normed.reshape(total, width), d_gate, (0, 0)).astype(bf16)

    def by_pack(d_in):
        return jnp.moveaxis(d_in.reshape(peers, packs, share, chans), 1, 0).reshape(packs, peers * share, chans)

    early = owned_parts(jnp.concatenate([d_out, by_pack(d_in_gate)], axis=1), "ctx")

    dt_w_t = jnp.pad(dt_weight.T, ((0, 0), (0, lanes - rank)))
    d_part, value_part, d_dt_weight, d_dt_bias, d_a_log_t = run_backward(
        proj, values, cut, dy, delta, dt_weight, dt_w_t, dt_b, a_log_t, skip_row, hist, states, span
    )
    early, d_part = lax.optimization_barrier((early, d_part))
    d_proj = sum_over_peers(d_part)
    early = tree_sum(early).astype(bf16)
    branch, early, d_proj = lax.optimization_barrier((branch, early, d_proj))
    d_out = jnp.moveaxis(early[: out_share * sides].reshape(sides, out_share, chans), 0, 1).reshape(out_share, width)
    counts = (low_cols, rank, states, taps)
    small_rows = -(-(sum(counts) + 3) // (16 * packs)) * 16 * packs
    d_normed_part, d_in_x, small, d_gain = run_exit(
        starts, d_proj, value_part, pre, x_in, values, conv_w, x_w, d_gate, my_cols, hidden_all, scale_all,
        norm_gain[None, :], d_dt_weight, d_a_log_t, d_dt_bias, d_skip, low_cols, small_rows, span,
    )
    d_normed = lax.psum_scatter(d_normed_part, "ch", scatter_dimension=0, tiled=True)

    gain_rows = d_gain.astype(bf16).reshape(sides, chans)
    gain_rows = jnp.pad(gain_rows, ((0, -sides % 16), (0, 0)))
    late = [by_pack(d_in_x), small.reshape(packs, small_rows // packs, chans)]
    late.append(jnp.broadcast_to(gain_rows, (packs,) + gain_rows.shape))
    late = tree_sum(owned_parts(jnp.concatenate(late, axis=1), "ctx")).astype(bf16)
    own_rows = peers * share
    gain_rows = late[own_rows + small_rows // packs :][:sides].reshape(peers, in_rows)
    pad_rows = -(-in_rows // chans)
    gain_rows = jnp.pad(gain_rows, ((0, 0), (0, pad_rows * chans - in_rows))).reshape(peers, pad_rows, chans)
    gain_rows = jnp.pad(gain_rows, ((0, 0), (0, -pad_rows % 16), (0, 0)))
    cross = [late[:own_rows].reshape(peers, share, chans), early[out_share * sides :].reshape(peers, share, chans)]
    cross, d_out = lax.optimization_barrier((jnp.concatenate([*cross, gain_rows], axis=1), d_out))
    cross = to_peers(cross)
    outs = [d_out] + [swap(d_out, "ctx", d) for d in range(1, packs)]
    outs, cross = lax.optimization_barrier((outs, cross))
    own = [cross[:, : 2 * share].reshape(2 * own_rows, chans), late[own_rows : own_rows + small_rows // packs]]
    own = jnp.concatenate(own, axis=0)
    late = [own] + [swap(own, "ctx", d) for d in range(1, packs)]
    finish = run_finish if share % 16 == 0 and chans % 128 == 0 else finish_plain
    (
        output, d_hidden, gain_sum, in_sum, conv_w_sum, conv_b_sum, x_w_sum, dt_w_sum, dt_b_sum, a_log_sum, skip_sum,
        out_sum,
    ) = finish(
        late, outs, cross, branch, d_normed, hidden_in, out_grad, norm_gain[None, :], (*counts, small_rows),
        lax.axis_index("ctx"),
    )
    return (
        output, d_hidden, gain_sum[0], in_sum, conv_w_sum.T, conv_b_sum[0], x_w_sum.T, dt_w_sum, dt_b_sum[0],
        a_log_sum.T, skip_sum[0], out_sum,
    )


def solution(mesh):
    return jax.shard_map(
        on_device,
        mesh=mesh,
        in_specs=(
            P(("ctx", "ch"), None), P(), P("ch", None), P(), P(), P(), P(None, "ch"), P("ch"), P("ch", None),
            P("ch"), P("ch", None), P("ctx", None), P("ctx"), P(("ctx", "ch"), None),
        ),
        out_specs=(
            P(("ctx", "ch"), None), P(("ctx", "ch"), None), P("ch"), P("ch", None), P("ch", None), P("ch"),
            P("ch", None), P(None, "ch"), P("ch"), P("ch", None), P("ch"), P("ch", None),
        ),
        check_vma=False,
    )
```

```python
import functools
import math

import jax
import jax.numpy as jnp
from jax import lax
from jax.experimental import pallas as pl
from jax.experimental.pallas import tpu as pltpu
from jax.sharding import PartitionSpec as P

f32 = jnp.float32
bf16 = jnp.bfloat16
eps = 1e-05
LOG2E = 1.4426950408889634
CUT = 1e30
SEGS = 8
BATCH = 4
TOGETHER = 4
MIB = 1 << 20
ROOM = 56 * MIB


def silu(v):
    return v * jax.nn.sigmoid(v)


def silu_slope(v):
    sig = jax.nn.sigmoid(v)
    return sig * (1.0 + v * (1.0 - sig))


def context_place(offsets, places):
    begins = jnp.max(jnp.where(offsets[:, None] <= places[None, :], offsets[:, None], 0), axis=0)
    return places - begins


def dot(a, b, dims, precision=None):
    return lax.dot_general(a, b, ((dims[:1], dims[1:]), ((), ())), precision=precision, preferred_element_type=f32)


def lane_groups(chans):
    width = 128 if chans % 128 == 0 else chans
    return chans // width, width


def softplus(v):
    small = jnp.exp(-jnp.abs(v))
    series = small * (1.0 - small * (0.5 - small * (1.0 / 3.0)))
    return jnp.maximum(v, 0.0) + jnp.where(small < 0.01, series, jnp.log(1.0 + small))


def mixing(span, back):
    size = span * SEGS
    row = lax.broadcasted_iota(jnp.int32, (size, size), 0)
    column = lax.broadcasted_iota(jnp.int32, (size, size), 1)
    if back:
        hit = (row % span) * SEGS + row // span == column
    else:
        hit = (row % SEGS) * span + row // SEGS == column
    return hit.astype(f32).astype(bf16)


def context_positions(starts_ref, first_row, rows, steps, lanes):
    row = lax.broadcasted_iota(jnp.int32, (rows, lanes), 0) + first_row
    token = jnp.bitwise_and(row, SEGS - 1) * steps + jnp.right_shift(row, SEGS.bit_length() - 1)
    begin = jnp.zeros((rows, lanes), jnp.int32)
    for c in range(starts_ref.shape[1]):
        begin = jnp.where(starts_ref[0, c] <= token, starts_ref[0, c], begin)
    return token - begin


def split_dot(wide, narrow, dims, swapped=False):
    high = wide.astype(bf16)
    low = (wide - high.astype(f32)).astype(bf16)
    if swapped:
        return dot(narrow, high, dims) + dot(narrow, low, dims)
    return dot(high, narrow, dims) + dot(low, narrow, dims)


def put(ref, rows, value, groups, width):
    for g in range(groups):
        ref[g, rows, :] = value[:, g * width : (g + 1) * width]


def take(ref, rows, groups):
    return jnp.concatenate([ref[g, rows, :] for g in range(groups)], axis=1) if groups > 1 else ref[0, rows, :]


def block_rows(t, size):
    return pl.ds(pl.multiple_of(t * size, size), size)


def entry_kernel(
    span, taps, rank_cols, starts_ref, hid_ref, w_ref, gain_ref, cw_ref, cb_ref, xw_ref,
    normed_ref, scale_ref, x_ref, gate_ref, val_ref, pre_ref, proj_ref, s_x, s_mixing,
):
    turn = pl.program_id(0)
    turns = pl.num_programs(0)
    chans = x_ref.shape[1]
    size = span * SEGS
    steps = span * turns
    halo = (taps - 1) * SEGS

    @pl.when(turn == 0)
    def _():
        s_mixing[...] = mixing(span, False)

    wide = hid_ref[...].astype(f32).reshape(size, hid_ref.shape[2])
    scale = lax.rsqrt(jnp.mean(wide * wide, axis=1, keepdims=True) + eps)
    normed = (wide * scale * gain_ref[...]).astype(bf16)
    normed_ref[...] = normed.reshape(normed_ref.shape)
    scale_ref[...] = jnp.broadcast_to(scale, (size, 128)).reshape(scale_ref.shape)
    mixed = dot(normed, w_ref[...], (1, 0)).astype(bf16)
    mixed = dot(s_mixing[...], mixed, (1, 0))
    rows = block_rows(turn, size)
    x_ref[rows, :] = mixed[:, :chans].astype(bf16)
    gate_ref[rows, :] = mixed[:, chans:].astype(bf16)
    s_x[pl.ds(pl.multiple_of(turn * size + halo, SEGS), size), :] = mixed[:, :chans]

    @pl.when(turn == turns - 1)
    def _():
        first = lax.broadcasted_iota(jnp.int32, (SEGS, chans), 0) == 0
        for j in range(taps - 1):
            last = s_x[steps * SEGS + j * SEGS : steps * SEGS + (j + 1) * SEGS, :]
            s_x[j * SEGS : (j + 1) * SEGS, :] = jnp.where(first, 0.0, pltpu.roll(last, 1, 0))

        def step(t, carry):
            groups, width = lane_groups(chans)
            place = jnp.concatenate([context_positions(starts_ref, t * size, size, steps, width)] * groups, axis=1)
            pre = cb_ref[...] + jnp.zeros((size, chans), f32)
            for k in range(taps):
                lag = taps - 1 - k
                at = pl.ds(pl.multiple_of(t * size + halo - lag * SEGS, SEGS), size)
                pre = pre + cw_ref[k : k + 1, :] * jnp.where(place >= lag, s_x[at, :], 0.0)
            rows = block_rows(t, size)
            pre_ref[rows, :] = pre
            values = silu(pre).astype(bf16)
            val_ref[rows, :] = values
            proj_ref[rows, :] = dot(values, xw_ref[...], (1, 0)).astype(bf16)
            return carry

        lax.fori_loop(0, turns, step, 0)


def gate_kernel(
    span, grad_ref, w_ref, gate_ref, val_ref, y_ref, skip_ref,
    branch_ref, gated_ref, dy_ref, dgate_ref, dskip_ref, s_in, s_out,
):
    turn = pl.program_id(0)
    size = span * SEGS

    @pl.when(turn == 0)
    def _():
        s_in[...] = mixing(span, False)
        s_out[...] = mixing(span, True)
        dskip_ref[...] = jnp.zeros_like(dskip_ref)

    vals = val_ref[...].astype(f32)
    gate = gate_ref[...].astype(f32)
    sig = jax.nn.sigmoid(gate)
    act = gate * sig
    scanned = y_ref[...] + skip_ref[...] * vals
    gated = dot(s_out[...], (scanned * act).astype(bf16), (1, 0)).astype(bf16)
    gated_ref[...] = gated.reshape(gated_ref.shape)
    branch_ref[...] = dot(gated, w_ref[...], (1, 0)).astype(bf16).reshape(branch_ref.shape)
    grad = grad_ref[...].reshape(size, grad_ref.shape[2])
    d_gated = dot(s_in[...], dot(grad, w_ref[...], (1, 1)).astype(bf16), (1, 0))
    dy = d_gated * act
    dy_ref[...] = dy
    d_gate = (d_gated * scanned * (sig * (1.0 + gate * (1.0 - sig)))).astype(bf16)
    d_gate = dot(s_out[...], d_gate, (1, 0)).astype(bf16)
    dgate_ref[...] = d_gate.reshape(dgate_ref.shape)
    dskip_ref[...] += jnp.sum(dy * vals, axis=0, keepdims=True)


def exit_kernel(
    span, taps, low_cols, starts_ref, dproj_ref, part_ref, pre_ref, x_ref, val_ref, cw_ref, xw_ref, dgate_ref, w_ref,
    hid_ref, scale_ref, gain_ref, ddtw_ref, dalog_ref, ddtb_ref, dskip_ref,
    dn_ref, din_ref, small_ref, dgain_ref, s_pre, s_dx, s_din, s_place,
):
    total, chans = x_ref.shape
    size = span * SEGS
    steps = total // SEGS
    turns = steps // span
    halo = (taps - 1) * SEGS
    groups, width = lane_groups(chans)
    turn = pl.program_id(0)

    @pl.when(turn == 0)
    def _():

        def first(t, carry):
            rows = block_rows(t, size)
            d_proj = dproj_ref[rows, :]
            d_values = part_ref[rows, :] + dot(d_proj, xw_ref[...], (1, 1))
            d_pre = d_values * silu_slope(pre_ref[rows, :])
            s_pre[rows, :] = d_pre
            s_place[rows, :] = context_positions(starts_ref, t * size, size, steps, width)
            d_bias, d_xw = carry
            return d_bias + jnp.sum(d_pre, axis=0, keepdims=True), d_xw + dot(d_proj, val_ref[rows, :], (0, 0))

        begin = (jnp.zeros((1, chans), f32), jnp.zeros((dproj_ref.shape[1], chans), f32))
        d_bias, d_xw = lax.fori_loop(0, turns, first, begin)
        s_place[total : total + halo, :] = context_positions(starts_ref, total, halo, steps, width)
        last = lax.broadcasted_iota(jnp.int32, (SEGS, chans), 0) == SEGS - 1
        for j in range(taps - 1):
            head = s_pre[j * SEGS : (j + 1) * SEGS, :]
            s_pre[total + j * SEGS : total + (j + 1) * SEGS, :] = jnp.where(last, 0.0, pltpu.roll(head, SEGS - 1, 0))
        back = mixing(span, True)

        def second(t, sums):
            rows = block_rows(t, size)
            x = x_ref[rows, :].astype(f32)
            d_x = jnp.zeros((size, chans), f32)
            out = []
            for k in range(taps):
                lag = taps - 1 - k
                at = pl.ds(pl.multiple_of(t * size + lag * SEGS, SEGS), size)
                valid = jnp.concatenate([s_place[at, :]] * groups, axis=1) >= lag
                later = jnp.where(valid, s_pre[at, :], 0.0)
                d_x = d_x + cw_ref[k : k + 1, :] * later
                out.append(sums[k] + jnp.sum(later * x, axis=0, keepdims=True))
            natural = dot(back, d_x.astype(bf16), (1, 0)).astype(bf16).reshape(SEGS, span, chans)
            s_dx[:, block_rows(t, span), :] = natural
            return tuple(out)

        sums = lax.fori_loop(0, turns, second, (jnp.zeros((1, chans), f32),) * taps)
        s_din[...] = jnp.zeros_like(s_din)
        dgain_ref[...] = jnp.zeros_like(dgain_ref)
        rest = [*sums, d_bias, ddtb_ref[...], dskip_ref[...]]
        pad = small_ref.shape[0] - low_cols - ddtw_ref.shape[0] - dalog_ref.shape[0] - len(rest)
        small = [d_xw[:low_cols], ddtw_ref[...], dalog_ref[...], *rest, jnp.zeros((pad, chans), f32)]
        small_ref[...] = jnp.concatenate(small, axis=0).astype(bf16)

    @pl.when(turn > 0)
    def _():
        rows = hid_ref.shape[0]
        per_segment = steps // rows if rows <= steps else 1
        if rows <= steps:
            here = pl.ds(pl.multiple_of((turn - 1) % per_segment * rows, rows), rows)
            d_x = s_dx[(turn - 1) // per_segment, here, :]
        else:
            d_x = s_dx[pl.ds((turn - 1) * (rows // steps), rows // steps)].reshape(rows, chans)
        both = jnp.concatenate([d_x, dgate_ref[...]], axis=1)
        d_normed = dot(both, w_ref[...], (1, 1)).astype(bf16)
        dn_ref[...] = d_normed
        unit = hid_ref[...].astype(f32) * jnp.concatenate([scale_ref[...]] * (hid_ref.shape[1] // 128), axis=1)
        dgain_ref[...] += jnp.sum(d_normed.astype(f32) * unit, axis=0, keepdims=True)
        s_din[...] += dot(d_x, (unit * gain_ref[...]).astype(bf16), (0, 0))

    @pl.when(turn == pl.num_programs(0) - 1)
    def _():
        din_ref[...] = s_din[...].T.astype(bf16)


def prepare_spread(hot_ref, rank, states):
    hot_ref[...] = jnp.zeros_like(hot_ref)
    row = lax.broadcasted_iota(jnp.int32, (16, 128), 0)
    for n in range(2 * states):
        first = (rank + n) // 16 * 16
        hot_ref[first : first + 16, n * 128 : (n + 1) * 128] = (row + first == rank + n).astype(f32).astype(bf16)


def spread_pair(out_ref, slot, hot_ref, proj_ref, rows, first, pair):
    at = first * 128 + pair * 256
    both = dot(proj_ref[rows, :], hot_ref[:, pl.ds(at if isinstance(at, int) else pl.multiple_of(at, 256), 256)], (1, 0))
    out_ref[slot, 2 * pair] = both[:, :128]
    out_ref[slot, 2 * pair + 1] = both[:, 128:]


def sum_lanes(mix_ref, hot_ref):
    return dot(hot_ref[...], mix_ref[...], (1, 1)).T


def forward_kernel(
    rank, states, span, proj_ref, val_ref, cut_ref, dtw_ref, dtb_ref, alog_ref,
    y_ref, hist_ref, delta_ref, s_cut, s_dx, s_rate, s_state, s_sum, s_b, s_c, s_hot,
):
    total, chans = val_ref.shape
    steps = total // SEGS
    size = span * SEGS
    groups, width = lane_groups(chans)
    turn = pl.program_id(0)
    turns = steps // span
    slots = s_b.shape[0]
    half = states // 2
    count = span // BATCH

    def rate(n, g):
        return s_rate[n : n + 1, g * width : (g + 1) * width]

    @pl.when(turn == 0)
    def _():
        s_rate[...] = -jnp.exp(alog_ref[...]) * LOG2E
        prepare_spread(s_hot, rank, states)
        s_state[...] = jnp.zeros_like(s_state)
        s_sum[...] = jnp.zeros_like(s_sum)
        def block(t, carry):
            rows = block_rows(t, size)
            slot = t if slots > 1 else 0
            for pair in range(half):
                spread_pair(s_b, slot, s_hot, proj_ref, rows, 0, pair)
                spread_pair(s_c, slot, s_hot, proj_ref, rows, states, pair)
            delta = softplus(dot(proj_ref[rows, :rank], dtw_ref[...], (1, 0)) + dtb_ref[...])
            put(delta_ref, rows, delta, groups, width)
            cut = cut_ref[rows, :].astype(f32) * CUT
            put(s_cut, rows, delta + jnp.concatenate([cut] * groups, axis=1), groups, width)
            put(s_dx, rows, delta * val_ref[rows, :].astype(f32), groups, width)

            def sweep(q, carry):
                at = [block_rows(t * span + q * BATCH + j, SEGS) for j in range(BATCH)]
                here = [block_rows(q * BATCH + j, SEGS) for j in range(BATCH)]
                for g in range(groups):
                    cuts = [s_cut[g, at[j], :] for j in range(BATCH)]
                    dxs = [s_dx[g, at[j], :] for j in range(BATCH)]
                    s_sum[g] = s_sum[g] + sum(cuts)
                    for n in range(states):
                        held = s_state[n * groups + g]
                        for j in range(BATCH):
                            push = dxs[j] * s_b[slot, n, here[j], :width]
                            held = jnp.exp2(cuts[j] * rate(n, g)) * held + push
                        s_state[n * groups + g] = held
                return carry

            return lax.fori_loop(0, count, sweep, carry)

        lax.fori_loop(0, turns, block, 0)
        first = lax.broadcasted_iota(jnp.int32, (SEGS, width), 0) == 0
        for n in range(states):
            for g in range(groups):
                gain = jnp.exp2(s_sum[g] * rate(n, g))
                end = s_state[n * groups + g]
                start = jnp.zeros((SEGS, width), f32)
                for _ in range(SEGS - 1):
                    start = jnp.where(first, 0.0, pltpu.roll(gain * start + end, 1, 0))
                s_state[n * groups + g] = start

    slot = turn if slots > 1 else 0
    if slots == 1:
        for pair in range(half):
            spread_pair(s_b, 0, s_hot, proj_ref, block_rows(turn, size), 0, pair)
            spread_pair(s_c, 0, s_hot, proj_ref, block_rows(turn, size), states, pair)

    def sweep(q, carry):
        at = [block_rows(turn * span + q * BATCH + j, SEGS) for j in range(BATCH)]
        here = [block_rows(q * BATCH + j, SEGS) for j in range(BATCH)]
        for g in range(groups):
            cuts = [s_cut[g, at[j], :] for j in range(BATCH)]
            dxs = [s_dx[g, at[j], :] for j in range(BATCH)]
            ys = [None] * BATCH
            for n in range(states):
                i = n * groups + g
                held = s_state[i]
                for j in range(BATCH):
                    hist_ref[0, q * BATCH + j, i] = held
                    push = dxs[j] * s_b[slot, n, here[j], :width]
                    held = jnp.exp2(cuts[j] * rate(n, g)) * held + push
                    term = held * s_c[slot, n, here[j], :width]
                    ys[j] = term if n == 0 else ys[j] + term
                s_state[i] = held
            for j in range(BATCH):
                y_ref[at[j], g * width : (g + 1) * width] = ys[j]
        return carry

    lax.fori_loop(0, count, sweep, 0)
    hist_ref[0, span] = s_state[...]


def backward_kernel(
    rank, states, span, proj_ref, val_ref, cut_ref, dy_ref, delta_ref, dtw_ref, dtwt_ref, dtb_ref, alog_ref, skip_ref,
    hist_ref, part_ref, dval_ref, ddtw_ref, ddtb_ref, dalog_ref,
    s_cut, s_val, s_dd, s_rate, s_state, s_sum, s_drate, s_b, s_c, s_mix, s_hot, s_bc,
):
    total, chans = val_ref.shape
    steps = total // SEGS
    size = span * SEGS
    groups, width = lane_groups(chans)
    turns = steps // span
    turn = pl.program_id(0)
    place = turns - 1 - turn
    slots = s_b.shape[0]
    half = states // 2
    count = span // BATCH
    lane = [slice(g * width, (g + 1) * width) for g in range(groups)]

    def rate(n, g):
        return s_rate[n : n + 1, lane[g]]

    @pl.when(turn == 0)
    def _():
        s_rate[...] = -jnp.exp(alog_ref[...]) * LOG2E
        s_drate[...] = jnp.zeros_like(s_drate)
        s_state[...] = jnp.zeros_like(s_state)
        s_sum[...] = jnp.zeros_like(s_sum)
        if width < 128:
            s_mix[...] = jnp.zeros_like(s_mix)
        prepare_spread(s_hot, rank, states)
        def block(turned, carry):
            t = turns - 1 - turned
            rows = block_rows(t, size)
            slot = t if slots > 1 else 0
            for pair in range(half):
                spread_pair(s_b, slot, s_hot, proj_ref, rows, 0, pair)
                spread_pair(s_c, slot, s_hot, proj_ref, rows, states, pair)
            cut = cut_ref[rows, :].astype(f32) * CUT
            delta = take(delta_ref, rows, groups)
            put(s_cut, rows, delta + jnp.concatenate([cut] * groups, axis=1), groups, width)
            put(s_val, rows, val_ref[rows, :].astype(f32), groups, width)

            def sweep(q, carry):
                k = span - BATCH - q * BATCH
                at = [block_rows(t * span + k + j, SEGS) for j in range(BATCH)]
                here = [block_rows(k + j, SEGS) for j in range(BATCH)]
                for g in range(groups):
                    cuts = [s_cut[g, at[j], :] for j in range(BATCH)]
                    dys = [dy_ref[at[j], lane[g]] for j in range(BATCH)]
                    s_sum[g] = s_sum[g] + sum(cuts)
                    for n in range(states):
                        held = s_state[n * groups + g]
                        for j in reversed(range(BATCH)):
                            held = dys[j] * s_c[slot, n, here[j], :width] + held
                            held = jnp.exp2(cuts[j] * rate(n, g)) * held
                        s_state[n * groups + g] = held
                return carry

            return lax.fori_loop(0, count, sweep, carry)

        lax.fori_loop(0, turns, block, 0)
        last = lax.broadcasted_iota(jnp.int32, (SEGS, width), 0) == SEGS - 1
        for n in range(states):
            for g in range(groups):
                gain = jnp.exp2(s_sum[g] * rate(n, g))
                end = s_state[n * groups + g]
                start = jnp.zeros((SEGS, width), f32)
                for _ in range(SEGS - 1):
                    start = jnp.where(last, 0.0, pltpu.roll(gain * start + end, SEGS - 1, 0))
                s_state[n * groups + g] = start

    slot = place if slots > 1 else 0
    if slots == 1:
        for pair in range(half):
            spread_pair(s_b, 0, s_hot, proj_ref, block_rows(place, size), 0, pair)
            spread_pair(s_c, 0, s_hot, proj_ref, block_rows(place, size), states, pair)

    def sweep(q, carry):
        k = span - BATCH - q * BATCH
        at = [block_rows(place * span + k + j, SEGS) for j in range(BATCH)]
        here = [block_rows(k + j, SEGS) for j in range(BATCH)]
        each = [(j, g) for j in range(BATCH) for g in range(groups)]
        cuts = {(j, g): s_cut[g, at[j], :] for j, g in each}
        deltas = {(j, g): delta_ref[g, at[j], :] for j, g in each}
        vals = {(j, g): s_val[g, at[j], :] for j, g in each}
        dys = {(j, g): dy_ref[at[j], lane[g]] for j, g in each}
        dxs = {e: deltas[e] * vals[e] for e in each}
        by_rate, by_b = {}, {}
        for first in range(0, states, TOGETHER):
            some = [(n, g) for n in range(first, first + TOGETHER) for g in range(groups)]
            held = {(n, g): s_state[n * groups + g] for n, g in some}
            d_rate = {(n, g): s_drate[n * groups + g] for n, g in some}
            after = {(n, g): hist_ref[0, k + BATCH, n * groups + g] for n, g in some}
            mix = {}
            for j in reversed(range(BATCH)):
                for n, g in some:
                    e, i = (j, g), (n, g)
                    b_n = s_b[slot, n, here[j], :width]
                    c_n = s_c[slot, n, here[j], :width]
                    before = hist_ref[0, k + j, n * groups + g]
                    lam = dys[e] * c_n + held[i]
                    held[i] = jnp.exp2(cuts[e] * rate(n, g)) * lam
                    through = held[i] * before
                    d_rate[i] = d_rate[i] + through * deltas[e]
                    terms = (through * rate(n, g), lam * b_n, lam * dxs[e], dys[e] * after[i])
                    by_rate[e] = by_rate[e] + terms[0] if e in by_rate else terms[0]
                    by_b[e] = by_b[e] + terms[1] if e in by_b else terms[1]
                    for m, term in ((n, terms[2]), (states + n, terms[3])):
                        mix[j, m] = mix[j, m] + term if (j, m) in mix else term
                    after[i] = before
                if j % 2 == 0:
                    two = pl.ds(pl.multiple_of((k + j) * SEGS, 2 * SEGS), 2 * SEGS)
                    for n in range(first, first + TOGETHER):
                        for m in (n, states + n):
                            value = jnp.concatenate([mix[j, m], mix[j + 1, m]], axis=0).astype(bf16)
                            s_mix[two, m * 128 : m * 128 + width] = value
            for n, g in some:
                s_state[n * groups + g] = held[n, g]
                s_drate[n * groups + g] = d_rate[n, g]
        for j, g in each:
            e = (j, g)
            s_dd[g, at[j], :] = by_rate[e] * (1.0 / LOG2E) + by_b[e] * vals[e]
            dval_ref[at[j], lane[g]] = by_b[e] * deltas[e] + dys[e] * skip_ref[:, lane[g]]
        return carry

    lax.fori_loop(0, count, sweep, 0)
    rows = block_rows(place, size)
    s_bc[...] = sum_lanes(s_mix, s_hot)
    pre = dot(proj_ref[rows, :rank], dtw_ref[...], (1, 0)) + dtb_ref[...]
    d_pre = take(s_dd, rows, groups) * jax.nn.sigmoid(pre)
    d_bias = jnp.sum(d_pre, axis=0, keepdims=True)
    d_dtw = split_dot(d_pre, proj_ref[rows, :rank], (0, 0), swapped=True)
    part = split_dot(d_pre, dtwt_ref[...], (1, 0))
    part_ref[rows, :] = (part + s_bc[...]).astype(bf16)

    @pl.when(turn == 0)
    def _():
        ddtb_ref[...] = d_bias
        ddtw_ref[...] = d_dtw

    @pl.when(turn > 0)
    def _():
        ddtb_ref[...] += d_bias
        ddtw_ref[...] += d_dtw

    @pl.when(turn == turns - 1)
    def _():
        sums = [jnp.sum(s_drate[i], axis=0, keepdims=True) for i in range(states * groups)]
        rows = [jnp.concatenate(sums[n * groups : (n + 1) * groups], axis=1) for n in range(states)]
        dalog_ref[...] = jnp.concatenate(rows, axis=0) * s_rate[...] * (1.0 / LOG2E)


def scan_kernel(
    rank, states, span, proj_ref, val_ref, gate_ref, cut_ref, grad_ref, w_ref, dtw_ref, dtwt_ref, dtb_ref, alog_ref,
    skip_ref, branch_ref, gated_ref, dgate_ref, part_ref, dval_ref, ddtw_ref, ddtb_ref, dalog_ref, dskip_ref,
    s_cut, s_delta, s_val, s_dy, s_hist, s_b, s_c, s_y, s_rate, s_state, s_drate, s_mix, s_hot, s_in, s_out,
):
    total, chans = val_ref.shape
    steps = total // SEGS
    size = span * SEGS
    groups, width = lane_groups(chans)
    pairs = [(n, g) for n in range(states) for g in range(groups)]
    every = range(groups)
    lane = [slice(g * width, (g + 1) * width) for g in every]
    turns = steps // span
    turn = pl.program_id(0)
    zero = jnp.zeros((SEGS, width), f32)
    sublane = lax.broadcasted_iota(jnp.int32, (SEGS, width), 0)

    def decay(cut, n, g):
        return jnp.exp2(cut * s_rate[n : n + 1, lane[g]])

    def chained(ends, sums, edge, shift):
        for n, g in pairs:
            gain = decay(sums[g], n, g)
            end = ends[n * groups + g]
            start = zero
            for _ in range(SEGS - 1):
                start = jnp.where(sublane == edge, 0.0, pltpu.roll(gain * start + end, shift, 0))
            s_state[n * groups + g] = start

    @pl.when(turn == 0)
    def _():
        s_rate[...] = -jnp.exp(alog_ref[...]) * LOG2E
        s_drate[...] = jnp.zeros_like(s_drate)
        dskip_ref[...] = jnp.zeros_like(dskip_ref)
        s_in[...] = mixing(span, False)
        s_out[...] = mixing(span, True)
        prepare_spread(s_hot, rank, states)

        def fill(t, carry):
            rows = block_rows(t, size)
            for n in range(0, states, 2):
                for ref, first in ((s_b, n), (s_c, states + n)):
                    both = dot(proj_ref[rows, :], s_hot[:, first * 128 : (first + 2) * 128], (1, 0))
                    ref[n, rows, :] = both[:, :128]
                    ref[n + 1, rows, :] = both[:, 128:]
            delta = softplus(dot(proj_ref[rows, :rank], dtw_ref[...], (1, 0)) + dtb_ref[...])
            cut = cut_ref[rows, :].astype(f32) * CUT
            put(s_delta, rows, delta, groups, width)
            put(s_cut, rows, delta + jnp.concatenate([cut] * groups, axis=1), groups, width)
            put(s_val, rows, val_ref[rows, :].astype(f32), groups, width)
            return carry

        lax.fori_loop(0, turns, fill, 0)

        def sweep(i, carry):
            held, sums = carry
            at = block_rows(i, SEGS)
            cuts = [s_cut[g, at, :] for g in every]
            dxs = [s_delta[g, at, :] * s_val[g, at, :] for g in every]
            out = [decay(cuts[g], n, g) * held[n * groups + g] + dxs[g] * s_b[n, at, :width] for n, g in pairs]
            return tuple(out), tuple(sums[g] + cuts[g] for g in every)

        begin = ((zero,) * len(pairs), (zero,) * groups)
        chained(*lax.fori_loop(0, steps, sweep, begin, unroll=4), 0, 1)

    @pl.when(turn < turns)
    def _():

        def sweep(k, held):
            i = turn * span + k
            at = block_rows(i, SEGS)
            cuts = [s_cut[g, at, :] for g in every]
            dxs = [s_delta[g, at, :] * s_val[g, at, :] for g in every]
            ys = [zero] * groups
            out = []
            for n in range(states):
                b_n = s_b[n, at, :width]
                c_n = s_c[n, at, :width]
                for g in every:
                    old = held[n * groups + g]
                    s_hist[i, n * groups + g] = old
                    new = decay(cuts[g], n, g) * old + dxs[g] * b_n
                    out.append(new)
                    ys[g] = ys[g] + new * c_n
            for g in every:
                s_y[block_rows(k, SEGS), lane[g]] = ys[g]
            return tuple(out)

        held = lax.fori_loop(0, span, sweep, tuple(s_state[j] for j in range(len(pairs))), unroll=4)
        for j in range(len(pairs)):
            s_state[j] = held[j]

        @pl.when(turn == turns - 1)
        def _():
            s_hist[steps] = s_state[...]

        rows = block_rows(turn, size)
        vals = val_ref[rows, :].astype(f32)
        gate = gate_ref[rows, :].astype(f32)
        sig = jax.nn.sigmoid(gate)
        act = gate * sig
        scanned = s_y[...] + skip_ref[...] * vals
        gated = dot(s_out[...], (scanned * act).astype(bf16), (1, 0)).astype(bf16)
        gated_ref[...] = gated.reshape(gated_ref.shape)
        branch_ref[...] = dot(gated, w_ref[...], (1, 0)).astype(bf16).reshape(branch_ref.shape)
        grad = grad_ref[...].reshape(size, grad_ref.shape[2])
        d_gated = dot(s_in[...], dot(grad, w_ref[...], (1, 1)).astype(bf16), (1, 0))
        dy = d_gated * act
        put(s_dy, rows, dy, groups, width)
        d_gate = (d_gated * scanned * (sig * (1.0 + gate * (1.0 - sig)))).astype(bf16)
        dgate_ref[...] = dot(s_out[...], d_gate, (1, 0)).astype(bf16).reshape(dgate_ref.shape)
        dskip_ref[...] += jnp.sum(dy * vals, axis=0, keepdims=True)

    @pl.when(turn == turns)
    def _():
        ddtb_ref[...] = jnp.zeros_like(ddtb_ref)
        ddtw_ref[...] = jnp.zeros_like(ddtw_ref)

        def sweep(back, carry):
            held, sums = carry
            at = block_rows(steps - 1 - back, SEGS)
            cuts = [s_cut[g, at, :] for g in every]
            dys = [s_dy[g, at, :] for g in every]
            out = []
            for n, g in pairs:
                lam = dys[g] * s_c[n, at, :width] + held[n * groups + g]
                out.append(decay(cuts[g], n, g) * lam)
            return tuple(out), tuple(sums[g] + cuts[g] for g in every)

        begin = ((zero,) * len(pairs), (zero,) * groups)
        chained(*lax.fori_loop(0, steps, sweep, begin, unroll=4), SEGS - 1, SEGS - 1)

    @pl.when(turn >= turns)
    def _():
        place = 2 * turns - 1 - turn

        def sweep(back, held):
            k = span - 1 - back
            i = place * span + k
            at = block_rows(i, SEGS)
            cuts = [s_cut[g, at, :] for g in every]
            deltas = [s_delta[g, at, :] for g in every]
            vals = [s_val[g, at, :] for g in every]
            dys = [s_dy[g, at, :] for g in every]
            dxs = [deltas[g] * vals[g] for g in every]
            by_rate = [zero] * groups
            by_b = [zero] * groups
            out = []
            mixes = {}
            for n in range(states):
                b_n = s_b[n, at, :width]
                c_n = s_c[n, at, :width]
                mix = mix_c = None
                for g in every:
                    j = n * groups + g
                    lam = dys[g] * c_n + held[j]
                    onward = decay(cuts[g], n, g) * lam
                    out.append(onward)
                    through = onward * s_hist[i, j]
                    by_rate[g] = by_rate[g] + through * s_rate[n : n + 1, lane[g]]
                    by_b[g] = by_b[g] + lam * b_n
                    s_drate[j] = s_drate[j] + through * deltas[g]
                    term, term_c = lam * dxs[g], dys[g] * s_hist[i + 1, j]
                    mix = term if mix is None else mix + term
                    mix_c = term_c if mix_c is None else mix_c + term_c
                mixes[n], mixes[states + n] = mix, mix_c
                if n % 2:
                    for first in (n - 1, states + n - 1):
                        two = jnp.concatenate([mixes[first], mixes[first + 1]], axis=0).astype(bf16)
                        s_mix[block_rows(k, 2 * SEGS), first * 64 : first * 64 + width] = two
            for g in every:
                s_cut[g, at, :] = by_rate[g] * (1.0 / LOG2E) + by_b[g] * vals[g]
                dval_ref[at, lane[g]] = by_b[g] * deltas[g] + dys[g] * skip_ref[:, lane[g]]
            return tuple(out)

        held = lax.fori_loop(0, span, sweep, tuple(s_state[j] for j in range(len(pairs))), unroll=4)
        for j in range(len(pairs)):
            s_state[j] = held[j]
        rows = block_rows(place, size)
        pre = dot(proj_ref[rows, :rank], dtw_ref[...], (1, 0)) + dtb_ref[...]
        d_pre = take(s_cut, rows, groups) * jax.nn.sigmoid(pre)
        ddtb_ref[...] += jnp.sum(d_pre, axis=0, keepdims=True)
        ddtw_ref[...] += split_dot(d_pre, proj_ref[rows, :rank], (0, 0), swapped=True)
        part = split_dot(d_pre, dtwt_ref[...], (1, 0))
        even = jnp.concatenate([s_hot[:, n * 128 : (n + 1) * 128] for n in range(0, 2 * states, 2)], axis=1)
        found = dot(s_mix[...], even, (1, 1)).reshape(span, 2, SEGS, part_ref.shape[1])
        odd = pltpu.roll(found[:, 1].reshape(size, part_ref.shape[1]), 1, 1)
        part_ref[rows, :] = (part + found[:, 0].reshape(size, part_ref.shape[1]) + odd).astype(bf16)

    @pl.when(turn == 2 * turns - 1)
    def _():
        sums = [jnp.sum(s_drate[i], axis=0, keepdims=True) for i in range(states * groups)]
        rows = [jnp.concatenate(sums[n * groups : (n + 1) * groups], axis=1) for n in range(states)]
        dalog_ref[...] = jnp.concatenate(rows, axis=0) * s_rate[...] * (1.0 / LOG2E)


def scan_span(steps):
    return math.gcd(steps, 32)


def wide_slots(steps, span, states):
    turns = steps // span
    return turns if turns * 2 * states * span * SEGS * 128 * 4 <= 16 * MIB else 1


def whole(*shape):
    return pl.BlockSpec(shape, lambda *t: (0,) * len(shape))


def like(*shape, dtype=f32):
    return jax.ShapeDtypeStruct(shape, dtype)


def about(micros):
    return pl.CostEstimate(flops=int(micros * 1.1e9), bytes_accessed=1 << 20, transcendentals=0)


SCALARS = pl.BlockSpec(memory_space=pltpu.SMEM)


def run_entry(starts, hidden_all, weight, gain, conv_w, conv_b, x_w, span):
    total, width = hidden_all.shape
    taps, chans = conv_w.shape
    lanes = x_w.shape[1]
    steps = total // SEGS
    segments = pl.BlockSpec((SEGS, span, width), lambda t: (0, t, 0))
    normed, scale, *rest = pl.pallas_call(
        functools.partial(entry_kernel, span, taps, lanes),
        grid=(steps // span,),
        in_specs=[
            SCALARS, segments, whole(width, 2 * chans), whole(1, width), whole(taps, chans), whole(1, chans),
            whole(chans, lanes),
        ],
        out_specs=[segments, pl.BlockSpec((SEGS, span, 128), lambda t: (0, t, 0))]
        + [whole(total, chans)] * 4 + [whole(total, lanes)],
        out_shape=[like(SEGS, steps, width, dtype=bf16), like(SEGS, steps, 128)] + [like(total, chans, dtype=bf16)] * 3
        + [like(total, chans), like(total, lanes, dtype=bf16)],
        scratch_shapes=[
            pltpu.VMEM((total + (taps - 1) * SEGS, chans), f32), pltpu.VMEM((span * SEGS, span * SEGS), bf16),
        ],
        compiler_params=pltpu.CompilerParams(vmem_limit_bytes=ROOM),
        cost_estimate=about(6 * total * chans / 262144),
        name="entry",
    )(starts, hidden_all.reshape(SEGS, steps, width), weight, gain, conv_w, conv_b, x_w)
    return (normed, scale.reshape(total, 128), *rest)


def run_gate(grad_all, out_w, gate, values, y, skip, span):
    total, width = grad_all.shape
    chans = gate.shape[1]
    steps = total // SEGS
    rows = pl.BlockSpec((span * SEGS, chans), lambda t: (t, 0))
    part = pl.BlockSpec((SEGS, span, chans), lambda t: (0, t, 0))
    full = pl.BlockSpec((SEGS, span, width), lambda t: (0, t, 0))
    natural = like(SEGS, steps, chans, dtype=bf16)
    branch, gated, dy, d_gate, d_skip = pl.pallas_call(
        functools.partial(gate_kernel, span),
        grid=(steps // span,),
        in_specs=[full, whole(chans, width), rows, rows, rows, whole(1, chans)],
        out_specs=[full, part, rows, part, whole(1, chans)],
        out_shape=[like(SEGS, steps, width, dtype=bf16), natural, like(total, chans), natural, like(1, chans)],
        scratch_shapes=[pltpu.VMEM((span * SEGS, span * SEGS), bf16)] * 2,
        compiler_params=pltpu.CompilerParams(vmem_limit_bytes=ROOM),
        cost_estimate=about(6 * total * chans / 262144),
        name="gate",
    )(grad_all.reshape(SEGS, steps, width), out_w, gate, values, y, skip)
    return branch.reshape(total, width), gated.reshape(total, chans), dy, d_gate.reshape(total, chans), d_skip


def run_scan(proj, values, gate, cut, grad_all, out_w, dt_weight, dt_weight_t, dt_bias, a_log_t, skip, states, span):
    total, chans = values.shape
    width_all = grad_all.shape[1]
    rank = dt_weight.shape[0]
    steps = total // SEGS
    groups, width = lane_groups(chans)
    count = states * groups
    lanes = proj.shape[1]
    turns = steps // span
    size = span * SEGS
    by_group = pltpu.VMEM((groups, total, width), f32)
    spread = pltpu.VMEM((states, total, 128), f32)
    held = pltpu.VMEM((count, SEGS, width), f32)
    order = pltpu.VMEM((size, size), bf16)
    part = pl.BlockSpec((SEGS, span, chans), lambda t: (0, jnp.minimum(t, turns - 1), 0))
    full = pl.BlockSpec((SEGS, span, width_all), lambda t: (0, jnp.minimum(t, turns - 1), 0))
    natural = like(SEGS, steps, chans, dtype=bf16)
    branch, gated, d_gate, *rest = pl.pallas_call(
        functools.partial(scan_kernel, rank, states, span),
        grid=(2 * turns,),
        in_specs=[
            whole(total, lanes), whole(total, chans), whole(total, chans), whole(total, width), full,
            whole(chans, width_all), whole(rank, chans), whole(chans, lanes), whole(1, chans), whole(states, chans),
            whole(1, chans),
        ],
        out_specs=[
            full, part, part, whole(total, lanes), whole(total, chans), whole(rank, chans), whole(1, chans),
            whole(states, chans), whole(1, chans),
        ],
        out_shape=[
            like(SEGS, steps, width_all, dtype=bf16), natural, natural, like(total, lanes, dtype=bf16),
            like(total, chans), like(rank, chans), like(1, chans), like(states, chans), like(1, chans),
        ],
        scratch_shapes=[
            by_group, by_group, by_group, by_group, pltpu.VMEM((steps + 1, count, SEGS, width), f32), spread, spread,
            pltpu.VMEM((size, chans), f32), pltpu.VMEM((states, chans), f32), held, held,
            pltpu.VMEM((2 * size, states * 128), bf16), pltpu.VMEM((lanes, 2 * states * 128), bf16), order, order,
        ],
        compiler_params=pltpu.CompilerParams(vmem_limit_bytes=ROOM),
        cost_estimate=about(38),
        name="scan",
    )(proj, values, gate, cut, grad_all.reshape(SEGS, steps, width_all), out_w, dt_weight, dt_weight_t, dt_bias, a_log_t, skip)
    return (branch.reshape(total, width_all), gated.reshape(total, chans), d_gate.reshape(total, chans), *rest)


def run_exit(
    starts, d_proj, value_part, pre, x_in, values, conv_w, x_w, d_gate, weight, hidden_all, scale, gain,
    d_dtw, d_alog_t, d_dtb, d_skip, low_cols, small_rows, span,
):
    total, chans = x_in.shape
    taps = conv_w.shape[0]
    lanes = x_w.shape[1]
    width = hidden_all.shape[1]
    steps = total // SEGS
    size = math.gcd(total, 256)

    def rows(lanes):
        return pl.BlockSpec((size, lanes), lambda t: (jnp.maximum(t - 1, 0), 0))

    return pl.pallas_call(
        functools.partial(exit_kernel, span, taps, low_cols),
        grid=(1 + total // size,),
        in_specs=[SCALARS, whole(total, lanes)] + [whole(total, chans)] * 4 + [
            whole(taps, chans), whole(chans, lanes), rows(chans), whole(width, 2 * chans), rows(width), rows(128),
            whole(1, width), whole(*d_dtw.shape), whole(*d_alog_t.shape), whole(1, chans), whole(1, chans),
        ],
        out_specs=[rows(width), whole(width, chans), whole(small_rows, chans), whole(1, width)],
        out_shape=[
            like(total, width, dtype=bf16), like(width, chans, dtype=bf16), like(small_rows, chans, dtype=bf16),
            like(1, width),
        ],
        scratch_shapes=[
            pltpu.VMEM((total + (taps - 1) * SEGS, chans), f32), pltpu.VMEM((SEGS, steps, chans), bf16),
            pltpu.VMEM((chans, width), f32), pltpu.VMEM((total + (taps - 1) * SEGS, lane_groups(chans)[1]), jnp.int32),
        ],
        compiler_params=pltpu.CompilerParams(vmem_limit_bytes=ROOM),
        cost_estimate=about(10 * total * chans / 262144),
        name="exit",
    )(
        starts, d_proj, value_part, pre, x_in, values, conv_w, x_w, d_gate, weight, hidden_all, scale, gain,
        d_dtw, d_alog_t, d_dtb, d_skip,
    )


def run_forward(proj, values, cut, dt_weight, dt_bias, a_log_t, states, span):
    total, chans = values.shape
    rank = dt_weight.shape[0]
    steps = total // SEGS
    groups, width = lane_groups(chans)
    count = states * groups
    lanes = proj.shape[1]
    slots = wide_slots(steps, span, states)
    by_group = pltpu.VMEM((groups, total, width), f32)
    return pl.pallas_call(
        functools.partial(forward_kernel, rank, states, span),
        grid=(steps // span,),
        in_specs=[
            whole(total, lanes), whole(total, chans), whole(total, width), whole(rank, chans), whole(1, chans),
            whole(states, chans),
        ],
        out_specs=[
            whole(total, chans), pl.BlockSpec((1, span + 1, count, SEGS, width), lambda t: (t, 0, 0, 0, 0)),
            whole(groups, total, width),
        ],
        out_shape=[
            like(total, chans), like(steps // span, span + 1, count, SEGS, width), like(groups, total, width),
        ],
        scratch_shapes=[
            by_group, by_group, pltpu.VMEM((states, chans), f32), pltpu.VMEM((count, SEGS, width), f32),
            pltpu.VMEM((groups, SEGS, width), f32),
            pltpu.VMEM((slots, states, span * SEGS, 128), f32),
            pltpu.VMEM((slots, states, span * SEGS, 128), f32), pltpu.VMEM((lanes, 2 * states * 128), bf16),
        ],
        compiler_params=pltpu.CompilerParams(vmem_limit_bytes=ROOM),
        cost_estimate=about(18 * total * chans / 262144),
        name="scan_forward",
    )(proj, values, cut, dt_weight, dt_bias, a_log_t)


def run_backward(proj, values, cut, dy, delta, dt_weight, dt_weight_t, dt_bias, a_log_t, skip, hist, states, span):
    total, chans = values.shape
    rank = dt_weight.shape[0]
    steps = total // SEGS
    groups, width = lane_groups(chans)
    count = states * groups
    lanes = proj.shape[1]
    turns = steps // span
    slots = wide_slots(steps, span, states)
    by_group = pltpu.VMEM((groups, total, width), f32)
    return pl.pallas_call(
        functools.partial(backward_kernel, rank, states, span),
        grid=(turns,),
        in_specs=[
            whole(total, lanes), whole(total, chans), whole(total, width), whole(total, chans), whole(groups, total, width),
            whole(rank, chans), whole(chans, lanes), whole(1, chans), whole(states, chans), whole(1, chans),
            pl.BlockSpec((1, span + 1, count, SEGS, width), lambda t: (turns - 1 - t, 0, 0, 0, 0)),
        ],
        out_specs=[
            whole(total, lanes), whole(total, chans), whole(rank, chans), whole(1, chans), whole(states, chans),
        ],
        out_shape=[
            like(total, lanes, dtype=bf16), like(total, chans), like(rank, chans), like(1, chans), like(states, chans),
        ],
        scratch_shapes=[
            by_group, by_group, by_group, pltpu.VMEM((states, chans), f32),
            pltpu.VMEM((count, SEGS, width), f32), pltpu.VMEM((groups, SEGS, width), f32),
            pltpu.VMEM((count, SEGS, width), f32),
            pltpu.VMEM((slots, states, span * SEGS, 128), f32),
            pltpu.VMEM((slots, states, span * SEGS, 128), f32), pltpu.VMEM((span * SEGS, 2 * states * 128), bf16),
            pltpu.VMEM((lanes, 2 * states * 128), bf16), pltpu.VMEM((span * SEGS, lanes), f32),
        ],
        compiler_params=pltpu.CompilerParams(vmem_limit_bytes=ROOM),
        cost_estimate=about(22 * total * chans / 262144),
        name="scan_backward",
    )(proj, values, cut, dy, delta, dt_weight, dt_weight_t, dt_bias, a_log_t, skip, hist)


def tree_sum(parts):
    parts = [p.astype(f32) for p in parts]
    while len(parts) > 1:
        parts = [parts[i] + parts[i + 1] for i in range(0, len(parts), 2)]
    return parts[0]


def swap(value, axis, mask):
    return lax.ppermute(value, axis, [(i, i ^ mask) for i in range(lax.axis_size(axis))])


def pick(blocks, index, dim=0):
    return lax.dynamic_index_in_dim(blocks, index, dim, keepdims=False)


def collected(pieces, me):
    out = jnp.zeros((len(pieces),) + pieces[0].shape, pieces[0].dtype)
    for d, piece in enumerate(pieces):
        out = lax.dynamic_update_index_in_dim(out, piece, me ^ d, 0)
    return out


def owned_parts(blocks, axis):
    me = lax.axis_index(axis)
    size = lax.axis_size(axis)
    return [pick(blocks, me)] + [swap(pick(blocks, me ^ d), axis, d) for d in range(1, size)]


def collect(value, axis):
    me = lax.axis_index(axis)
    return collected([value] + [swap(value, axis, d) for d in range(1, lax.axis_size(axis))], me)


def sum_over_peers(part):
    peers = lax.axis_size("ch")
    rows, lanes = part.shape
    if peers != 8:
        got = lax.all_to_all(part.reshape(peers, rows // peers, lanes), "ch", split_axis=0, concat_axis=0, tiled=True)
        return lax.all_gather(got.astype(f32).sum(axis=0).astype(bf16), "ch", axis=0, tiled=True)
    core, chip = lax.axis_index("ch") % 2, lax.axis_index("ch") // 2
    chips = peers // 2
    halves = part.reshape(2, chips, rows // peers, lanes)
    got = swap(pick(halves, 1 - core), "ch", 1)
    half = tree_sum([pick(halves, core), got]).astype(bf16)
    pieces = [pick(half, chip)] + [swap(pick(half, chip ^ d), "ch", 2 * d) for d in range(1, chips)]
    own = tree_sum(pieces).astype(bf16)
    half = collected([own] + [swap(own, "ch", 2 * d) for d in range(1, chips)], chip)
    return collected([half, swap(half, "ch", 1)], core).reshape(rows, lanes)


def to_peers(blocks):
    return lax.all_to_all(blocks, "ch", split_axis=0, concat_axis=0, tiled=True)


def finish_kernel(
    parts, me_ref, *refs,
):
    n = parts
    late, outs, (cross_ref, branch_ref, dn_ref, hid_ref, grad_ref, gain_ref) = refs[:n], refs[n : 2 * n], refs[2 * n : 2 * n + 6]
    (out_ref, dh_ref, dgain_ref, din_ref, dcw_ref, dcb_ref, dxw_ref, ddtw_ref, ddtb_ref, dalog_ref, dskip_ref,
     dout_ref, s_small) = refs[2 * n + 6 :]
    chans = dcb_ref.shape[1]
    inner = din_ref.shape[1] // 2
    share = din_ref.shape[0] // n
    peers = inner // chans
    low_cols, rank, states, taps = dxw_ref.shape[0], ddtw_ref.shape[0], dalog_ref.shape[0], dcw_ref.shape[0]
    for d in range(n):
        who = jnp.bitwise_xor(me_ref[0], d)
        rows = block_rows(who, share)
        for p in range(peers):
            block = late[d][p * 2 * share : (p + 1) * 2 * share, :].astype(f32)
            din_ref[rows, p * chans : (p + 1) * chans] = block[:share]
            din_ref[rows, inner + p * chans : inner + (p + 1) * chans] = block[share:]
        small = late[d][2 * share * peers :, :].astype(f32)
        s_small[block_rows(who, small.shape[0]), :] = small
        dout_ref[block_rows(who, outs[d].shape[0]), :] = outs[d][...].astype(f32)
    gain = jnp.sum(cross_ref[:, 2 * share :, :].astype(f32), axis=0)
    dgain_ref[...] = gain[:1, : dgain_ref.shape[1]]
    at = low_cols + rank
    ddtw_ref[...] = s_small[low_cols:at, :]
    dxw_ref[...] = s_small[:low_cols, :]
    tail = s_small[at:, :]
    dalog_ref[...] = tail[:states]
    dcw_ref[...] = tail[states : states + taps]
    at = states + taps
    dcb_ref[...] = tail[at : at + 1]
    ddtb_ref[...] = tail[at + 1 : at + 2]
    dskip_ref[...] = tail[at + 2 : at + 3]
    hidden = hid_ref[...].astype(f32)
    out_ref[...] = (hidden + branch_ref[...].astype(f32)).astype(bf16)
    scale = lax.rsqrt(jnp.mean(hidden * hidden, axis=1, keepdims=True) + eps)
    unit = hidden * scale
    d_unit = dn_ref[...].astype(f32) * gain_ref[...]
    mean = jnp.mean(d_unit * unit, axis=1, keepdims=True)
    dh_ref[...] = (grad_ref[...].astype(f32) + scale * (d_unit - unit * mean)).astype(bf16)


def run_finish(late, outs, cross, branch, d_normed, hidden, grad, gain, sizes, me):
    rows, width = hidden.shape
    low_cols, rank, states, taps, small_rows = sizes
    packs = len(late)
    chans = late[0].shape[1]
    in_rows = width // cross.shape[0]
    inner = chans * cross.shape[0]
    wide = [*late, *outs, cross, branch, d_normed, hidden, grad, gain]
    shapes = [
        like(rows, width, dtype=bf16), like(rows, width, dtype=bf16), like(1, in_rows), like(in_rows, 2 * inner),
        like(taps, chans), like(1, chans), like(low_cols, chans), like(rank, chans), like(1, chans),
        like(states, chans), like(1, chans), like(chans, width),
    ]
    return pl.pallas_call(
        functools.partial(finish_kernel, packs),
        grid=(1,),
        in_specs=[SCALARS] + [whole(*a.shape) for a in wide],
        out_specs=[whole(*a.shape) for a in shapes],
        out_shape=shapes,
        scratch_shapes=[pltpu.VMEM((small_rows, chans), f32)],
        compiler_params=pltpu.CompilerParams(vmem_limit_bytes=ROOM),
        cost_estimate=about(4),
        name="finish",
    )(me[None], *wide)


def finish_plain(late, outs, cross, branch, d_normed, hidden, grad, gain, sizes, me):
    low_cols, rank, states, taps, small_rows = sizes
    packs, peers, chans = len(late), cross.shape[0], late[0].shape[1]
    share = hidden.shape[1] // (peers * packs)
    late = collected(late, me).astype(f32)
    halves = late[:, : 2 * share * peers].reshape(packs, peers, 2, share, chans)
    d_in = jnp.transpose(halves, (0, 3, 2, 1, 4)).reshape(packs * share, 2 * peers * chans)
    small = late[:, 2 * share * peers :].reshape(small_rows, chans)
    parts = []
    at = 0
    for count in (low_cols, rank, states, taps, 1, 1, 1):
        parts.append(small[at : at + count])
        at += count
    d_xw, d_dtw, d_alog, d_cw, d_cb, d_dtb, d_skip = parts
    d_gain = cross[:, 2 * share :].astype(f32).sum(axis=0).reshape(1, -1)[:, : share * packs]
    hidden = hidden.astype(f32)
    output = (hidden + branch.astype(f32)).astype(bf16)
    scale = lax.rsqrt(jnp.mean(hidden * hidden, axis=1, keepdims=True) + eps)
    unit = hidden * scale
    d_unit = d_normed.astype(f32) * gain
    mean = jnp.mean(d_unit * unit, axis=1, keepdims=True)
    d_hidden = (grad.astype(f32) + scale * (d_unit - unit * mean)).astype(bf16)
    d_out = collected(outs, me).astype(f32).reshape(chans, -1)
    return output, d_hidden, d_gain, d_in, d_cw, d_cb, d_xw, d_dtw, d_dtb, d_alog, d_skip, d_out


def on_device(
    hidden_in, norm_gain, in_weight, conv_weight, conv_bias, x_weight, dt_weight, dt_bias, a_log, skip, out_weight,
    lengths, resets, out_grad,
):
    peers = lax.axis_size("ch")
    packs = lax.axis_size("ctx")
    me = lax.axis_index("ch")
    rows, width = hidden_in.shape
    chans = out_weight.shape[0]
    taps = conv_weight.shape[1]
    rank, states = dt_weight.shape[0], a_log.shape[1]
    total = rows * peers

    hidden_all = lax.all_gather(hidden_in, "ch", axis=0, tiled=True)
    in_rows = in_weight.shape[0]
    share = in_rows // packs
    my_share = lax.dynamic_slice_in_dim(in_weight, lax.axis_index("ctx") * share, share, 0)
    got = to_peers(jnp.moveaxis(my_share.reshape(share, 2, peers, chans), 2, 0))
    shares = collect(got.reshape(peers, share, 2 * chans), "ctx")
    my_cols = jnp.moveaxis(shares, 0, 1).reshape(width, 2 * chans)
    grad_all = lax.all_gather(out_grad, "ch", axis=0, tiled=True)

    steps = total // SEGS
    span = scan_span(steps)
    low_cols = rank + 2 * states
    lanes = -(-low_cols // 128) * 128
    sizes = lengths[0]
    offsets = jnp.cumsum(sizes) - sizes
    where_in = context_place(offsets, jnp.arange(total, dtype=jnp.int32))
    cut = ((where_in == 0) | (resets == 1)).astype(bf16).reshape(SEGS, steps).T.reshape(total, 1)
    cut = jnp.broadcast_to(cut, (total, lane_groups(chans)[1]))
    starts = offsets[None, :]
    conv_w = lax.dynamic_slice_in_dim(conv_weight, me * chans, chans, 0).T
    conv_b = lax.dynamic_slice_in_dim(conv_bias, me * chans, chans, 0)[None, :]
    x_w = lax.dynamic_slice_in_dim(x_weight, me * chans, chans, 0)
    x_w = jnp.pad(x_w, ((0, 0), (0, lanes - low_cols)))

    normed, scale_all, x_in, gate, values, pre, proj_part = run_entry(
        starts, hidden_all, my_cols, norm_gain[None, :], conv_w, conv_b, x_w, span
    )
    proj = sum_over_peers(proj_part)

    a_log_t = a_log.T
    dt_b, skip_row = dt_bias[None, :], skip[None, :]
    dt_w_t = jnp.pad(dt_weight.T, ((0, 0), (0, lanes - rank)))
    if total * chans * states <= 1 << 22 and chans % 128 == 0:
        (
            branch_part, gated, d_gate, d_part, value_part, d_dt_weight, d_dt_bias, d_a_log_t, d_skip,
        ) = run_scan(
            proj, values, gate, cut, grad_all, out_weight, dt_weight, dt_w_t, dt_b, a_log_t, skip_row, states, span
        )
    else:
        y, hist, delta = run_forward(proj, values, cut, dt_weight, dt_b, a_log_t, states, span)
        branch_part, gated, dy, d_gate, d_skip = run_gate(grad_all, out_weight, gate, values, y, skip_row, span)
        d_part, value_part, d_dt_weight, d_dt_bias, d_a_log_t = run_backward(
            proj, values, cut, dy, delta, dt_weight, dt_w_t, dt_b, a_log_t, skip_row, hist, states, span
        )
    branch = lax.psum_scatter(branch_part, "ch", scatter_dimension=0, tiled=True)
    sides = width // chans
    out_share = chans // packs
    d_out = dot(gated, grad_all, (0, 0)).astype(bf16).reshape(packs, out_share, sides, chans)
    d_out = jnp.moveaxis(d_out, 2, 1).reshape(packs, out_share * sides, chans)
    d_in_gate = dot(normed.reshape(total, width), d_gate, (0, 0)).astype(bf16)

    def by_pack(d_in):
        return jnp.moveaxis(d_in.reshape(peers, packs, share, chans), 1, 0).reshape(packs, peers * share, chans)

    early = owned_parts(jnp.concatenate([d_out, by_pack(d_in_gate)], axis=1), "ctx")

    d_proj = sum_over_peers(d_part)
    early, d_proj = lax.optimization_barrier((early, d_proj))
    early = tree_sum(early).astype(bf16)
    d_out = jnp.moveaxis(early[: out_share * sides].reshape(sides, out_share, chans), 0, 1).reshape(out_share, width)
    counts = (low_cols, rank, states, taps)
    small_rows = -(-(sum(counts) + 3) // (16 * packs)) * 16 * packs
    d_normed_part, d_in_x, small, d_gain = run_exit(
        starts, d_proj, value_part, pre, x_in, values, conv_w, x_w, d_gate, my_cols, hidden_all, scale_all,
        norm_gain[None, :], d_dt_weight, d_a_log_t, d_dt_bias, d_skip, low_cols, small_rows, span,
    )
    d_normed = lax.psum_scatter(d_normed_part, "ch", scatter_dimension=0, tiled=True)

    gain_rows = d_gain.astype(bf16).reshape(sides, chans)
    gain_rows = jnp.pad(gain_rows, ((0, -sides % 16), (0, 0)))
    late = [by_pack(d_in_x), small.reshape(packs, small_rows // packs, chans)]
    late.append(jnp.broadcast_to(gain_rows, (packs,) + gain_rows.shape))
    late = tree_sum(owned_parts(jnp.concatenate(late, axis=1), "ctx")).astype(bf16)
    own_rows = peers * share
    gain_rows = late[own_rows + small_rows // packs :][:sides].reshape(peers, in_rows)
    pad_rows = -(-in_rows // chans)
    gain_rows = jnp.pad(gain_rows, ((0, 0), (0, pad_rows * chans - in_rows))).reshape(peers, pad_rows, chans)
    gain_rows = jnp.pad(gain_rows, ((0, 0), (0, -pad_rows % 16), (0, 0)))
    cross = [late[:own_rows].reshape(peers, share, chans), early[out_share * sides :].reshape(peers, share, chans)]
    cross, d_out = lax.optimization_barrier((jnp.concatenate([*cross, gain_rows], axis=1), d_out))
    cross = to_peers(cross)
    outs = [d_out] + [swap(d_out, "ctx", d) for d in range(1, packs)]
    outs, cross = lax.optimization_barrier((outs, cross))
    own = [cross[:, : 2 * share].reshape(2 * own_rows, chans), late[own_rows : own_rows + small_rows // packs]]
    own = jnp.concatenate(own, axis=0)
    late = [own] + [swap(own, "ctx", d) for d in range(1, packs)]
    finish = run_finish if share % 16 == 0 and chans % 128 == 0 else finish_plain
    (
        output, d_hidden, gain_sum, in_sum, conv_w_sum, conv_b_sum, x_w_sum, dt_w_sum, dt_b_sum, a_log_sum, skip_sum,
        out_sum,
    ) = finish(
        late, outs, cross, branch, d_normed, hidden_in, out_grad, norm_gain[None, :], (*counts, small_rows),
        lax.axis_index("ctx"),
    )
    return (
        output, d_hidden, gain_sum[0], in_sum, conv_w_sum.T, conv_b_sum[0], x_w_sum.T, dt_w_sum, dt_b_sum[0],
        a_log_sum.T, skip_sum[0], out_sum,
    )


def solution(mesh):
    return jax.shard_map(
        on_device,
        mesh=mesh,
        in_specs=(
            P(("ctx", "ch"), None), P(), P("ch", None), P(), P(), P(), P(None, "ch"), P("ch"), P("ch", None),
            P("ch"), P("ch", None), P("ctx", None), P("ctx"), P(("ctx", "ch"), None),
        ),
        out_specs=(
            P(("ctx", "ch"), None), P(("ctx", "ch"), None), P("ch"), P("ch", None), P("ch", None), P("ch"),
            P("ch", None), P(None, "ch"), P("ch"), P("ch", None), P("ch"), P("ch", None),
        ),
        check_vma=False,
    )
```

```python
import functools
import math

import jax
import jax.numpy as jnp
from jax import lax
from jax.experimental import pallas as pl
from jax.experimental.pallas import tpu as pltpu
from jax.sharding import PartitionSpec as P

f32 = jnp.float32
bf16 = jnp.bfloat16
eps = 1e-05
LOG2E = 1.4426950408889634
CUT = 1e30
SEGS = 8
BATCH = 4
TOGETHER = 4
MIB = 1 << 20
ROOM = 56 * MIB


def silu(v):
    return v * jax.nn.sigmoid(v)


def silu_slope(v):
    sig = jax.nn.sigmoid(v)
    return sig * (1.0 + v * (1.0 - sig))


def context_place(offsets, places):
    begins = jnp.max(jnp.where(offsets[:, None] <= places[None, :], offsets[:, None], 0), axis=0)
    return places - begins


def dot(a, b, dims, precision=None):
    return lax.dot_general(a, b, ((dims[:1], dims[1:]), ((), ())), precision=precision, preferred_element_type=f32)


def lane_groups(chans):
    width = 128 if chans % 128 == 0 else chans
    return chans // width, width


def softplus(v):
    small = jnp.exp(-jnp.abs(v))
    series = small * (1.0 - small * (0.5 - small * (1.0 / 3.0)))
    return jnp.maximum(v, 0.0) + jnp.where(small < 0.01, series, jnp.log(1.0 + small))


def mixing(span, back):
    size = span * SEGS
    row = lax.broadcasted_iota(jnp.int32, (size, size), 0)
    column = lax.broadcasted_iota(jnp.int32, (size, size), 1)
    if back:
        hit = (row % span) * SEGS + row // span == column
    else:
        hit = (row % SEGS) * span + row // SEGS == column
    return hit.astype(f32).astype(bf16)


def context_positions(starts_ref, first_row, rows, steps, lanes):
    row = lax.broadcasted_iota(jnp.int32, (rows, lanes), 0) + first_row
    token = jnp.bitwise_and(row, SEGS - 1) * steps + jnp.right_shift(row, SEGS.bit_length() - 1)
    begin = jnp.zeros((rows, lanes), jnp.int32)
    for c in range(starts_ref.shape[1]):
        begin = jnp.where(starts_ref[0, c] <= token, starts_ref[0, c], begin)
    return token - begin


def split_dot(wide, narrow, dims, swapped=False):
    high = wide.astype(bf16)
    low = (wide - high.astype(f32)).astype(bf16)
    if swapped:
        return dot(narrow, high, dims) + dot(narrow, low, dims)
    return dot(high, narrow, dims) + dot(low, narrow, dims)


def put(ref, rows, value, groups, width):
    for g in range(groups):
        ref[g, rows, :] = value[:, g * width : (g + 1) * width]


def take(ref, rows, groups):
    return jnp.concatenate([ref[g, rows, :] for g in range(groups)], axis=1) if groups > 1 else ref[0, rows, :]


def piece_rows(me_ref, core, apart, chips, rows):
    place = jnp.bitwise_xor(me_ref[0], core) * chips + jnp.bitwise_xor(me_ref[1], apart)
    return pl.ds(pl.multiple_of(place * rows, rows), rows)


def put_pieces(me_ref, refs, source_ref):
    for core, ref in enumerate(refs):
        for apart in range(ref.shape[0]):
            ref[apart] = source_ref[piece_rows(me_ref, core, apart, ref.shape[0], ref.shape[1]), :]


def take_pieces(me_ref, refs, target_ref):
    for core, ref in enumerate(refs):
        for apart in range(ref.shape[0]):
            target_ref[piece_rows(me_ref, core, apart, ref.shape[0], ref.shape[1]), :] = ref[apart]


def block_rows(t, size):
    return pl.ds(pl.multiple_of(t * size, size), size)


def entry_kernel(
    span, taps, me_ref, starts_ref, hid_ref, w_ref, gain_ref, cw_ref, cb_ref, xw_ref,
    normed_ref, scale_ref, x_ref, gate_ref, val_ref, pre_ref, mine_ref, other_ref, s_x, s_mixing, s_proj,
):
    turn = pl.program_id(0)
    turns = pl.num_programs(0) - 1
    chans = x_ref.shape[1]
    size = span * SEGS
    steps = span * turns
    halo = (taps - 1) * SEGS
    groups, width = lane_groups(chans)

    @pl.when(turn == 0)
    def _():
        s_mixing[...] = mixing(span, False)

    @pl.when(turn < turns)
    def _():
        wide = hid_ref[...].astype(f32).reshape(size, hid_ref.shape[2])
        scale = lax.rsqrt(jnp.mean(wide * wide, axis=1, keepdims=True) + eps)
        normed = (wide * scale * gain_ref[...]).astype(bf16)
        normed_ref[...] = normed.reshape(normed_ref.shape)
        scale_ref[...] = jnp.broadcast_to(scale, (size, 128)).reshape(scale_ref.shape)
        mixed = dot(normed, w_ref[...], (1, 0)).astype(bf16)
        mixed = dot(s_mixing[...], mixed, (1, 0))
        x_ref[...] = mixed[:, :chans].astype(bf16)
        gate_ref[...] = mixed[:, chans:].astype(bf16)
        s_x[pl.ds(pl.multiple_of(turn * size + halo, SEGS), size), :] = mixed[:, :chans]

    @pl.when(turn == turns)
    def _():
        first = lax.broadcasted_iota(jnp.int32, (SEGS, chans), 0) == 0
        for j in range(taps - 1):
            last = s_x[pl.ds(pl.multiple_of(steps * SEGS + j * SEGS, SEGS), SEGS), :]
            s_x[j * SEGS : (j + 1) * SEGS, :] = jnp.where(first, 0.0, pltpu.roll(last, 1, 0))

    @pl.when(turn > 0)
    def _():
        t = jnp.where(turn == turns, 0, turn)
        place = jnp.concatenate([context_positions(starts_ref, t * size, size, steps, width)] * groups, axis=1)
        pre = cb_ref[...] + jnp.zeros((size, chans), f32)
        for k in range(taps):
            lag = taps - 1 - k
            at = pl.ds(pl.multiple_of(t * size + halo - lag * SEGS, SEGS), size)
            pre = pre + cw_ref[k : k + 1, :] * jnp.where(place >= lag, s_x[at, :], 0.0)
        pre_ref[...] = pre
        values = silu(pre).astype(bf16)
        val_ref[...] = values
        s_proj[block_rows(t, size), :] = dot(values, xw_ref[...], (1, 0)).astype(bf16)

    @pl.when(turn == turns)
    def _():
        put_pieces(me_ref, (mine_ref, other_ref), s_proj)


def gate_kernel(
    span, grad_ref, w_ref, gate_ref, val_ref, y_ref, skip_ref,
    branch_ref, gated_ref, dy_ref, dgate_ref, dskip_ref, s_in, s_out,
):
    turn = pl.program_id(0)
    size = span * SEGS

    @pl.when(turn == 0)
    def _():
        s_in[...] = mixing(span, False)
        s_out[...] = mixing(span, True)
        dskip_ref[...] = jnp.zeros_like(dskip_ref)

    vals = val_ref[...].astype(f32)
    gate = gate_ref[...].astype(f32)
    sig = jax.nn.sigmoid(gate)
    act = gate * sig
    scanned = y_ref[...] + skip_ref[...] * vals
    gated = dot(s_out[...], (scanned * act).astype(bf16), (1, 0)).astype(bf16)
    gated_ref[...] = gated.reshape(gated_ref.shape)
    branch_ref[...] = dot(gated, w_ref[...], (1, 0)).astype(bf16).reshape(branch_ref.shape)
    grad = grad_ref[...].reshape(size, grad_ref.shape[2])
    d_gated = dot(s_in[...], dot(grad, w_ref[...], (1, 1)).astype(bf16), (1, 0))
    dy = d_gated * act
    dy_ref[...] = dy
    d_gate = (d_gated * scanned * (sig * (1.0 + gate * (1.0 - sig)))).astype(bf16)
    d_gate = dot(s_out[...], d_gate, (1, 0)).astype(bf16)
    dgate_ref[...] = d_gate.reshape(dgate_ref.shape)
    dskip_ref[...] += jnp.sum(dy * vals, axis=0, keepdims=True)


def exit_kernel(
    span, taps, low_cols, packs, peers, me_ref, starts_ref, mine_ref, other_ref, part_ref, pre_ref, x_ref, val_ref, cw_ref, xw_ref, dgate_ref, w_ref,
    hid_ref, scale_ref, gain_ref, ddtw_ref, dalog_ref, ddtb_ref, dskip_ref,
    dn_ref, *refs,
):
    *out_refs, s_pre, s_dx, s_din, s_place, s_small, dgain_ref, dproj_ref = refs
    total, chans = x_ref.shape
    size = span * SEGS
    steps = total // SEGS
    turns = steps // span
    halo = (taps - 1) * SEGS
    groups, width = lane_groups(chans)
    turn = pl.program_id(0)

    @pl.when(turn == 0)
    def _():
        take_pieces(me_ref, (mine_ref, other_ref), dproj_ref)

        def first(t, carry):
            rows = block_rows(t, size)
            d_proj = dproj_ref[rows, :]
            d_values = part_ref[rows, :] + dot(d_proj, xw_ref[...], (1, 1))
            d_pre = d_values * silu_slope(pre_ref[rows, :])
            s_pre[rows, :] = d_pre
            s_place[rows, :] = context_positions(starts_ref, t * size, size, steps, width)
            d_bias, d_xw = carry
            return d_bias + jnp.sum(d_pre, axis=0, keepdims=True), d_xw + dot(d_proj, val_ref[rows, :], (0, 0))

        begin = (jnp.zeros((1, chans), f32), jnp.zeros((dproj_ref.shape[1], chans), f32))
        d_bias, d_xw = lax.fori_loop(0, turns, first, begin)
        s_place[total : total + halo, :] = context_positions(starts_ref, total, halo, steps, width)
        last = lax.broadcasted_iota(jnp.int32, (SEGS, chans), 0) == SEGS - 1
        for j in range(taps - 1):
            head = s_pre[j * SEGS : (j + 1) * SEGS, :]
            s_pre[total + j * SEGS : total + (j + 1) * SEGS, :] = jnp.where(last, 0.0, pltpu.roll(head, SEGS - 1, 0))
        back = mixing(span, True)

        def second(t, sums):
            rows = block_rows(t, size)
            x = x_ref[rows, :].astype(f32)
            d_x = jnp.zeros((size, chans), f32)
            out = []
            for k in range(taps):
                lag = taps - 1 - k
                at = pl.ds(pl.multiple_of(t * size + lag * SEGS, SEGS), size)
                valid = jnp.concatenate([s_place[at, :]] * groups, axis=1) >= lag
                later = jnp.where(valid, s_pre[at, :], 0.0)
                d_x = d_x + cw_ref[k : k + 1, :] * later
                out.append(sums[k] + jnp.sum(later * x, axis=0, keepdims=True))
            natural = dot(back, d_x.astype(bf16), (1, 0)).astype(bf16).reshape(SEGS, span, chans)
            s_dx[:, block_rows(t, span), :] = natural
            return tuple(out)

        sums = lax.fori_loop(0, turns, second, (jnp.zeros((1, chans), f32),) * taps)
        s_din[...] = jnp.zeros_like(s_din)
        dgain_ref[...] = jnp.zeros_like(dgain_ref)
        rest = [*sums, d_bias, ddtb_ref[...], dskip_ref[...]]
        small = [d_xw[:low_cols], ddtw_ref[...], dalog_ref[...], *rest]
        pad = s_small.shape[0] - sum(a.shape[0] for a in small)
        s_small[...] = jnp.concatenate([*small, jnp.zeros((pad, chans), f32)], axis=0)

    @pl.when(turn > 0)
    def _():
        rows = hid_ref.shape[0]
        per_segment = steps // rows if rows <= steps else 1
        if rows <= steps:
            here = pl.ds(pl.multiple_of((turn - 1) % per_segment * rows, rows), rows)
            d_x = s_dx[(turn - 1) // per_segment, here, :]
        else:
            d_x = s_dx[pl.ds((turn - 1) * (rows // steps), rows // steps)].reshape(rows, chans)
        both = jnp.concatenate([d_x, dgate_ref[...]], axis=1)
        d_normed = dot(both, w_ref[...], (1, 1)).astype(bf16)
        dn_ref[...] = d_normed
        unit = hid_ref[...].astype(f32) * jnp.concatenate([scale_ref[...]] * (hid_ref.shape[1] // 128), axis=1)
        dgain_ref[...] += jnp.sum(d_normed.astype(f32) * unit, axis=0, keepdims=True)
        s_din[...] += dot(d_x, (unit * gain_ref[...]).astype(bf16), (0, 0))

    @pl.when(turn == pl.num_programs(0) - 1)
    def _():
        d_in = s_din[...].T
        if len(out_refs) < packs:
            out_refs[0][...] = d_in.astype(bf16)
            out_refs[1][...] = s_small[...].astype(bf16)
            out_refs[2][...] = dgain_ref[...]
            return
        each = s_small.shape[0] // packs
        share = d_in.shape[0] // (peers * packs)
        sides = d_in.shape[0] // chans
        gain = [dgain_ref[:, i * chans : (i + 1) * chans] for i in range(sides)]
        gain = jnp.concatenate([*gain, jnp.zeros((16 - sides, chans), f32)], axis=0).astype(bf16)
        for d, ref in enumerate(out_refs):
            who = jnp.bitwise_xor(me_ref[2], d)
            ref[peers * share : peers * share + each, :] = s_small[block_rows(who, each), :].astype(bf16)
            ref[peers * share + each :, :] = gain
            for p in range(packs):

                @pl.when(who == p)
                def _():
                    for q in range(peers):
                        at = (q * packs + p) * share
                        ref[q * share : (q + 1) * share, :] = d_in[at : at + share].astype(bf16)


def prepare_spread(hot_ref, rank, states):
    hot_ref[...] = jnp.zeros_like(hot_ref)
    row = lax.broadcasted_iota(jnp.int32, (16, 128), 0)
    for n in range(2 * states):
        first = (rank + n) // 16 * 16
        hot_ref[first : first + 16, n * 128 : (n + 1) * 128] = (row + first == rank + n).astype(f32).astype(bf16)


def spread_pair(out_ref, slot, hot_ref, proj_ref, rows, first, pair):
    at = first * 128 + pair * 256
    both = dot(proj_ref[rows, :], hot_ref[:, pl.ds(at if isinstance(at, int) else pl.multiple_of(at, 256), 256)], (1, 0))
    out_ref[slot, 2 * pair] = both[:, :128]
    out_ref[slot, 2 * pair + 1] = both[:, 128:]


def sum_lanes(mix_ref, hot_ref):
    return dot(hot_ref[...], mix_ref[...], (1, 1)).T


def forward_kernel(
    rank, states, span, proj_ref, val_ref, cut_ref, dtw_ref, dtb_ref, alog_ref,
    y_ref, hist_ref, delta_ref, s_cut, s_dx, s_rate, s_state, s_sum, s_b, s_c, s_hot,
):
    total, chans = val_ref.shape
    steps = total // SEGS
    size = span * SEGS
    groups, width = lane_groups(chans)
    turn = pl.program_id(0)
    turns = steps // span
    slots = s_b.shape[0]
    half = states // 2
    count = span // BATCH

    def rate(n, g):
        return s_rate[n : n + 1, g * width : (g + 1) * width]

    @pl.when(turn == 0)
    def _():
        s_rate[...] = -jnp.exp(alog_ref[...]) * LOG2E
        prepare_spread(s_hot, rank, states)
        s_state[...] = jnp.zeros_like(s_state)
        s_sum[...] = jnp.zeros_like(s_sum)
        def block(t, carry):
            rows = block_rows(t, size)
            slot = t if slots > 1 else 0
            for pair in range(half):
                spread_pair(s_b, slot, s_hot, proj_ref, rows, 0, pair)
                spread_pair(s_c, slot, s_hot, proj_ref, rows, states, pair)
            delta = softplus(dot(proj_ref[rows, :rank], dtw_ref[...], (1, 0)) + dtb_ref[...])
            put(delta_ref, rows, delta, groups, width)
            cut = cut_ref[rows, :].astype(f32) * CUT
            put(s_cut, rows, delta + jnp.concatenate([cut] * groups, axis=1), groups, width)
            put(s_dx, rows, delta * val_ref[rows, :].astype(f32), groups, width)

            def sweep(q, carry):
                at = [block_rows(t * span + q * BATCH + j, SEGS) for j in range(BATCH)]
                here = [block_rows(q * BATCH + j, SEGS) for j in range(BATCH)]
                for g in range(groups):
                    cuts = [s_cut[g, at[j], :] for j in range(BATCH)]
                    dxs = [s_dx[g, at[j], :] for j in range(BATCH)]
                    s_sum[g] = s_sum[g] + sum(cuts)
                    for n in range(states):
                        held = s_state[n * groups + g]
                        for j in range(BATCH):
                            push = dxs[j] * s_b[slot, n, here[j], :width]
                            held = jnp.exp2(cuts[j] * rate(n, g)) * held + push
                        s_state[n * groups + g] = held
                return carry

            return lax.fori_loop(0, count, sweep, carry)

        lax.fori_loop(0, turns, block, 0)
        first = lax.broadcasted_iota(jnp.int32, (SEGS, width), 0) == 0
        for n in range(states):
            for g in range(groups):
                gain = jnp.exp2(s_sum[g] * rate(n, g))
                end = s_state[n * groups + g]
                start = jnp.zeros((SEGS, width), f32)
                for _ in range(SEGS - 1):
                    start = jnp.where(first, 0.0, pltpu.roll(gain * start + end, 1, 0))
                s_state[n * groups + g] = start

    slot = turn if slots > 1 else 0
    if slots == 1:
        for pair in range(half):
            spread_pair(s_b, 0, s_hot, proj_ref, block_rows(turn, size), 0, pair)
            spread_pair(s_c, 0, s_hot, proj_ref, block_rows(turn, size), states, pair)

    def sweep(q, carry):
        at = [block_rows(turn * span + q * BATCH + j, SEGS) for j in range(BATCH)]
        here = [block_rows(q * BATCH + j, SEGS) for j in range(BATCH)]
        for g in range(groups):
            cuts = [s_cut[g, at[j], :] for j in range(BATCH)]
            dxs = [s_dx[g, at[j], :] for j in range(BATCH)]
            ys = [None] * BATCH
            for n in range(states):
                i = n * groups + g
                held = s_state[i]
                for j in range(BATCH):
                    hist_ref[0, q * BATCH + j, i] = held
                    push = dxs[j] * s_b[slot, n, here[j], :width]
                    held = jnp.exp2(cuts[j] * rate(n, g)) * held + push
                    term = held * s_c[slot, n, here[j], :width]
                    ys[j] = term if n == 0 else ys[j] + term
                s_state[i] = held
            for j in range(BATCH):
                y_ref[at[j], g * width : (g + 1) * width] = ys[j]
        return carry

    lax.fori_loop(0, count, sweep, 0)
    hist_ref[0, span] = s_state[...]


def backward_kernel(
    rank, states, span, proj_ref, val_ref, cut_ref, dy_ref, delta_ref, dtw_ref, dtwt_ref, dtb_ref, alog_ref, skip_ref,
    hist_ref, part_ref, dval_ref, ddtw_ref, ddtb_ref, dalog_ref,
    s_cut, s_val, s_dd, s_rate, s_state, s_sum, s_drate, s_b, s_c, s_mix, s_hot, s_bc,
):
    total, chans = val_ref.shape
    steps = total // SEGS
    size = span * SEGS
    groups, width = lane_groups(chans)
    turns = steps // span
    turn = pl.program_id(0)
    place = turns - 1 - turn
    slots = s_b.shape[0]
    half = states // 2
    count = span // BATCH
    lane = [slice(g * width, (g + 1) * width) for g in range(groups)]

    def rate(n, g):
        return s_rate[n : n + 1, lane[g]]

    @pl.when(turn == 0)
    def _():
        s_rate[...] = -jnp.exp(alog_ref[...]) * LOG2E
        s_drate[...] = jnp.zeros_like(s_drate)
        s_state[...] = jnp.zeros_like(s_state)
        s_sum[...] = jnp.zeros_like(s_sum)
        if width < 128:
            s_mix[...] = jnp.zeros_like(s_mix)
        prepare_spread(s_hot, rank, states)
        def block(turned, carry):
            t = turns - 1 - turned
            rows = block_rows(t, size)
            slot = t if slots > 1 else 0
            for pair in range(half):
                spread_pair(s_b, slot, s_hot, proj_ref, rows, 0, pair)
                spread_pair(s_c, slot, s_hot, proj_ref, rows, states, pair)
            cut = cut_ref[rows, :].astype(f32) * CUT
            delta = take(delta_ref, rows, groups)
            put(s_cut, rows, delta + jnp.concatenate([cut] * groups, axis=1), groups, width)
            put(s_val, rows, val_ref[rows, :].astype(f32), groups, width)

            def sweep(q, carry):
                k = span - BATCH - q * BATCH
                at = [block_rows(t * span + k + j, SEGS) for j in range(BATCH)]
                here = [block_rows(k + j, SEGS) for j in range(BATCH)]
                for g in range(groups):
                    cuts = [s_cut[g, at[j], :] for j in range(BATCH)]
                    dys = [dy_ref[at[j], lane[g]] for j in range(BATCH)]
                    s_sum[g] = s_sum[g] + sum(cuts)
                    for n in range(states):
                        held = s_state[n * groups + g]
                        for j in reversed(range(BATCH)):
                            held = dys[j] * s_c[slot, n, here[j], :width] + held
                            held = jnp.exp2(cuts[j] * rate(n, g)) * held
                        s_state[n * groups + g] = held
                return carry

            return lax.fori_loop(0, count, sweep, carry)

        lax.fori_loop(0, turns, block, 0)
        last = lax.broadcasted_iota(jnp.int32, (SEGS, width), 0) == SEGS - 1
        for n in range(states):
            for g in range(groups):
                gain = jnp.exp2(s_sum[g] * rate(n, g))
                end = s_state[n * groups + g]
                start = jnp.zeros((SEGS, width), f32)
                for _ in range(SEGS - 1):
                    start = jnp.where(last, 0.0, pltpu.roll(gain * start + end, SEGS - 1, 0))
                s_state[n * groups + g] = start

    slot = place if slots > 1 else 0
    if slots == 1:
        for pair in range(half):
            spread_pair(s_b, 0, s_hot, proj_ref, block_rows(place, size), 0, pair)
            spread_pair(s_c, 0, s_hot, proj_ref, block_rows(place, size), states, pair)

    def sweep(q, carry):
        k = span - BATCH - q * BATCH
        at = [block_rows(place * span + k + j, SEGS) for j in range(BATCH)]
        here = [block_rows(k + j, SEGS) for j in range(BATCH)]
        each = [(j, g) for j in range(BATCH) for g in range(groups)]
        cuts = {(j, g): s_cut[g, at[j], :] for j, g in each}
        deltas = {(j, g): delta_ref[g, at[j], :] for j, g in each}
        vals = {(j, g): s_val[g, at[j], :] for j, g in each}
        dys = {(j, g): dy_ref[at[j], lane[g]] for j, g in each}
        dxs = {e: deltas[e] * vals[e] for e in each}
        by_rate, by_b = {}, {}
        for first in range(0, states, TOGETHER):
            some = [(n, g) for n in range(first, first + TOGETHER) for g in range(groups)]
            held = {(n, g): s_state[n * groups + g] for n, g in some}
            d_rate = {(n, g): s_drate[n * groups + g] for n, g in some}
            after = {(n, g): hist_ref[0, k + BATCH, n * groups + g] for n, g in some}
            mix = {}
            for j in reversed(range(BATCH)):
                for n, g in some:
                    e, i = (j, g), (n, g)
                    b_n = s_b[slot, n, here[j], :width]
                    c_n = s_c[slot, n, here[j], :width]
                    before = hist_ref[0, k + j, n * groups + g]
                    lam = dys[e] * c_n + held[i]
                    held[i] = jnp.exp2(cuts[e] * rate(n, g)) * lam
                    through = held[i] * before
                    d_rate[i] = d_rate[i] + through * deltas[e]
                    terms = (through * rate(n, g), lam * b_n, lam * dxs[e], dys[e] * after[i])
                    by_rate[e] = by_rate[e] + terms[0] if e in by_rate else terms[0]
                    by_b[e] = by_b[e] + terms[1] if e in by_b else terms[1]
                    for m, term in ((n, terms[2]), (states + n, terms[3])):
                        mix[j, m] = mix[j, m] + term if (j, m) in mix else term
                    after[i] = before
                if j % 2 == 0:
                    two = pl.ds(pl.multiple_of((k + j) * SEGS, 2 * SEGS), 2 * SEGS)
                    for n in range(first, first + TOGETHER):
                        for m in (n, states + n):
                            value = jnp.concatenate([mix[j, m], mix[j + 1, m]], axis=0).astype(bf16)
                            s_mix[two, m * 128 : m * 128 + width] = value
            for n, g in some:
                s_state[n * groups + g] = held[n, g]
                s_drate[n * groups + g] = d_rate[n, g]
        for j, g in each:
            e = (j, g)
            s_dd[g, at[j], :] = by_rate[e] * (1.0 / LOG2E) + by_b[e] * vals[e]
            dval_ref[at[j], lane[g]] = by_b[e] * deltas[e] + dys[e] * skip_ref[:, lane[g]]
        return carry

    lax.fori_loop(0, count, sweep, 0)
    rows = block_rows(place, size)
    s_bc[...] = sum_lanes(s_mix, s_hot)
    pre = dot(proj_ref[rows, :rank], dtw_ref[...], (1, 0)) + dtb_ref[...]
    d_pre = take(s_dd, rows, groups) * jax.nn.sigmoid(pre)
    d_bias = jnp.sum(d_pre, axis=0, keepdims=True)
    d_dtw = split_dot(d_pre, proj_ref[rows, :rank], (0, 0), swapped=True)
    part = split_dot(d_pre, dtwt_ref[...], (1, 0))
    part_ref[rows, :] = (part + s_bc[...]).astype(bf16)

    @pl.when(turn == 0)
    def _():
        ddtb_ref[...] = d_bias
        ddtw_ref[...] = d_dtw

    @pl.when(turn > 0)
    def _():
        ddtb_ref[...] += d_bias
        ddtw_ref[...] += d_dtw

    @pl.when(turn == turns - 1)
    def _():
        sums = [jnp.sum(s_drate[i], axis=0, keepdims=True) for i in range(states * groups)]
        rows = [jnp.concatenate(sums[n * groups : (n + 1) * groups], axis=1) for n in range(states)]
        dalog_ref[...] = jnp.concatenate(rows, axis=0) * s_rate[...] * (1.0 / LOG2E)


def scan_kernel(
    rank, states, span, me_ref, mine_ref, other_ref, val_ref, gate_ref, cut_ref, grad_ref, w_ref, dtw_ref, dtwt_ref, dtb_ref, alog_ref,
    skip_ref, branch_ref, gated_ref, dgate_ref, pmine_ref, pother_ref, dval_ref, ddtw_ref, ddtb_ref, dalog_ref, dskip_ref,
    s_cut, s_delta, s_val, s_dy, s_hist, s_b, s_c, s_y, s_rate, s_state, s_drate, s_mix, s_hot, s_in, s_out, s_even, proj_ref, part_ref,
):
    total, chans = val_ref.shape
    steps = total // SEGS
    size = span * SEGS
    groups, width = lane_groups(chans)
    pairs = [(n, g) for n in range(states) for g in range(groups)]
    every = range(groups)
    lane = [slice(g * width, (g + 1) * width) for g in every]
    turns = steps // span
    turn = pl.program_id(0)
    zero = jnp.zeros((SEGS, width), f32)
    sublane = lax.broadcasted_iota(jnp.int32, (SEGS, width), 0)

    def decay(cut, n, g):
        return jnp.exp2(cut * s_rate[n : n + 1, lane[g]])

    def chained(ends, sums, edge, shift):
        for n, g in pairs:
            gain = decay(sums[g], n, g)
            end = ends[n * groups + g]
            start = zero
            for _ in range(SEGS - 1):
                start = jnp.where(sublane == edge, 0.0, pltpu.roll(gain * start + end, shift, 0))
            s_state[n * groups + g] = start

    @pl.when(turn == 0)
    def _():
        s_rate[...] = -jnp.exp(alog_ref[...]) * LOG2E
        s_drate[...] = jnp.zeros_like(s_drate)
        dskip_ref[...] = jnp.zeros_like(dskip_ref)
        s_in[...] = mixing(span, False)
        s_out[...] = mixing(span, True)
        prepare_spread(s_hot, rank, states)
        take_pieces(me_ref, (mine_ref, other_ref), proj_ref)
        s_even[...] = jnp.concatenate([s_hot[:, n * 128 : (n + 1) * 128] for n in range(0, 2 * states, 2)], axis=1)

        def fill(t, carry):
            rows = block_rows(t, size)
            for n in range(0, states, 2):
                for ref, first in ((s_b, n), (s_c, states + n)):
                    both = dot(proj_ref[rows, :], s_hot[:, first * 128 : (first + 2) * 128], (1, 0))
                    ref[n, rows, :] = both[:, :128]
                    ref[n + 1, rows, :] = both[:, 128:]
            delta = softplus(dot(proj_ref[rows, :rank], dtw_ref[...], (1, 0)) + dtb_ref[...])
            cut = cut_ref[rows, :].astype(f32) * CUT
            put(s_delta, rows, delta, groups, width)
            put(s_cut, rows, delta + jnp.concatenate([cut] * groups, axis=1), groups, width)
            put(s_val, rows, val_ref[rows, :].astype(f32), groups, width)
            return carry

        lax.fori_loop(0, turns, fill, 0)

        def sweep(i, carry):
            held, sums = carry
            at = block_rows(i, SEGS)
            cuts = [s_cut[g, at, :] for g in every]
            dxs = [s_delta[g, at, :] * s_val[g, at, :] for g in every]
            out = [decay(cuts[g], n, g) * held[n * groups + g] + dxs[g] * s_b[n, at, :width] for n, g in pairs]
            return tuple(out), tuple(sums[g] + cuts[g] for g in every)

        begin = ((zero,) * len(pairs), (zero,) * groups)
        chained(*lax.fori_loop(0, steps, sweep, begin, unroll=16), 0, 1)

    @pl.when(turn < turns)
    def _():

        def sweep(k, held):
            i = turn * span + k
            at = block_rows(i, SEGS)
            cuts = [s_cut[g, at, :] for g in every]
            dxs = [s_delta[g, at, :] * s_val[g, at, :] for g in every]
            ys = [zero] * groups
            out = []
            for n in range(states):
                b_n = s_b[n, at, :width]
                c_n = s_c[n, at, :width]
                for g in every:
                    old = held[n * groups + g]
                    s_hist[i, n * groups + g] = old
                    new = decay(cuts[g], n, g) * old + dxs[g] * b_n
                    out.append(new)
                    ys[g] = ys[g] + new * c_n
            for g in every:
                s_y[block_rows(k, SEGS), lane[g]] = ys[g]
            return tuple(out)

        held = lax.fori_loop(0, span, sweep, tuple(s_state[j] for j in range(len(pairs))), unroll=16)
        for j in range(len(pairs)):
            s_state[j] = held[j]

        @pl.when(turn == turns - 1)
        def _():
            s_hist[steps] = s_state[...]

        rows = block_rows(turn, size)
        vals = val_ref[rows, :].astype(f32)
        gate = gate_ref[...].astype(f32)
        sig = jax.nn.sigmoid(gate)
        act = gate * sig
        scanned = s_y[...] + skip_ref[...] * vals
        grad = grad_ref[...].reshape(size, grad_ref.shape[2])
        d_gated = dot(s_in[...], dot(grad, w_ref[...], (1, 1)).astype(bf16), (1, 0))
        dy = d_gated * act
        put(s_dy, rows, dy, groups, width)
        d_gate = d_gated * scanned * (sig * (1.0 + gate * (1.0 - sig)))
        both = jnp.concatenate([(scanned * act).astype(bf16), d_gate.astype(bf16)], axis=1)
        both = dot(s_out[...], both, (1, 0)).astype(bf16)
        gated_ref[...] = both[:, :chans].reshape(gated_ref.shape)
        dgate_ref[...] = both[:, chans:].reshape(dgate_ref.shape)
        branch_ref[...] = dot(both[:, :chans], w_ref[...], (1, 0)).astype(bf16).reshape(branch_ref.shape)
        dskip_ref[...] += jnp.sum(dy * vals, axis=0, keepdims=True)

    @pl.when(turn == turns)
    def _():
        ddtb_ref[...] = jnp.zeros_like(ddtb_ref)
        ddtw_ref[...] = jnp.zeros_like(ddtw_ref)

        def sweep(back, carry):
            held, sums = carry
            at = block_rows(steps - 1 - back, SEGS)
            cuts = [s_cut[g, at, :] for g in every]
            dys = [s_dy[g, at, :] for g in every]
            out = []
            for n, g in pairs:
                lam = dys[g] * s_c[n, at, :width] + held[n * groups + g]
                out.append(decay(cuts[g], n, g) * lam)
            return tuple(out), tuple(sums[g] + cuts[g] for g in every)

        begin = ((zero,) * len(pairs), (zero,) * groups)
        chained(*lax.fori_loop(0, steps, sweep, begin, unroll=16), SEGS - 1, SEGS - 1)

    @pl.when(turn >= turns)
    def _():
        place = 2 * turns - 1 - turn

        def sweep(back, held):
            k = span - 1 - back
            i = place * span + k
            at = block_rows(i, SEGS)
            cuts = [s_cut[g, at, :] for g in every]
            deltas = [s_delta[g, at, :] for g in every]
            vals = [s_val[g, at, :] for g in every]
            dys = [s_dy[g, at, :] for g in every]
            dxs = [deltas[g] * vals[g] for g in every]
            by_rate = [zero] * groups
            by_b = [zero] * groups
            out = []
            mixes = {}
            for n in range(states):
                b_n = s_b[n, at, :width]
                c_n = s_c[n, at, :width]
                mix = mix_c = None
                for g in every:
                    j = n * groups + g
                    lam = dys[g] * c_n + held[j]
                    onward = decay(cuts[g], n, g) * lam
                    out.append(onward)
                    through = onward * s_hist[i, j]
                    by_rate[g] = by_rate[g] + through * s_rate[n : n + 1, lane[g]]
                    by_b[g] = by_b[g] + lam * b_n
                    s_drate[j] = s_drate[j] + through * deltas[g]
                    term, term_c = lam * dxs[g], dys[g] * s_hist[i + 1, j]
                    mix = term if mix is None else mix + term
                    mix_c = term_c if mix_c is None else mix_c + term_c
                mixes[n], mixes[states + n] = mix, mix_c
                if n % 2:
                    for first in (n - 1, states + n - 1):
                        two = jnp.concatenate([mixes[first], mixes[first + 1]], axis=0).astype(bf16)
                        s_mix[block_rows(k, 2 * SEGS), first * 64 : first * 64 + width] = two
            for g in every:
                s_cut[g, at, :] = by_rate[g] * (1.0 / LOG2E) + by_b[g] * vals[g]
                dval_ref[block_rows(k, SEGS), lane[g]] = by_b[g] * deltas[g] + dys[g] * skip_ref[:, lane[g]]
            return tuple(out)

        held = lax.fori_loop(0, span, sweep, tuple(s_state[j] for j in range(len(pairs))), unroll=16)
        for j in range(len(pairs)):
            s_state[j] = held[j]
        rows = block_rows(place, size)
        pre = dot(proj_ref[rows, :rank], dtw_ref[...], (1, 0)) + dtb_ref[...]
        d_pre = take(s_cut, rows, groups) * jax.nn.sigmoid(pre)
        ddtb_ref[...] += jnp.sum(d_pre, axis=0, keepdims=True)
        ddtw_ref[...] += split_dot(d_pre, proj_ref[rows, :rank], (0, 0), swapped=True)
        part = split_dot(d_pre, dtwt_ref[...], (1, 0))
        found = dot(s_mix[...], s_even[...], (1, 1)).reshape(span, 2, SEGS, part_ref.shape[1])
        odd = pltpu.roll(found[:, 1].reshape(size, part_ref.shape[1]), 1, 1)
        part_ref[rows, :] = (part + found[:, 0].reshape(size, part_ref.shape[1]) + odd).astype(bf16)

    @pl.when(turn == 2 * turns - 1)
    def _():
        put_pieces(me_ref, (pmine_ref, pother_ref), part_ref)
        sums = [jnp.sum(s_drate[i], axis=0, keepdims=True) for i in range(states * groups)]
        rows = [jnp.concatenate(sums[n * groups : (n + 1) * groups], axis=1) for n in range(states)]
        dalog_ref[...] = jnp.concatenate(rows, axis=0) * s_rate[...] * (1.0 / LOG2E)


def scan_span(steps):
    return math.gcd(steps, 32)


def wide_slots(steps, span, states):
    turns = steps // span
    return turns if turns * 2 * states * span * SEGS * 128 * 4 <= 16 * MIB else 1


def whole(*shape):
    return pl.BlockSpec(shape, lambda *t: (0,) * len(shape))


def like(*shape, dtype=f32):
    return jax.ShapeDtypeStruct(shape, dtype)


def about(micros):
    return pl.CostEstimate(flops=int(micros * 1.1e9), bytes_accessed=1 << 20, transcendentals=0)


SCALARS = pl.BlockSpec(memory_space=pltpu.SMEM)


def run_entry(me, starts, hidden_all, weight, gain, conv_w, conv_b, x_w, peers, span):
    total, width = hidden_all.shape
    taps, chans = conv_w.shape
    lanes = x_w.shape[1]
    steps = total // SEGS
    turns = steps // span
    size = span * SEGS
    piece = (peers // 2, total // peers, lanes)

    def segments(lanes):
        return pl.BlockSpec((SEGS, span, lanes), lambda t: (0, jnp.minimum(t, turns - 1), 0))

    mixed = pl.BlockSpec((size, chans), lambda t: (jnp.minimum(t, turns - 1), 0))

    def late(lanes):
        return pl.BlockSpec((size, lanes), lambda t: (jnp.where(t == turns, 0, jnp.maximum(t, 1)), 0))

    normed, scale, *rest = pl.pallas_call(
        functools.partial(entry_kernel, span, taps),
        grid=(turns + 1,),
        in_specs=[
            SCALARS, SCALARS, segments(width), whole(width, 2 * chans), whole(1, width), whole(taps, chans), whole(1, chans),
            whole(chans, lanes),
        ],
        out_specs=[segments(width), segments(128), mixed, mixed, late(chans), late(chans)]
        + [whole(*piece)] * 2,
        out_shape=[like(SEGS, steps, width, dtype=bf16), like(SEGS, steps, 128)] + [like(total, chans, dtype=bf16)] * 3
        + [like(total, chans)] + [like(*piece, dtype=bf16)] * 2,
        scratch_shapes=[
            pltpu.VMEM((total + (taps - 1) * SEGS, chans), f32), pltpu.VMEM((size, size), bf16),
            pltpu.VMEM((total, lanes), bf16),
        ],
        compiler_params=pltpu.CompilerParams(vmem_limit_bytes=ROOM),
        cost_estimate=about(6 * total * chans / 262144),
        name="entry",
    )(me, starts, hidden_all.reshape(SEGS, steps, width), weight, gain, conv_w, conv_b, x_w)
    return (normed, scale.reshape(total, 128), *rest)


def run_gate(grad_all, out_w, gate, values, y, skip, span):
    total, width = grad_all.shape
    chans = gate.shape[1]
    steps = total // SEGS
    rows = pl.BlockSpec((span * SEGS, chans), lambda t: (t, 0))
    part = pl.BlockSpec((SEGS, span, chans), lambda t: (0, t, 0))
    full = pl.BlockSpec((SEGS, span, width), lambda t: (0, t, 0))
    natural = like(SEGS, steps, chans, dtype=bf16)
    branch, gated, dy, d_gate, d_skip = pl.pallas_call(
        functools.partial(gate_kernel, span),
        grid=(steps // span,),
        in_specs=[full, whole(chans, width), rows, rows, rows, whole(1, chans)],
        out_specs=[full, part, rows, part, whole(1, chans)],
        out_shape=[like(SEGS, steps, width, dtype=bf16), natural, like(total, chans), natural, like(1, chans)],
        scratch_shapes=[pltpu.VMEM((span * SEGS, span * SEGS), bf16)] * 2,
        compiler_params=pltpu.CompilerParams(vmem_limit_bytes=ROOM),
        cost_estimate=about(6 * total * chans / 262144),
        name="gate",
    )(grad_all.reshape(SEGS, steps, width), out_w, gate, values, y, skip)
    return branch.reshape(total, width), gated.reshape(total, chans), dy, d_gate.reshape(total, chans), d_skip


def run_scan(me, mine, other, values, gate, cut, grad_all, out_w, dt_weight, dt_weight_t, dt_bias, a_log_t, skip, states, span):
    total, chans = values.shape
    width_all = grad_all.shape[1]
    rank = dt_weight.shape[0]
    steps = total // SEGS
    groups, width = lane_groups(chans)
    count = states * groups
    lanes = mine.shape[2]
    turns = steps // span
    size = span * SEGS
    by_group = pltpu.VMEM((groups, total, width), f32)
    spread = pltpu.VMEM((states, total, 128), f32)
    held = pltpu.VMEM((count, SEGS, width), f32)
    order = pltpu.VMEM((size, size), bf16)
    part = pl.BlockSpec((SEGS, span, chans), lambda t: (0, jnp.minimum(t, turns - 1), 0))
    full = pl.BlockSpec((SEGS, span, width_all), lambda t: (0, jnp.minimum(t, turns - 1), 0))
    ahead = pl.BlockSpec((size, chans), lambda t: (jnp.minimum(t, turns - 1), 0))

    def behind(lanes):
        return pl.BlockSpec((size, lanes), lambda t: (jnp.minimum(turns, 2 * turns - t) - 1, 0))

    natural = like(SEGS, steps, chans, dtype=bf16)
    branch, gated, d_gate, *rest = pl.pallas_call(
        functools.partial(scan_kernel, rank, states, span),
        grid=(2 * turns,),
        in_specs=[
            SCALARS, whole(*mine.shape), whole(*mine.shape), whole(total, chans), ahead, whole(total, width), full,
            whole(chans, width_all), whole(rank, chans), whole(chans, lanes), whole(1, chans), whole(states, chans),
            whole(1, chans),
        ],
        out_specs=[
            full, part, part, whole(*mine.shape), whole(*mine.shape), behind(chans), whole(rank, chans), whole(1, chans),
            whole(states, chans), whole(1, chans),
        ],
        out_shape=[
            like(SEGS, steps, width_all, dtype=bf16), natural, natural, like(*mine.shape, dtype=bf16),
            like(*mine.shape, dtype=bf16), like(total, chans), like(rank, chans), like(1, chans), like(states, chans), like(1, chans),
        ],
        scratch_shapes=[
            by_group, by_group, by_group, by_group, pltpu.VMEM((steps + 1, count, SEGS, width), f32), spread, spread,
            pltpu.VMEM((size, chans), f32), pltpu.VMEM((states, chans), f32), held, held,
            pltpu.VMEM((2 * size, states * 128), bf16), pltpu.VMEM((lanes, 2 * states * 128), bf16), order, order,
            pltpu.VMEM((lanes, states * 128), bf16), pltpu.VMEM((total, lanes), bf16), pltpu.VMEM((total, lanes), bf16),
        ],
        compiler_params=pltpu.CompilerParams(vmem_limit_bytes=ROOM),
        cost_estimate=about(38),
        name="scan",
    )(me, mine, other, values, gate, cut, grad_all.reshape(SEGS, steps, width_all), out_w, dt_weight, dt_weight_t, dt_bias, a_log_t, skip)
    return (branch.reshape(total, width_all), gated.reshape(total, chans), d_gate.reshape(total, chans), *rest)


def run_exit(
    me, starts, mine, other, value_part, pre, x_in, values, conv_w, x_w, d_gate, weight, hidden_all, scale, gain,
    d_dtw, d_alog_t, d_dtb, d_skip, low_cols, small_rows, packs, peers,
    span,
):
    total, chans = x_in.shape
    taps = conv_w.shape[0]
    lanes = x_w.shape[1]
    width = hidden_all.shape[1]
    steps = total // SEGS
    size = math.gcd(total, 256)

    def rows(lanes):
        return pl.BlockSpec((size, lanes), lambda t: (jnp.maximum(t - 1, 0), 0))

    sides = width // chans
    packed = width // (peers * packs) % 16 == 0 and sides <= 16
    if packed:
        shapes = [like((width + small_rows) // packs + 16, chans, dtype=bf16)] * packs
    else:
        shapes = [like(width, chans, dtype=bf16), like(small_rows, chans, dtype=bf16), like(1, width)]
    d_normed, *out = pl.pallas_call(
        functools.partial(exit_kernel, span, taps, low_cols, packs, peers),
        grid=(1 + total // size,),
        in_specs=[SCALARS, SCALARS, whole(*mine.shape), whole(*mine.shape)] + [whole(total, chans)] * 4 + [
            whole(taps, chans), whole(chans, lanes), rows(chans), whole(width, 2 * chans), rows(width), rows(128),
            whole(1, width), whole(*d_dtw.shape), whole(*d_alog_t.shape), whole(1, chans), whole(1, chans),
        ],
        out_specs=[rows(width)] + [whole(*a.shape) for a in shapes],
        out_shape=[like(total, width, dtype=bf16), *shapes],
        scratch_shapes=[
            pltpu.VMEM((total + (taps - 1) * SEGS, chans), f32), pltpu.VMEM((SEGS, steps, chans), bf16),
            pltpu.VMEM((chans, width), f32), pltpu.VMEM((total + (taps - 1) * SEGS, lane_groups(chans)[1]), jnp.int32),
            pltpu.VMEM((small_rows, chans), f32), pltpu.VMEM((1, width), f32), pltpu.VMEM((total, lanes), bf16),
        ],
        compiler_params=pltpu.CompilerParams(vmem_limit_bytes=ROOM),
        cost_estimate=about(10 * total * chans / 262144),
        name="exit",
    )(
        me, starts, mine, other, value_part, pre, x_in, values, conv_w, x_w, d_gate, weight, hidden_all, scale, gain,
        d_dtw, d_alog_t, d_dtb, d_skip,
    )
    if packed:
        return d_normed, out
    late = jnp.moveaxis(out[0].reshape(peers, packs, -1, chans), 1, 0).reshape(packs, -1, chans)
    gain = jnp.pad(out[2].astype(bf16).reshape(sides, chans), ((0, -sides % 16), (0, 0)))
    late = [late, out[1].reshape(packs, -1, chans), jnp.broadcast_to(gain, (packs,) + gain.shape)]
    late = jnp.concatenate(late, axis=1)
    return d_normed, [pick(late, jnp.bitwise_xor(me[2], d)) for d in range(packs)]


def run_forward(proj, values, cut, dt_weight, dt_bias, a_log_t, states, span):
    total, chans = values.shape
    rank = dt_weight.shape[0]
    steps = total // SEGS
    groups, width = lane_groups(chans)
    count = states * groups
    lanes = proj.shape[1]
    slots = wide_slots(steps, span, states)
    by_group = pltpu.VMEM((groups, total, width), f32)
    return pl.pallas_call(
        functools.partial(forward_kernel, rank, states, span),
        grid=(steps // span,),
        in_specs=[
            whole(total, lanes), whole(total, chans), whole(total, width), whole(rank, chans), whole(1, chans),
            whole(states, chans),
        ],
        out_specs=[
            whole(total, chans), pl.BlockSpec((1, span + 1, count, SEGS, width), lambda t: (t, 0, 0, 0, 0)),
            whole(groups, total, width),
        ],
        out_shape=[
            like(total, chans), like(steps // span, span + 1, count, SEGS, width), like(groups, total, width),
        ],
        scratch_shapes=[
            by_group, by_group, pltpu.VMEM((states, chans), f32), pltpu.VMEM((count, SEGS, width), f32),
            pltpu.VMEM((groups, SEGS, width), f32),
            pltpu.VMEM((slots, states, span * SEGS, 128), f32),
            pltpu.VMEM((slots, states, span * SEGS, 128), f32), pltpu.VMEM((lanes, 2 * states * 128), bf16),
        ],
        compiler_params=pltpu.CompilerParams(vmem_limit_bytes=ROOM),
        cost_estimate=about(18 * total * chans / 262144),
        name="scan_forward",
    )(proj, values, cut, dt_weight, dt_bias, a_log_t)


def run_backward(proj, values, cut, dy, delta, dt_weight, dt_weight_t, dt_bias, a_log_t, skip, hist, states, span):
    total, chans = values.shape
    rank = dt_weight.shape[0]
    steps = total // SEGS
    groups, width = lane_groups(chans)
    count = states * groups
    lanes = proj.shape[1]
    turns = steps // span
    slots = wide_slots(steps, span, states)
    by_group = pltpu.VMEM((groups, total, width), f32)
    return pl.pallas_call(
        functools.partial(backward_kernel, rank, states, span),
        grid=(turns,),
        in_specs=[
            whole(total, lanes), whole(total, chans), whole(total, width), whole(total, chans), whole(groups, total, width),
            whole(rank, chans), whole(chans, lanes), whole(1, chans), whole(states, chans), whole(1, chans),
            pl.BlockSpec((1, span + 1, count, SEGS, width), lambda t: (turns - 1 - t, 0, 0, 0, 0)),
        ],
        out_specs=[
            whole(total, lanes), whole(total, chans), whole(rank, chans), whole(1, chans), whole(states, chans),
        ],
        out_shape=[
            like(total, lanes, dtype=bf16), like(total, chans), like(rank, chans), like(1, chans), like(states, chans),
        ],
        scratch_shapes=[
            by_group, by_group, by_group, pltpu.VMEM((states, chans), f32),
            pltpu.VMEM((count, SEGS, width), f32), pltpu.VMEM((groups, SEGS, width), f32),
            pltpu.VMEM((count, SEGS, width), f32),
            pltpu.VMEM((slots, states, span * SEGS, 128), f32),
            pltpu.VMEM((slots, states, span * SEGS, 128), f32), pltpu.VMEM((span * SEGS, 2 * states * 128), bf16),
            pltpu.VMEM((lanes, 2 * states * 128), bf16), pltpu.VMEM((span * SEGS, lanes), f32),
        ],
        compiler_params=pltpu.CompilerParams(vmem_limit_bytes=ROOM),
        cost_estimate=about(22 * total * chans / 262144),
        name="scan_backward",
    )(proj, values, cut, dy, delta, dt_weight, dt_weight_t, dt_bias, a_log_t, skip, hist)


def tree_sum(parts):
    parts = [p.astype(f32) for p in parts]
    while len(parts) > 1:
        parts = [parts[i] + parts[i + 1] for i in range(0, len(parts), 2)]
    return parts[0]


def swap(value, axis, mask):
    return lax.ppermute(value, axis, [(i, i ^ mask) for i in range(lax.axis_size(axis))])


def pick(blocks, index, dim=0):
    return lax.dynamic_index_in_dim(blocks, index, dim, keepdims=False)


def collected(pieces, me):
    out = jnp.zeros((len(pieces),) + pieces[0].shape, pieces[0].dtype)
    for d, piece in enumerate(pieces):
        out = lax.dynamic_update_index_in_dim(out, piece, me ^ d, 0)
    return out


def owned_parts(blocks, axis):
    return [blocks[0]] + [swap(block, axis, d) for d, block in enumerate(blocks) if d]


def by_distance(blocks, axis):
    me = lax.axis_index(axis)
    return [pick(blocks, jnp.bitwise_xor(me, d)) for d in range(blocks.shape[0])]


def collect(value, axis):
    me = lax.axis_index(axis)
    return collected([value] + [swap(value, axis, d) for d in range(1, lax.axis_size(axis))], me)


def sum_over_peers(mine, other, beside=()):
    peers = lax.axis_size("ch")
    if peers != 8:
        part = jnp.concatenate([mine, other], axis=0).reshape(peers, -1, mine.shape[2])
        got = lax.all_to_all(part, "ch", split_axis=0, concat_axis=0, tiled=True)
        part = lax.all_gather(got.astype(f32).sum(axis=0).astype(bf16), "ch", axis=0, tiled=True).reshape(part.shape)
        return part[: peers // 2], part[peers // 2 :], beside
    half = tree_sum([mine, swap(other, "ch", 1)]).astype(bf16)
    pieces = [half[0]] + [swap(half[d], "ch", 2 * d) for d in range(1, peers // 2)]
    own = tree_sum(pieces).astype(bf16)
    pieces = [own] + [swap(own, "ch", 2 * d) for d in range(1, peers // 2)]
    pieces, beside = lax.optimization_barrier((pieces, beside))
    half = jnp.stack(pieces)
    return half, swap(half, "ch", 1), beside


def in_order(mine, other, place):
    chips = jnp.bitwise_xor(jnp.arange(mine.shape[0]), place[1])
    halves = jnp.stack([mine[chips], other[chips]])
    return halves[jnp.bitwise_xor(jnp.arange(2), place[0])].reshape(-1, mine.shape[2])


def by_place(part, peers, place):
    halves = part.reshape(2, peers // 2, -1, part.shape[1])[jnp.bitwise_xor(jnp.arange(2), place[0])]
    halves = halves[:, jnp.bitwise_xor(jnp.arange(peers // 2), place[1])]
    return halves[0], halves[1]


def to_peers(blocks):
    return lax.all_to_all(blocks, "ch", split_axis=0, concat_axis=0, tiled=True)


def finish_kernel(
    parts, me_ref, *refs,
):
    n = parts
    late, outs, (cross_ref, branch_ref, dn_ref, hid_ref, grad_ref, gain_ref) = refs[:n], refs[n : 2 * n], refs[2 * n : 2 * n + 6]
    (out_ref, dh_ref, dgain_ref, din_ref, dcw_ref, dcb_ref, dxw_ref, ddtw_ref, ddtb_ref, dalog_ref, dskip_ref,
     dout_ref, s_small) = refs[2 * n + 6 :]
    chans = dcb_ref.shape[1]
    inner = din_ref.shape[1] // 2
    share = din_ref.shape[0] // n
    peers = inner // chans
    low_cols, rank, states, taps = dxw_ref.shape[0], ddtw_ref.shape[0], dalog_ref.shape[0], dcw_ref.shape[0]
    for d in range(n):
        who = jnp.bitwise_xor(me_ref[0], d)
        rows = block_rows(who, share)
        sides = dout_ref.shape[1] // chans
        out_share = dout_ref.shape[0] // n
        for p in range(peers):
            here = slice(p * share, (p + 1) * share)
            din_ref[rows, p * chans : (p + 1) * chans] = late[d][here, :].astype(f32)
            here = slice(sides * out_share + p * share, sides * out_share + (p + 1) * share)
            din_ref[rows, inner + p * chans : inner + (p + 1) * chans] = outs[d][here, :].astype(f32)
        small = late[d][share * peers :, :].astype(f32)
        s_small[block_rows(who, small.shape[0]), :] = small
        for i in range(sides):
            part = outs[d][i * out_share : (i + 1) * out_share, :].astype(f32)
            dout_ref[block_rows(who, out_share), i * chans : (i + 1) * chans] = part
    gain = jnp.sum(cross_ref[:, share:, :].astype(f32), axis=0)
    dgain_ref[...] = gain[:1, : dgain_ref.shape[1]]
    at = low_cols + rank
    ddtw_ref[...] = s_small[low_cols:at, :]
    dxw_ref[...] = s_small[:low_cols, :]
    tail = s_small[at:, :]
    dalog_ref[...] = tail[:states]
    dcw_ref[...] = tail[states : states + taps]
    at = states + taps
    dcb_ref[...] = tail[at : at + 1]
    ddtb_ref[...] = tail[at + 1 : at + 2]
    dskip_ref[...] = tail[at + 2 : at + 3]
    hidden = hid_ref[...].astype(f32)
    out_ref[...] = (hidden + branch_ref[...].astype(f32)).astype(bf16)
    scale = lax.rsqrt(jnp.mean(hidden * hidden, axis=1, keepdims=True) + eps)
    unit = hidden * scale
    d_unit = dn_ref[...].astype(f32) * gain_ref[...]
    mean = jnp.mean(d_unit * unit, axis=1, keepdims=True)
    dh_ref[...] = (grad_ref[...].astype(f32) + scale * (d_unit - unit * mean)).astype(bf16)


def run_finish(late, outs, cross, branch, d_normed, hidden, grad, gain, sizes, me):
    rows, width = hidden.shape
    low_cols, rank, states, taps, small_rows = sizes
    packs = len(late)
    chans = late[0].shape[1]
    in_rows = width // cross.shape[0]
    inner = chans * cross.shape[0]
    wide = [*late, *outs, cross, branch, d_normed, hidden, grad, gain]
    shapes = [
        like(rows, width, dtype=bf16), like(rows, width, dtype=bf16), like(1, in_rows), like(in_rows, 2 * inner),
        like(taps, chans), like(1, chans), like(low_cols, chans), like(rank, chans), like(1, chans),
        like(states, chans), like(1, chans), like(chans, width),
    ]
    return pl.pallas_call(
        functools.partial(finish_kernel, packs),
        grid=(1,),
        in_specs=[SCALARS] + [whole(*a.shape) for a in wide],
        out_specs=[whole(*a.shape) for a in shapes],
        out_shape=shapes,
        scratch_shapes=[pltpu.VMEM((small_rows, chans), f32)],
        compiler_params=pltpu.CompilerParams(vmem_limit_bytes=20 * MIB),
        cost_estimate=about(4),
        name="finish",
    )(me[None], *wide)


def finish_plain(late, outs, cross, branch, d_normed, hidden, grad, gain, sizes, me):
    low_cols, rank, states, taps, small_rows = sizes
    packs, peers, chans = len(late), cross.shape[0], late[0].shape[1]
    share = hidden.shape[1] // (peers * packs)
    late = collected(late, me).astype(f32)
    outs = collected(outs, me).astype(f32)
    sides = hidden.shape[1] // chans
    out_share = chans // packs
    halves = [late[:, : share * peers], outs[:, sides * out_share :]]
    halves = jnp.stack(halves).reshape(2, packs, peers, share, chans)
    d_in = jnp.transpose(halves, (1, 3, 0, 2, 4)).reshape(packs * share, 2 * peers * chans)
    d_out = outs[:, : sides * out_share].reshape(packs, sides, out_share, chans)
    d_out = jnp.moveaxis(d_out, 1, 2).reshape(chans, sides * chans)
    small = late[:, share * peers :].reshape(small_rows, chans)
    parts = []
    at = 0
    for count in (low_cols, rank, states, taps, 1, 1, 1):
        parts.append(small[at : at + count])
        at += count
    d_xw, d_dtw, d_alog, d_cw, d_cb, d_dtb, d_skip = parts
    d_gain = cross[:, share:].astype(f32).sum(axis=0).reshape(1, -1)[:, : share * packs]
    hidden = hidden.astype(f32)
    output = (hidden + branch.astype(f32)).astype(bf16)
    scale = lax.rsqrt(jnp.mean(hidden * hidden, axis=1, keepdims=True) + eps)
    unit = hidden * scale
    d_unit = d_normed.astype(f32) * gain
    mean = jnp.mean(d_unit * unit, axis=1, keepdims=True)
    d_hidden = (grad.astype(f32) + scale * (d_unit - unit * mean)).astype(bf16)
    return output, d_hidden, d_gain, d_in, d_cw, d_cb, d_xw, d_dtw, d_dtb, d_alog, d_skip, d_out


def on_device(
    hidden_in, norm_gain, in_weight, conv_weight, conv_bias, x_weight, dt_weight, dt_bias, a_log, skip, out_weight,
    lengths, resets, out_grad,
):
    peers = lax.axis_size("ch")
    packs = lax.axis_size("ctx")
    me = lax.axis_index("ch")
    rows, width = hidden_in.shape
    chans = out_weight.shape[0]
    taps = conv_weight.shape[1]
    rank, states = dt_weight.shape[0], a_log.shape[1]
    total = rows * peers

    hidden_all = lax.all_gather(hidden_in, "ch", axis=0, tiled=True)
    in_rows = in_weight.shape[0]
    share = in_rows // packs
    my_share = lax.dynamic_slice_in_dim(in_weight, lax.axis_index("ctx") * share, share, 0)
    got = to_peers(jnp.moveaxis(my_share.reshape(share, 2, peers, chans), 2, 0))
    grad_all = lax.all_gather(out_grad, "ch", axis=0, tiled=True)

    steps = total // SEGS
    span = scan_span(steps)
    low_cols = rank + 2 * states
    lanes = -(-low_cols // 128) * 128
    sizes = lengths[0]
    offsets = jnp.cumsum(sizes) - sizes
    where_in = context_place(offsets, jnp.arange(total, dtype=jnp.int32))
    cut = ((where_in == 0) | (resets == 1)).astype(bf16).reshape(SEGS, steps).T.reshape(total, 1)
    cut = jnp.broadcast_to(cut, (total, lane_groups(chans)[1]))
    starts = offsets[None, :]
    conv_w = lax.dynamic_slice_in_dim(conv_weight, me * chans, chans, 0).T
    conv_b = lax.dynamic_slice_in_dim(conv_bias, me * chans, chans, 0)[None, :]
    x_w = lax.dynamic_slice_in_dim(x_weight, me * chans, chans, 0)
    x_w = jnp.pad(x_w, ((0, 0), (0, lanes - low_cols)))

    near = peers == 8
    place = jnp.stack([me % 2 if near else 0 * me, me // 2 if near else 0 * me, lax.axis_index("ctx")])
    dt_w_t = jnp.pad(dt_weight.T, ((0, 0), (0, lanes - rank)))
    got, cut, dt_w_t, conv_w, conv_b, x_w, starts = lax.optimization_barrier(
        (got, cut, dt_w_t, conv_w, conv_b, x_w, starts)
    )
    shares = collect(got.reshape(peers, share, 2 * chans), "ctx")
    my_cols = jnp.moveaxis(shares, 0, 1).reshape(width, 2 * chans)

    normed, scale_all, x_in, gate, values, pre, *proj_part = run_entry(
        place, starts, hidden_all, my_cols, norm_gain[None, :], conv_w, conv_b, x_w, peers, span
    )
    mine, other, _ = sum_over_peers(*proj_part)

    a_log_t = a_log.T
    dt_b, skip_row = dt_bias[None, :], skip[None, :]
    if total * chans * states <= 1 << 22 and chans % 128 == 0:
        (
            branch_part, gated, d_gate, d_mine, d_other, value_part, d_dt_weight, d_dt_bias, d_a_log_t, d_skip,
        ) = run_scan(
            place, mine, other, values, gate, cut, grad_all, out_weight, dt_weight, dt_w_t, dt_b, a_log_t, skip_row,
            states, span,
        )
    else:
        proj = in_order(mine, other, place)
        y, hist, delta = run_forward(proj, values, cut, dt_weight, dt_b, a_log_t, states, span)
        branch_part, gated, dy, d_gate, d_skip = run_gate(grad_all, out_weight, gate, values, y, skip_row, span)
        d_part, value_part, d_dt_weight, d_dt_bias, d_a_log_t = run_backward(
            proj, values, cut, dy, delta, dt_weight, dt_w_t, dt_b, a_log_t, skip_row, hist, states, span
        )
        d_mine, d_other = by_place(d_part, peers, place)
    branch = lax.psum_scatter(branch_part, "ch", scatter_dimension=0, tiled=True)
    sides = width // chans
    out_share = chans // packs
    d_out = dot(gated, grad_all, (0, 0)).astype(bf16).reshape(packs, out_share, sides, chans)
    d_out = jnp.moveaxis(d_out, 2, 1).reshape(packs, out_share * sides, chans)
    d_in_gate = dot(normed.reshape(total, width), d_gate, (0, 0)).astype(bf16)

    def by_pack(d_in):
        return jnp.moveaxis(d_in.reshape(peers, packs, share, chans), 1, 0).reshape(packs, peers * share, chans)

    early = owned_parts(by_distance(jnp.concatenate([d_out, by_pack(d_in_gate)], axis=1), "ctx"), "ctx")

    mine, other, early = sum_over_peers(d_mine, d_other, early)
    early = tree_sum(early).astype(bf16)
    counts = (low_cols, rank, states, taps)
    small_rows = -(-(sum(counts) + 3) // (16 * packs)) * 16 * packs
    d_normed_part, late = run_exit(
        place, starts, mine, other, value_part, pre, x_in, values, conv_w, x_w, d_gate, my_cols, hidden_all, scale_all,
        norm_gain[None, :], d_dt_weight, d_a_log_t, d_dt_bias, d_skip, low_cols, small_rows, packs, peers, span,
    )
    d_normed = lax.psum_scatter(d_normed_part, "ch", scatter_dimension=0, tiled=True)

    late = tree_sum(owned_parts(late, "ctx")).astype(bf16)
    own_rows = peers * share
    gain_rows = late[own_rows + small_rows // packs :][:sides].reshape(peers, in_rows)
    pad_rows = -(-in_rows // chans)
    gain_rows = jnp.pad(gain_rows, ((0, 0), (0, pad_rows * chans - in_rows))).reshape(peers, pad_rows, chans)
    gain_rows = jnp.pad(gain_rows, ((0, 0), (0, -pad_rows % 16), (0, 0)))
    early_in = to_peers(early[out_share * sides :].reshape(peers, share, chans)).reshape(own_rows, chans)
    early = jnp.concatenate([early[: out_share * sides], early_in], axis=0)
    cross = jnp.concatenate([late[:own_rows].reshape(peers, share, chans), gain_rows], axis=1)
    early, _ = lax.optimization_barrier((early, cross))
    cross = to_peers(cross)
    outs = [early] + [swap(early, "ctx", d) for d in range(1, packs)]
    own = [cross[:, :share].reshape(own_rows, chans), late[own_rows : own_rows + small_rows // packs]]
    own = jnp.concatenate(own, axis=0)
    late = [own] + [swap(own, "ctx", d) for d in range(1, packs)]
    finish = run_finish if share % 16 == 0 and chans % 128 == 0 else finish_plain
    (
        output, d_hidden, gain_sum, in_sum, conv_w_sum, conv_b_sum, x_w_sum, dt_w_sum, dt_b_sum, a_log_sum, skip_sum,
        out_sum,
    ) = finish(
        late, outs, cross, branch, d_normed, hidden_in, out_grad, norm_gain[None, :], (*counts, small_rows),
        lax.axis_index("ctx"),
    )
    return (
        output, d_hidden, gain_sum[0], in_sum, conv_w_sum.T, conv_b_sum[0], x_w_sum.T, dt_w_sum, dt_b_sum[0],
        a_log_sum.T, skip_sum[0], out_sum,
    )


def solution(mesh):
    return jax.shard_map(
        on_device,
        mesh=mesh,
        in_specs=(
            P(("ctx", "ch"), None), P(), P("ch", None), P(), P(), P(), P(None, "ch"), P("ch"), P("ch", None),
            P("ch"), P("ch", None), P("ctx", None), P("ctx"), P(("ctx", "ch"), None),
        ),
        out_specs=(
            P(("ctx", "ch"), None), P(("ctx", "ch"), None), P("ch"), P("ch", None), P("ch", None), P("ch"),
            P("ch", None), P(None, "ch"), P("ch"), P("ch", None), P("ch"), P("ch", None),
        ),
        check_vma=False,
    )
```

```python
import functools
import math

import jax
import jax.numpy as jnp
from jax import lax
from jax.experimental import pallas as pl
from jax.experimental.pallas import tpu as pltpu
from jax.sharding import PartitionSpec as P

f32 = jnp.float32
bf16 = jnp.bfloat16
eps = 1e-05
LOG2E = 1.4426950408889634
CUT = 1e30
SEGS = 8
BATCH = 4
TOGETHER = 4
MIB = 1 << 20
ROOM = 56 * MIB


def silu(v):
    return v * jax.nn.sigmoid(v)


def silu_slope(v):
    sig = jax.nn.sigmoid(v)
    return sig * (1.0 + v * (1.0 - sig))


def context_place(offsets, places):
    begins = jnp.max(jnp.where(offsets[:, None] <= places[None, :], offsets[:, None], 0), axis=0)
    return places - begins


def dot(a, b, dims, precision=None):
    return lax.dot_general(a, b, ((dims[:1], dims[1:]), ((), ())), precision=precision, preferred_element_type=f32)


def lane_groups(chans):
    width = 128 if chans % 128 == 0 else chans
    return chans // width, width


def softplus(v):
    small = jnp.exp(-jnp.abs(v))
    series = small * (1.0 - small * (0.5 - small * (1.0 / 3.0)))
    return jnp.maximum(v, 0.0) + jnp.where(small < 0.01, series, jnp.log(1.0 + small))


def mixing(span, back):
    size = span * SEGS
    row = lax.broadcasted_iota(jnp.int32, (size, size), 0)
    column = lax.broadcasted_iota(jnp.int32, (size, size), 1)
    if back:
        hit = (row % span) * SEGS + row // span == column
    else:
        hit = (row % SEGS) * span + row // SEGS == column
    return hit.astype(f32).astype(bf16)


def context_positions(starts_ref, first_row, rows, steps, lanes):
    row = lax.broadcasted_iota(jnp.int32, (rows, lanes), 0) + first_row
    token = jnp.bitwise_and(row, SEGS - 1) * steps + jnp.right_shift(row, SEGS.bit_length() - 1)
    begin = jnp.zeros((rows, lanes), jnp.int32)
    for c in range(starts_ref.shape[1]):
        begin = jnp.where(starts_ref[0, c] <= token, starts_ref[0, c], begin)
    return token - begin


def split_dot(wide, narrow, dims, swapped=False):
    high = wide.astype(bf16)
    low = (wide - high.astype(f32)).astype(bf16)
    if swapped:
        return dot(narrow, high, dims) + dot(narrow, low, dims)
    return dot(high, narrow, dims) + dot(low, narrow, dims)


def put(ref, rows, value, groups, width):
    for g in range(groups):
        ref[g, rows, :] = value[:, g * width : (g + 1) * width]


def take(ref, rows, groups):
    return jnp.concatenate([ref[g, rows, :] for g in range(groups)], axis=1) if groups > 1 else ref[0, rows, :]


def piece_rows(me_ref, core, apart, chips, rows):
    place = jnp.bitwise_xor(me_ref[0], core) * chips + jnp.bitwise_xor(me_ref[1], apart)
    return pl.ds(pl.multiple_of(place * rows, rows), rows)


def put_pieces(me_ref, refs, source_ref):
    for core, ref in enumerate(refs):
        for apart in range(ref.shape[0]):
            ref[apart] = source_ref[piece_rows(me_ref, core, apart, ref.shape[0], ref.shape[1]), :]


def take_pieces(me_ref, refs, target_ref):
    for core, ref in enumerate(refs):
        for apart in range(ref.shape[0]):
            target_ref[piece_rows(me_ref, core, apart, ref.shape[0], ref.shape[1]), :] = ref[apart]


def block_rows(t, size):
    return pl.ds(pl.multiple_of(t * size, size), size)


def entry_kernel(
    span, taps, me_ref, starts_ref, hid_ref, w_ref, gain_ref, cw_ref, cb_ref, xw_ref,
    normed_ref, scale_ref, x_ref, gate_ref, val_ref, pre_ref, mine_ref, other_ref, s_x, s_mixing, s_proj,
):
    turn = pl.program_id(0)
    turns = pl.num_programs(0) - 1
    chans = x_ref.shape[1]
    size = span * SEGS
    steps = span * turns
    halo = (taps - 1) * SEGS
    groups, width = lane_groups(chans)

    @pl.when(turn == 0)
    def _():
        s_mixing[...] = mixing(span, False)

    @pl.when(turn < turns)
    def _():
        wide = hid_ref[...].astype(f32).reshape(size, hid_ref.shape[2])
        scale = lax.rsqrt(jnp.mean(wide * wide, axis=1, keepdims=True) + eps)
        normed = (wide * scale * gain_ref[...]).astype(bf16)
        normed_ref[...] = normed.reshape(normed_ref.shape)
        scale_ref[...] = jnp.broadcast_to(scale, (size, 128)).reshape(scale_ref.shape)
        mixed = dot(normed, w_ref[...], (1, 0)).astype(bf16)
        mixed = dot(s_mixing[...], mixed, (1, 0))
        x_ref[...] = mixed[:, :chans].astype(bf16)
        gate_ref[...] = mixed[:, chans:].astype(bf16)
        s_x[pl.ds(pl.multiple_of(turn * size + halo, SEGS), size), :] = mixed[:, :chans]

    @pl.when(turn == turns)
    def _():
        first = lax.broadcasted_iota(jnp.int32, (SEGS, chans), 0) == 0
        for j in range(taps - 1):
            last = s_x[pl.ds(pl.multiple_of(steps * SEGS + j * SEGS, SEGS), SEGS), :]
            s_x[j * SEGS : (j + 1) * SEGS, :] = jnp.where(first, 0.0, pltpu.roll(last, 1, 0))

    @pl.when(turn > 0)
    def _():
        t = jnp.where(turn == turns, 0, turn)
        place = jnp.concatenate([context_positions(starts_ref, t * size, size, steps, width)] * groups, axis=1)
        pre = cb_ref[...] + jnp.zeros((size, chans), f32)
        for k in range(taps):
            lag = taps - 1 - k
            at = pl.ds(pl.multiple_of(t * size + halo - lag * SEGS, SEGS), size)
            pre = pre + cw_ref[k : k + 1, :] * jnp.where(place >= lag, s_x[at, :], 0.0)
        pre_ref[...] = pre
        values = silu(pre).astype(bf16)
        val_ref[...] = values
        s_proj[block_rows(t, size), :] = dot(values, xw_ref[...], (1, 0)).astype(bf16)

    @pl.when(turn == turns)
    def _():
        put_pieces(me_ref, (mine_ref, other_ref), s_proj)


def gate_kernel(
    span, grad_ref, w_ref, gate_ref, val_ref, y_ref, skip_ref,
    branch_ref, gated_ref, dy_ref, dgate_ref, dskip_ref, s_in, s_out,
):
    turn = pl.program_id(0)
    size = span * SEGS

    @pl.when(turn == 0)
    def _():
        s_in[...] = mixing(span, False)
        s_out[...] = mixing(span, True)
        dskip_ref[...] = jnp.zeros_like(dskip_ref)

    vals = val_ref[...].astype(f32)
    gate = gate_ref[...].astype(f32)
    sig = jax.nn.sigmoid(gate)
    act = gate * sig
    scanned = y_ref[...] + skip_ref[...] * vals
    gated = dot(s_out[...], (scanned * act).astype(bf16), (1, 0)).astype(bf16)
    gated_ref[...] = gated.reshape(gated_ref.shape)
    branch_ref[...] = dot(gated, w_ref[...], (1, 0)).astype(bf16).reshape(branch_ref.shape)
    grad = grad_ref[...].reshape(size, grad_ref.shape[2])
    d_gated = dot(s_in[...], dot(grad, w_ref[...], (1, 1)).astype(bf16), (1, 0))
    dy = d_gated * act
    dy_ref[...] = dy
    d_gate = (d_gated * scanned * (sig * (1.0 + gate * (1.0 - sig)))).astype(bf16)
    d_gate = dot(s_out[...], d_gate, (1, 0)).astype(bf16)
    dgate_ref[...] = d_gate.reshape(dgate_ref.shape)
    dskip_ref[...] += jnp.sum(dy * vals, axis=0, keepdims=True)


def exit_kernel(
    span, taps, low_cols, packs, peers, me_ref, starts_ref, mine_ref, other_ref, part_ref, pre_ref, x_ref, val_ref, cw_ref, xw_ref, dgate_ref, w_ref,
    hid_ref, scale_ref, gain_ref, ddtw_ref, dalog_ref, ddtb_ref, dskip_ref,
    dn_ref, *refs,
):
    *out_refs, s_pre, s_dx, s_din, s_place, s_small, dgain_ref, dproj_ref = refs
    total, chans = x_ref.shape
    size = span * SEGS
    steps = total // SEGS
    turns = steps // span
    halo = (taps - 1) * SEGS
    groups, width = lane_groups(chans)
    turn = pl.program_id(0)

    @pl.when(turn == 0)
    def _():
        take_pieces(me_ref, (mine_ref, other_ref), dproj_ref)

        def first(t, carry):
            rows = block_rows(t, size)
            d_proj = dproj_ref[rows, :]
            d_values = part_ref[rows, :] + dot(d_proj, xw_ref[...], (1, 1))
            d_pre = d_values * silu_slope(pre_ref[rows, :])
            s_pre[rows, :] = d_pre
            s_place[rows, :] = context_positions(starts_ref, t * size, size, steps, width)
            d_bias, d_xw = carry
            return d_bias + jnp.sum(d_pre, axis=0, keepdims=True), d_xw + dot(d_proj, val_ref[rows, :], (0, 0))

        begin = (jnp.zeros((1, chans), f32), jnp.zeros((dproj_ref.shape[1], chans), f32))
        d_bias, d_xw = lax.fori_loop(0, turns, first, begin)
        s_place[total : total + halo, :] = context_positions(starts_ref, total, halo, steps, width)
        last = lax.broadcasted_iota(jnp.int32, (SEGS, chans), 0) == SEGS - 1
        for j in range(taps - 1):
            head = s_pre[j * SEGS : (j + 1) * SEGS, :]
            s_pre[total + j * SEGS : total + (j + 1) * SEGS, :] = jnp.where(last, 0.0, pltpu.roll(head, SEGS - 1, 0))
        back = mixing(span, True)

        def second(t, sums):
            rows = block_rows(t, size)
            x = x_ref[rows, :].astype(f32)
            d_x = jnp.zeros((size, chans), f32)
            out = []
            for k in range(taps):
                lag = taps - 1 - k
                at = pl.ds(pl.multiple_of(t * size + lag * SEGS, SEGS), size)
                valid = jnp.concatenate([s_place[at, :]] * groups, axis=1) >= lag
                later = jnp.where(valid, s_pre[at, :], 0.0)
                d_x = d_x + cw_ref[k : k + 1, :] * later
                out.append(sums[k] + jnp.sum(later * x, axis=0, keepdims=True))
            natural = dot(back, d_x.astype(bf16), (1, 0)).astype(bf16).reshape(SEGS, span, chans)
            s_dx[:, block_rows(t, span), :] = natural
            return tuple(out)

        sums = lax.fori_loop(0, turns, second, (jnp.zeros((1, chans), f32),) * taps)
        s_din[...] = jnp.zeros_like(s_din)
        dgain_ref[...] = jnp.zeros_like(dgain_ref)
        rest = [*sums, d_bias, ddtb_ref[...], dskip_ref[...]]
        small = [d_xw[:low_cols], ddtw_ref[...], dalog_ref[...], *rest]
        pad = s_small.shape[0] - sum(a.shape[0] for a in small)
        s_small[...] = jnp.concatenate([*small, jnp.zeros((pad, chans), f32)], axis=0)

    @pl.when(turn > 0)
    def _():
        rows = hid_ref.shape[0]
        per_segment = steps // rows if rows <= steps else 1
        if rows <= steps:
            here = pl.ds(pl.multiple_of((turn - 1) % per_segment * rows, rows), rows)
            d_x = s_dx[(turn - 1) // per_segment, here, :]
        else:
            d_x = s_dx[pl.ds((turn - 1) * (rows // steps), rows // steps)].reshape(rows, chans)
        both = jnp.concatenate([d_x, dgate_ref[...]], axis=1)
        d_normed = dot(both, w_ref[...], (1, 1)).astype(bf16)
        dn_ref[...] = d_normed
        unit = hid_ref[...].astype(f32) * jnp.concatenate([scale_ref[...]] * (hid_ref.shape[1] // 128), axis=1)
        dgain_ref[...] += jnp.sum(d_normed.astype(f32) * unit, axis=0, keepdims=True)
        s_din[...] += dot(d_x, (unit * gain_ref[...]).astype(bf16), (0, 0))

    @pl.when(turn == pl.num_programs(0) - 1)
    def _():
        d_in = s_din[...].T
        if len(out_refs) < packs:
            out_refs[0][...] = d_in.astype(bf16)
            out_refs[1][...] = s_small[...].astype(bf16)
            out_refs[2][...] = dgain_ref[...]
            return
        each = s_small.shape[0] // packs
        share = d_in.shape[0] // (peers * packs)
        sides = d_in.shape[0] // chans
        gain = [dgain_ref[:, i * chans : (i + 1) * chans] for i in range(sides)]
        gain = jnp.concatenate([*gain, jnp.zeros((16 - sides, chans), f32)], axis=0).astype(bf16)
        for d, ref in enumerate(out_refs):
            who = jnp.bitwise_xor(me_ref[2], d)
            ref[peers * share : peers * share + each, :] = s_small[block_rows(who, each), :].astype(bf16)
            ref[peers * share + each :, :] = gain
            for p in range(packs):

                @pl.when(who == p)
                def _():
                    for q in range(peers):
                        at = (q * packs + p) * share
                        ref[q * share : (q + 1) * share, :] = d_in[at : at + share].astype(bf16)


def prepare_spread(hot_ref, rank, states):
    hot_ref[...] = jnp.zeros_like(hot_ref)
    row = lax.broadcasted_iota(jnp.int32, (16, 128), 0)
    for n in range(2 * states):
        first = (rank + n) // 16 * 16
        hot_ref[first : first + 16, n * 128 : (n + 1) * 128] = (row + first == rank + n).astype(f32).astype(bf16)


def spread_pair(out_ref, slot, hot_ref, proj_ref, rows, first, pair):
    at = first * 128 + pair * 256
    both = dot(proj_ref[rows, :], hot_ref[:, pl.ds(at if isinstance(at, int) else pl.multiple_of(at, 256), 256)], (1, 0))
    out_ref[slot, 2 * pair] = both[:, :128]
    out_ref[slot, 2 * pair + 1] = both[:, 128:]


def sum_lanes(mix_ref, hot_ref):
    return dot(hot_ref[...], mix_ref[...], (1, 1)).T


def forward_kernel(
    rank, states, span, proj_ref, val_ref, cut_ref, dtw_ref, dtb_ref, alog_ref,
    y_ref, hist_ref, delta_ref, s_cut, s_dx, s_rate, s_state, s_sum, s_b, s_c, s_hot,
):
    total, chans = val_ref.shape
    steps = total // SEGS
    size = span * SEGS
    groups, width = lane_groups(chans)
    turn = pl.program_id(0)
    turns = steps // span
    slots = s_b.shape[0]
    half = states // 2
    count = span // BATCH

    def rate(n, g):
        return s_rate[n : n + 1, g * width : (g + 1) * width]

    @pl.when(turn == 0)
    def _():
        s_rate[...] = -jnp.exp(alog_ref[...]) * LOG2E
        prepare_spread(s_hot, rank, states)
        s_state[...] = jnp.zeros_like(s_state)
        s_sum[...] = jnp.zeros_like(s_sum)
        def block(t, carry):
            rows = block_rows(t, size)
            slot = t if slots > 1 else 0
            for pair in range(half):
                spread_pair(s_b, slot, s_hot, proj_ref, rows, 0, pair)
                spread_pair(s_c, slot, s_hot, proj_ref, rows, states, pair)
            delta = softplus(dot(proj_ref[rows, :rank], dtw_ref[...], (1, 0)) + dtb_ref[...])
            put(delta_ref, rows, delta, groups, width)
            cut = cut_ref[rows, :].astype(f32) * CUT
            put(s_cut, rows, delta + jnp.concatenate([cut] * groups, axis=1), groups, width)
            put(s_dx, rows, delta * val_ref[rows, :].astype(f32), groups, width)

            def sweep(q, carry):
                at = [block_rows(t * span + q * BATCH + j, SEGS) for j in range(BATCH)]
                here = [block_rows(q * BATCH + j, SEGS) for j in range(BATCH)]
                for g in range(groups):
                    cuts = [s_cut[g, at[j], :] for j in range(BATCH)]
                    dxs = [s_dx[g, at[j], :] for j in range(BATCH)]
                    s_sum[g] = s_sum[g] + sum(cuts)
                    for n in range(states):
                        held = s_state[n * groups + g]
                        for j in range(BATCH):
                            push = dxs[j] * s_b[slot, n, here[j], :width]
                            held = jnp.exp2(cuts[j] * rate(n, g)) * held + push
                        s_state[n * groups + g] = held
                return carry

            return lax.fori_loop(0, count, sweep, carry)

        lax.fori_loop(0, turns, block, 0)
        first = lax.broadcasted_iota(jnp.int32, (SEGS, width), 0) == 0
        for n in range(states):
            for g in range(groups):
                gain = jnp.exp2(s_sum[g] * rate(n, g))
                end = s_state[n * groups + g]
                start = jnp.zeros((SEGS, width), f32)
                for _ in range(SEGS - 1):
                    start = jnp.where(first, 0.0, pltpu.roll(gain * start + end, 1, 0))
                s_state[n * groups + g] = start

    slot = turn if slots > 1 else 0
    if slots == 1:
        for pair in range(half):
            spread_pair(s_b, 0, s_hot, proj_ref, block_rows(turn, size), 0, pair)
            spread_pair(s_c, 0, s_hot, proj_ref, block_rows(turn, size), states, pair)

    def sweep(q, carry):
        at = [block_rows(turn * span + q * BATCH + j, SEGS) for j in range(BATCH)]
        here = [block_rows(q * BATCH + j, SEGS) for j in range(BATCH)]
        for g in range(groups):
            cuts = [s_cut[g, at[j], :] for j in range(BATCH)]
            dxs = [s_dx[g, at[j], :] for j in range(BATCH)]
            ys = [None] * BATCH
            for n in range(states):
                i = n * groups + g
                held = s_state[i]
                for j in range(BATCH):
                    hist_ref[0, q * BATCH + j, i] = held
                    push = dxs[j] * s_b[slot, n, here[j], :width]
                    held = jnp.exp2(cuts[j] * rate(n, g)) * held + push
                    term = held * s_c[slot, n, here[j], :width]
                    ys[j] = term if n == 0 else ys[j] + term
                s_state[i] = held
            for j in range(BATCH):
                y_ref[at[j], g * width : (g + 1) * width] = ys[j]
        return carry

    lax.fori_loop(0, count, sweep, 0)
    hist_ref[0, span] = s_state[...]


def backward_kernel(
    rank, states, span, proj_ref, val_ref, cut_ref, dy_ref, delta_ref, dtw_ref, dtwt_ref, dtb_ref, alog_ref, skip_ref,
    hist_ref, part_ref, dval_ref, ddtw_ref, ddtb_ref, dalog_ref,
    s_cut, s_val, s_dd, s_rate, s_state, s_sum, s_drate, s_b, s_c, s_mix, s_hot, s_bc,
):
    total, chans = val_ref.shape
    steps = total // SEGS
    size = span * SEGS
    groups, width = lane_groups(chans)
    turns = steps // span
    turn = pl.program_id(0)
    place = turns - 1 - turn
    slots = s_b.shape[0]
    half = states // 2
    count = span // BATCH
    lane = [slice(g * width, (g + 1) * width) for g in range(groups)]

    def rate(n, g):
        return s_rate[n : n + 1, lane[g]]

    @pl.when(turn == 0)
    def _():
        s_rate[...] = -jnp.exp(alog_ref[...]) * LOG2E
        s_drate[...] = jnp.zeros_like(s_drate)
        s_state[...] = jnp.zeros_like(s_state)
        s_sum[...] = jnp.zeros_like(s_sum)
        if width < 128:
            s_mix[...] = jnp.zeros_like(s_mix)
        prepare_spread(s_hot, rank, states)
        def block(turned, carry):
            t = turns - 1 - turned
            rows = block_rows(t, size)
            slot = t if slots > 1 else 0
            for pair in range(half):
                spread_pair(s_b, slot, s_hot, proj_ref, rows, 0, pair)
                spread_pair(s_c, slot, s_hot, proj_ref, rows, states, pair)
            cut = cut_ref[rows, :].astype(f32) * CUT
            delta = take(delta_ref, rows, groups)
            put(s_cut, rows, delta + jnp.concatenate([cut] * groups, axis=1), groups, width)
            put(s_val, rows, val_ref[rows, :].astype(f32), groups, width)

            def sweep(q, carry):
                k = span - BATCH - q * BATCH
                at = [block_rows(t * span + k + j, SEGS) for j in range(BATCH)]
                here = [block_rows(k + j, SEGS) for j in range(BATCH)]
                for g in range(groups):
                    cuts = [s_cut[g, at[j], :] for j in range(BATCH)]
                    dys = [dy_ref[at[j], lane[g]] for j in range(BATCH)]
                    s_sum[g] = s_sum[g] + sum(cuts)
                    for n in range(states):
                        held = s_state[n * groups + g]
                        for j in reversed(range(BATCH)):
                            held = dys[j] * s_c[slot, n, here[j], :width] + held
                            held = jnp.exp2(cuts[j] * rate(n, g)) * held
                        s_state[n * groups + g] = held
                return carry

            return lax.fori_loop(0, count, sweep, carry)

        lax.fori_loop(0, turns, block, 0)
        last = lax.broadcasted_iota(jnp.int32, (SEGS, width), 0) == SEGS - 1
        for n in range(states):
            for g in range(groups):
                gain = jnp.exp2(s_sum[g] * rate(n, g))
                end = s_state[n * groups + g]
                start = jnp.zeros((SEGS, width), f32)
                for _ in range(SEGS - 1):
                    start = jnp.where(last, 0.0, pltpu.roll(gain * start + end, SEGS - 1, 0))
                s_state[n * groups + g] = start

    slot = place if slots > 1 else 0
    if slots == 1:
        for pair in range(half):
            spread_pair(s_b, 0, s_hot, proj_ref, block_rows(place, size), 0, pair)
            spread_pair(s_c, 0, s_hot, proj_ref, block_rows(place, size), states, pair)

    def sweep(q, carry):
        k = span - BATCH - q * BATCH
        at = [block_rows(place * span + k + j, SEGS) for j in range(BATCH)]
        here = [block_rows(k + j, SEGS) for j in range(BATCH)]
        each = [(j, g) for j in range(BATCH) for g in range(groups)]
        cuts = {(j, g): s_cut[g, at[j], :] for j, g in each}
        deltas = {(j, g): delta_ref[g, at[j], :] for j, g in each}
        vals = {(j, g): s_val[g, at[j], :] for j, g in each}
        dys = {(j, g): dy_ref[at[j], lane[g]] for j, g in each}
        dxs = {e: deltas[e] * vals[e] for e in each}
        by_rate, by_b = {}, {}
        for first in range(0, states, TOGETHER):
            some = [(n, g) for n in range(first, first + TOGETHER) for g in range(groups)]
            held = {(n, g): s_state[n * groups + g] for n, g in some}
            d_rate = {(n, g): s_drate[n * groups + g] for n, g in some}
            after = {(n, g): hist_ref[0, k + BATCH, n * groups + g] for n, g in some}
            mix = {}
            for j in reversed(range(BATCH)):
                for n, g in some:
                    e, i = (j, g), (n, g)
                    b_n = s_b[slot, n, here[j], :width]
                    c_n = s_c[slot, n, here[j], :width]
                    before = hist_ref[0, k + j, n * groups + g]
                    lam = dys[e] * c_n + held[i]
                    held[i] = jnp.exp2(cuts[e] * rate(n, g)) * lam
                    through = held[i] * before
                    d_rate[i] = d_rate[i] + through * deltas[e]
                    terms = (through * rate(n, g), lam * b_n, lam * dxs[e], dys[e] * after[i])
                    by_rate[e] = by_rate[e] + terms[0] if e in by_rate else terms[0]
                    by_b[e] = by_b[e] + terms[1] if e in by_b else terms[1]
                    for m, term in ((n, terms[2]), (states + n, terms[3])):
                        mix[j, m] = mix[j, m] + term if (j, m) in mix else term
                    after[i] = before
                if j % 2 == 0:
                    two = pl.ds(pl.multiple_of((k + j) * SEGS, 2 * SEGS), 2 * SEGS)
                    for n in range(first, first + TOGETHER):
                        for m in (n, states + n):
                            value = jnp.concatenate([mix[j, m], mix[j + 1, m]], axis=0).astype(bf16)
                            s_mix[two, m * 128 : m * 128 + width] = value
            for n, g in some:
                s_state[n * groups + g] = held[n, g]
                s_drate[n * groups + g] = d_rate[n, g]
        for j, g in each:
            e = (j, g)
            s_dd[g, at[j], :] = by_rate[e] * (1.0 / LOG2E) + by_b[e] * vals[e]
            dval_ref[at[j], lane[g]] = by_b[e] * deltas[e] + dys[e] * skip_ref[:, lane[g]]
        return carry

    lax.fori_loop(0, count, sweep, 0)
    rows = block_rows(place, size)
    s_bc[...] = sum_lanes(s_mix, s_hot)
    pre = dot(proj_ref[rows, :rank], dtw_ref[...], (1, 0)) + dtb_ref[...]
    d_pre = take(s_dd, rows, groups) * jax.nn.sigmoid(pre)
    d_bias = jnp.sum(d_pre, axis=0, keepdims=True)
    d_dtw = split_dot(d_pre, proj_ref[rows, :rank], (0, 0), swapped=True)
    part = split_dot(d_pre, dtwt_ref[...], (1, 0))
    part_ref[rows, :] = (part + s_bc[...]).astype(bf16)

    @pl.when(turn == 0)
    def _():
        ddtb_ref[...] = d_bias
        ddtw_ref[...] = d_dtw

    @pl.when(turn > 0)
    def _():
        ddtb_ref[...] += d_bias
        ddtw_ref[...] += d_dtw

    @pl.when(turn == turns - 1)
    def _():
        sums = [jnp.sum(s_drate[i], axis=0, keepdims=True) for i in range(states * groups)]
        rows = [jnp.concatenate(sums[n * groups : (n + 1) * groups], axis=1) for n in range(states)]
        dalog_ref[...] = jnp.concatenate(rows, axis=0) * s_rate[...] * (1.0 / LOG2E)


def scan_kernel(
    rank, states, span, me_ref, mine_ref, other_ref, val_ref, gate_ref, cut_ref, grad_ref, w_ref, dtw_ref, dtwt_ref, dtb_ref, alog_ref,
    skip_ref, branch_ref, gated_ref, dgate_ref, pmine_ref, pother_ref, dval_ref, ddtw_ref, ddtb_ref, dalog_ref, dskip_ref,
    s_cut, s_delta, s_val, s_dy, s_hist, s_b, s_c, s_y, s_rate, s_state, s_drate, s_mix, s_hot, s_in, s_out, s_even, proj_ref, part_ref,
):
    total, chans = val_ref.shape
    steps = total // SEGS
    size = span * SEGS
    groups, width = lane_groups(chans)
    pairs = [(n, g) for n in range(states) for g in range(groups)]
    every = range(groups)
    lane = [slice(g * width, (g + 1) * width) for g in every]
    turns = steps // span
    turn = pl.program_id(0)
    zero = jnp.zeros((SEGS, width), f32)
    sublane = lax.broadcasted_iota(jnp.int32, (SEGS, width), 0)

    def decay(cut, n, g):
        return jnp.exp2(cut * s_rate[n : n + 1, lane[g]])

    def chained(ends, sums, edge, shift):
        for n, g in pairs:
            gain = decay(sums[g], n, g)
            end = ends[n * groups + g]
            start = zero
            for _ in range(SEGS - 1):
                start = jnp.where(sublane == edge, 0.0, pltpu.roll(gain * start + end, shift, 0))
            s_state[n * groups + g] = start

    @pl.when(turn == 0)
    def _():
        s_rate[...] = -jnp.exp(alog_ref[...]) * LOG2E
        s_drate[...] = jnp.zeros_like(s_drate)
        dskip_ref[...] = jnp.zeros_like(dskip_ref)
        s_in[...] = mixing(span, False)
        s_out[...] = mixing(span, True)
        prepare_spread(s_hot, rank, states)
        take_pieces(me_ref, (mine_ref, other_ref), proj_ref)
        s_even[...] = jnp.concatenate([s_hot[:, n * 128 : (n + 1) * 128] for n in range(0, 2 * states, 2)], axis=1)

        def fill(t, carry):
            rows = block_rows(t, size)
            for n in range(0, states, 2):
                for ref, first in ((s_b, n), (s_c, states + n)):
                    both = dot(proj_ref[rows, :], s_hot[:, first * 128 : (first + 2) * 128], (1, 0))
                    ref[n, rows, :] = both[:, :128]
                    ref[n + 1, rows, :] = both[:, 128:]
            delta = softplus(dot(proj_ref[rows, :rank], dtw_ref[...], (1, 0)) + dtb_ref[...])
            cut = cut_ref[rows, :].astype(f32) * CUT
            put(s_delta, rows, delta, groups, width)
            put(s_cut, rows, delta + jnp.concatenate([cut] * groups, axis=1), groups, width)
            put(s_val, rows, val_ref[rows, :].astype(f32), groups, width)
            return carry

        lax.fori_loop(0, turns, fill, 0)

        def sweep(i, carry):
            held, sums = carry
            at = block_rows(i, SEGS)
            cuts = [s_cut[g, at, :] for g in every]
            dxs = [s_delta[g, at, :] * s_val[g, at, :] for g in every]
            out = [decay(cuts[g], n, g) * held[n * groups + g] + dxs[g] * s_b[n, at, :width] for n, g in pairs]
            return tuple(out), tuple(sums[g] + cuts[g] for g in every)

        begin = ((zero,) * len(pairs), (zero,) * groups)
        chained(*lax.fori_loop(0, steps, sweep, begin, unroll=16), 0, 1)

    @pl.when(turn < turns)
    def _():

        def sweep(k, held):
            i = turn * span + k
            at = block_rows(i, SEGS)
            cuts = [s_cut[g, at, :] for g in every]
            dxs = [s_delta[g, at, :] * s_val[g, at, :] for g in every]
            ys = [zero] * groups
            out = []
            for n in range(states):
                b_n = s_b[n, at, :width]
                c_n = s_c[n, at, :width]
                for g in every:
                    old = held[n * groups + g]
                    s_hist[i, n * groups + g] = old
                    new = decay(cuts[g], n, g) * old + dxs[g] * b_n
                    out.append(new)
                    ys[g] = ys[g] + new * c_n
            for g in every:
                s_y[block_rows(k, SEGS), lane[g]] = ys[g]
            return tuple(out)

        held = lax.fori_loop(0, span, sweep, tuple(s_state[j] for j in range(len(pairs))), unroll=16)
        for j in range(len(pairs)):
            s_state[j] = held[j]

        @pl.when(turn == turns - 1)
        def _():
            s_hist[steps] = s_state[...]

        rows = block_rows(turn, size)
        vals = val_ref[rows, :].astype(f32)
        gate = gate_ref[...].astype(f32)
        sig = jax.nn.sigmoid(gate)
        act = gate * sig
        scanned = s_y[...] + skip_ref[...] * vals
        grad = grad_ref[...].reshape(size, grad_ref.shape[2])
        d_gated = dot(s_in[...], dot(grad, w_ref[...], (1, 1)).astype(bf16), (1, 0))
        dy = d_gated * act
        put(s_dy, rows, dy, groups, width)
        d_gate = d_gated * scanned * (sig * (1.0 + gate * (1.0 - sig)))
        both = jnp.concatenate([(scanned * act).astype(bf16), d_gate.astype(bf16)], axis=1)
        both = dot(s_out[...], both, (1, 0)).astype(bf16)
        gated_ref[...] = both[:, :chans].reshape(gated_ref.shape)
        dgate_ref[...] = both[:, chans:].reshape(dgate_ref.shape)
        branch_ref[...] = dot(both[:, :chans], w_ref[...], (1, 0)).astype(bf16).reshape(branch_ref.shape)
        dskip_ref[...] += jnp.sum(dy * vals, axis=0, keepdims=True)

    @pl.when(turn == turns)
    def _():
        ddtb_ref[...] = jnp.zeros_like(ddtb_ref)
        ddtw_ref[...] = jnp.zeros_like(ddtw_ref)

        def sweep(back, carry):
            held, sums = carry
            at = block_rows(steps - 1 - back, SEGS)
            cuts = [s_cut[g, at, :] for g in every]
            dys = [s_dy[g, at, :] for g in every]
            out = []
            for n, g in pairs:
                lam = dys[g] * s_c[n, at, :width] + held[n * groups + g]
                out.append(decay(cuts[g], n, g) * lam)
            return tuple(out), tuple(sums[g] + cuts[g] for g in every)

        begin = ((zero,) * len(pairs), (zero,) * groups)
        chained(*lax.fori_loop(0, steps, sweep, begin, unroll=16), SEGS - 1, SEGS - 1)

    @pl.when(turn >= turns)
    def _():
        place = 2 * turns - 1 - turn

        def sweep(back, held):
            k = span - 1 - back
            i = place * span + k
            at = block_rows(i, SEGS)
            cuts = [s_cut[g, at, :] for g in every]
            deltas = [s_delta[g, at, :] for g in every]
            vals = [s_val[g, at, :] for g in every]
            dys = [s_dy[g, at, :] for g in every]
            dxs = [deltas[g] * vals[g] for g in every]
            by_rate = [zero] * groups
            by_b = [zero] * groups
            out = []
            mixes = {}
            for n in range(states):
                b_n = s_b[n, at, :width]
                c_n = s_c[n, at, :width]
                mix = mix_c = None
                for g in every:
                    j = n * groups + g
                    lam = dys[g] * c_n + held[j]
                    onward = decay(cuts[g], n, g) * lam
                    out.append(onward)
                    through = onward * s_hist[i, j]
                    by_rate[g] = by_rate[g] + through * s_rate[n : n + 1, lane[g]]
                    by_b[g] = by_b[g] + lam * b_n
                    s_drate[j] = s_drate[j] + through * deltas[g]
                    term, term_c = lam * dxs[g], dys[g] * s_hist[i + 1, j]
                    mix = term if mix is None else mix + term
                    mix_c = term_c if mix_c is None else mix_c + term_c
                mixes[n], mixes[states + n] = mix, mix_c
                if n % 2:
                    for first in (n - 1, states + n - 1):
                        two = jnp.concatenate([mixes[first], mixes[first + 1]], axis=0).astype(bf16)
                        s_mix[block_rows(k, 2 * SEGS), first * 64 : first * 64 + width] = two
            for g in every:
                s_cut[g, at, :] = by_rate[g] * (1.0 / LOG2E) + by_b[g] * vals[g]
                dval_ref[block_rows(k, SEGS), lane[g]] = by_b[g] * deltas[g] + dys[g] * skip_ref[:, lane[g]]
            return tuple(out)

        held = lax.fori_loop(0, span, sweep, tuple(s_state[j] for j in range(len(pairs))), unroll=16)
        for j in range(len(pairs)):
            s_state[j] = held[j]
        rows = block_rows(place, size)
        pre = dot(proj_ref[rows, :rank], dtw_ref[...], (1, 0)) + dtb_ref[...]
        d_pre = take(s_cut, rows, groups) * jax.nn.sigmoid(pre)
        ddtb_ref[...] += jnp.sum(d_pre, axis=0, keepdims=True)
        ddtw_ref[...] += split_dot(d_pre, proj_ref[rows, :rank], (0, 0), swapped=True)
        part = split_dot(d_pre, dtwt_ref[...], (1, 0))
        found = dot(s_mix[...], s_even[...], (1, 1)).reshape(span, 2, SEGS, part_ref.shape[1])
        odd = pltpu.roll(found[:, 1].reshape(size, part_ref.shape[1]), 1, 1)
        part_ref[rows, :] = (part + found[:, 0].reshape(size, part_ref.shape[1]) + odd).astype(bf16)

    @pl.when(turn == 2 * turns - 1)
    def _():
        put_pieces(me_ref, (pmine_ref, pother_ref), part_ref)
        sums = [jnp.sum(s_drate[i], axis=0, keepdims=True) for i in range(states * groups)]
        rows = [jnp.concatenate(sums[n * groups : (n + 1) * groups], axis=1) for n in range(states)]
        dalog_ref[...] = jnp.concatenate(rows, axis=0) * s_rate[...] * (1.0 / LOG2E)


def scan_span(steps):
    return math.gcd(steps, 32)


def wide_slots(steps, span, states):
    turns = steps // span
    return turns if turns * 2 * states * span * SEGS * 128 * 4 <= 16 * MIB else 1


def whole(*shape):
    return pl.BlockSpec(shape, lambda *t: (0,) * len(shape))


def like(*shape, dtype=f32):
    return jax.ShapeDtypeStruct(shape, dtype)


def about(micros):
    return pl.CostEstimate(flops=int(micros * 1.1e9), bytes_accessed=1 << 20, transcendentals=0)


SCALARS = pl.BlockSpec(memory_space=pltpu.SMEM)


def run_entry(me, starts, hidden_all, weight, gain, conv_w, conv_b, x_w, peers, span):
    total, width = hidden_all.shape
    taps, chans = conv_w.shape
    lanes = x_w.shape[1]
    steps = total // SEGS
    turns = steps // span
    size = span * SEGS
    piece = (peers // 2, total // peers, lanes)

    def segments(lanes):
        return pl.BlockSpec((SEGS, span, lanes), lambda t: (0, jnp.minimum(t, turns - 1), 0))

    mixed = pl.BlockSpec((size, chans), lambda t: (jnp.minimum(t, turns - 1), 0))

    def late(lanes):
        return pl.BlockSpec((size, lanes), lambda t: (jnp.where(t == turns, 0, jnp.maximum(t, min(1, turns - 1))), 0))

    normed, scale, *rest = pl.pallas_call(
        functools.partial(entry_kernel, span, taps),
        grid=(turns + 1,),
        in_specs=[
            SCALARS, SCALARS, segments(width), whole(width, 2 * chans), whole(1, width), whole(taps, chans), whole(1, chans),
            whole(chans, lanes),
        ],
        out_specs=[segments(width), segments(128), mixed, mixed, late(chans), late(chans)]
        + [whole(*piece)] * 2,
        out_shape=[like(SEGS, steps, width, dtype=bf16), like(SEGS, steps, 128)] + [like(total, chans, dtype=bf16)] * 3
        + [like(total, chans)] + [like(*piece, dtype=bf16)] * 2,
        scratch_shapes=[
            pltpu.VMEM((total + (taps - 1) * SEGS, chans), f32), pltpu.VMEM((size, size), bf16),
            pltpu.VMEM((total, lanes), bf16),
        ],
        compiler_params=pltpu.CompilerParams(vmem_limit_bytes=ROOM),
        cost_estimate=about(6 * total * chans / 262144),
        name="entry",
    )(me, starts, hidden_all.reshape(SEGS, steps, width), weight, gain, conv_w, conv_b, x_w)
    return (normed, scale.reshape(total, 128), *rest)


def run_gate(grad_all, out_w, gate, values, y, skip, span):
    total, width = grad_all.shape
    chans = gate.shape[1]
    steps = total // SEGS
    rows = pl.BlockSpec((span * SEGS, chans), lambda t: (t, 0))
    part = pl.BlockSpec((SEGS, span, chans), lambda t: (0, t, 0))
    full = pl.BlockSpec((SEGS, span, width), lambda t: (0, t, 0))
    natural = like(SEGS, steps, chans, dtype=bf16)
    branch, gated, dy, d_gate, d_skip = pl.pallas_call(
        functools.partial(gate_kernel, span),
        grid=(steps // span,),
        in_specs=[full, whole(chans, width), rows, rows, rows, whole(1, chans)],
        out_specs=[full, part, rows, part, whole(1, chans)],
        out_shape=[like(SEGS, steps, width, dtype=bf16), natural, like(total, chans), natural, like(1, chans)],
        scratch_shapes=[pltpu.VMEM((span * SEGS, span * SEGS), bf16)] * 2,
        compiler_params=pltpu.CompilerParams(vmem_limit_bytes=ROOM),
        cost_estimate=about(6 * total * chans / 262144),
        name="gate",
    )(grad_all.reshape(SEGS, steps, width), out_w, gate, values, y, skip)
    return branch.reshape(total, width), gated.reshape(total, chans), dy, d_gate.reshape(total, chans), d_skip


def run_scan(me, mine, other, values, gate, cut, grad_all, out_w, dt_weight, dt_weight_t, dt_bias, a_log_t, skip, states, span):
    total, chans = values.shape
    width_all = grad_all.shape[1]
    rank = dt_weight.shape[0]
    steps = total // SEGS
    groups, width = lane_groups(chans)
    count = states * groups
    lanes = mine.shape[2]
    turns = steps // span
    size = span * SEGS
    by_group = pltpu.VMEM((groups, total, width), f32)
    spread = pltpu.VMEM((states, total, 128), f32)
    held = pltpu.VMEM((count, SEGS, width), f32)
    order = pltpu.VMEM((size, size), bf16)
    part = pl.BlockSpec((SEGS, span, chans), lambda t: (0, jnp.minimum(t, turns - 1), 0))
    full = pl.BlockSpec((SEGS, span, width_all), lambda t: (0, jnp.minimum(t, turns - 1), 0))
    ahead = pl.BlockSpec((size, chans), lambda t: (jnp.minimum(t, turns - 1), 0))

    def behind(lanes):
        return pl.BlockSpec((size, lanes), lambda t: (jnp.minimum(turns, 2 * turns - t) - 1, 0))

    natural = like(SEGS, steps, chans, dtype=bf16)
    branch, gated, d_gate, *rest = pl.pallas_call(
        functools.partial(scan_kernel, rank, states, span),
        grid=(2 * turns,),
        in_specs=[
            SCALARS, whole(*mine.shape), whole(*mine.shape), whole(total, chans), ahead, whole(total, width), full,
            whole(chans, width_all), whole(rank, chans), whole(chans, lanes), whole(1, chans), whole(states, chans),
            whole(1, chans),
        ],
        out_specs=[
            full, part, part, whole(*mine.shape), whole(*mine.shape), behind(chans), whole(rank, chans), whole(1, chans),
            whole(states, chans), whole(1, chans),
        ],
        out_shape=[
            like(SEGS, steps, width_all, dtype=bf16), natural, natural, like(*mine.shape, dtype=bf16),
            like(*mine.shape, dtype=bf16), like(total, chans), like(rank, chans), like(1, chans), like(states, chans), like(1, chans),
        ],
        scratch_shapes=[
            by_group, by_group, by_group, by_group, pltpu.VMEM((steps + 1, count, SEGS, width), f32), spread, spread,
            pltpu.VMEM((size, chans), f32), pltpu.VMEM((states, chans), f32), held, held,
            pltpu.VMEM((2 * size, states * 128), bf16), pltpu.VMEM((lanes, 2 * states * 128), bf16), order, order,
            pltpu.VMEM((lanes, states * 128), bf16), pltpu.VMEM((total, lanes), bf16), pltpu.VMEM((total, lanes), bf16),
        ],
        compiler_params=pltpu.CompilerParams(vmem_limit_bytes=ROOM),
        cost_estimate=about(38),
        name="scan",
    )(me, mine, other, values, gate, cut, grad_all.reshape(SEGS, steps, width_all), out_w, dt_weight, dt_weight_t, dt_bias, a_log_t, skip)
    return (branch.reshape(total, width_all), gated.reshape(total, chans), d_gate.reshape(total, chans), *rest)


def run_exit(
    me, starts, mine, other, value_part, pre, x_in, values, conv_w, x_w, d_gate, weight, hidden_all, scale, gain,
    d_dtw, d_alog_t, d_dtb, d_skip, low_cols, small_rows, packs, peers,
    span,
):
    total, chans = x_in.shape
    taps = conv_w.shape[0]
    lanes = x_w.shape[1]
    width = hidden_all.shape[1]
    steps = total // SEGS
    size = math.gcd(total, 512)

    def rows(lanes):
        return pl.BlockSpec((size, lanes), lambda t: (jnp.maximum(t - 1, 0), 0))

    sides = width // chans
    packed = width // (peers * packs) % 16 == 0 and sides <= 16
    if packed:
        shapes = [like((width + small_rows) // packs + 16, chans, dtype=bf16)] * packs
    else:
        shapes = [like(width, chans, dtype=bf16), like(small_rows, chans, dtype=bf16), like(1, width)]
    d_normed, *out = pl.pallas_call(
        functools.partial(exit_kernel, span, taps, low_cols, packs, peers),
        grid=(1 + total // size,),
        in_specs=[SCALARS, SCALARS, whole(*mine.shape), whole(*mine.shape)] + [whole(total, chans)] * 4 + [
            whole(taps, chans), whole(chans, lanes), rows(chans), whole(width, 2 * chans), rows(width), rows(128),
            whole(1, width), whole(*d_dtw.shape), whole(*d_alog_t.shape), whole(1, chans), whole(1, chans),
        ],
        out_specs=[rows(width)] + [whole(*a.shape) for a in shapes],
        out_shape=[like(total, width, dtype=bf16), *shapes],
        scratch_shapes=[
            pltpu.VMEM((total + (taps - 1) * SEGS, chans), f32), pltpu.VMEM((SEGS, steps, chans), bf16),
            pltpu.VMEM((chans, width), f32), pltpu.VMEM((total + (taps - 1) * SEGS, lane_groups(chans)[1]), jnp.int32),
            pltpu.VMEM((small_rows, chans), f32), pltpu.VMEM((1, width), f32), pltpu.VMEM((total, lanes), bf16),
        ],
        compiler_params=pltpu.CompilerParams(vmem_limit_bytes=ROOM),
        cost_estimate=about(10 * total * chans / 262144),
        name="exit",
    )(
        me, starts, mine, other, value_part, pre, x_in, values, conv_w, x_w, d_gate, weight, hidden_all, scale, gain,
        d_dtw, d_alog_t, d_dtb, d_skip,
    )
    if packed:
        return d_normed, out
    late = jnp.moveaxis(out[0].reshape(peers, packs, -1, chans), 1, 0).reshape(packs, -1, chans)
    gain = jnp.pad(out[2].astype(bf16).reshape(sides, chans), ((0, -sides % 16), (0, 0)))
    late = [late, out[1].reshape(packs, -1, chans), jnp.broadcast_to(gain, (packs,) + gain.shape)]
    late = jnp.concatenate(late, axis=1)
    return d_normed, [pick(late, jnp.bitwise_xor(me[2], d)) for d in range(packs)]


def run_forward(proj, values, cut, dt_weight, dt_bias, a_log_t, states, span):
    total, chans = values.shape
    rank = dt_weight.shape[0]
    steps = total // SEGS
    groups, width = lane_groups(chans)
    count = states * groups
    lanes = proj.shape[1]
    slots = wide_slots(steps, span, states)
    by_group = pltpu.VMEM((groups, total, width), f32)
    return pl.pallas_call(
        functools.partial(forward_kernel, rank, states, span),
        grid=(steps // span,),
        in_specs=[
            whole(total, lanes), whole(total, chans), whole(total, width), whole(rank, chans), whole(1, chans),
            whole(states, chans),
        ],
        out_specs=[
            whole(total, chans), pl.BlockSpec((1, span + 1, count, SEGS, width), lambda t: (t, 0, 0, 0, 0)),
            whole(groups, total, width),
        ],
        out_shape=[
            like(total, chans), like(steps // span, span + 1, count, SEGS, width), like(groups, total, width),
        ],
        scratch_shapes=[
            by_group, by_group, pltpu.VMEM((states, chans), f32), pltpu.VMEM((count, SEGS, width), f32),
            pltpu.VMEM((groups, SEGS, width), f32),
            pltpu.VMEM((slots, states, span * SEGS, 128), f32),
            pltpu.VMEM((slots, states, span * SEGS, 128), f32), pltpu.VMEM((lanes, 2 * states * 128), bf16),
        ],
        compiler_params=pltpu.CompilerParams(vmem_limit_bytes=ROOM),
        cost_estimate=about(18 * total * chans / 262144),
        name="scan_forward",
    )(proj, values, cut, dt_weight, dt_bias, a_log_t)


def run_backward(proj, values, cut, dy, delta, dt_weight, dt_weight_t, dt_bias, a_log_t, skip, hist, states, span):
    total, chans = values.shape
    rank = dt_weight.shape[0]
    steps = total // SEGS
    groups, width = lane_groups(chans)
    count = states * groups
    lanes = proj.shape[1]
    turns = steps // span
    slots = wide_slots(steps, span, states)
    by_group = pltpu.VMEM((groups, total, width), f32)
    return pl.pallas_call(
        functools.partial(backward_kernel, rank, states, span),
        grid=(turns,),
        in_specs=[
            whole(total, lanes), whole(total, chans), whole(total, width), whole(total, chans), whole(groups, total, width),
            whole(rank, chans), whole(chans, lanes), whole(1, chans), whole(states, chans), whole(1, chans),
            pl.BlockSpec((1, span + 1, count, SEGS, width), lambda t: (turns - 1 - t, 0, 0, 0, 0)),
        ],
        out_specs=[
            whole(total, lanes), whole(total, chans), whole(rank, chans), whole(1, chans), whole(states, chans),
        ],
        out_shape=[
            like(total, lanes, dtype=bf16), like(total, chans), like(rank, chans), like(1, chans), like(states, chans),
        ],
        scratch_shapes=[
            by_group, by_group, by_group, pltpu.VMEM((states, chans), f32),
            pltpu.VMEM((count, SEGS, width), f32), pltpu.VMEM((groups, SEGS, width), f32),
            pltpu.VMEM((count, SEGS, width), f32),
            pltpu.VMEM((slots, states, span * SEGS, 128), f32),
            pltpu.VMEM((slots, states, span * SEGS, 128), f32), pltpu.VMEM((span * SEGS, 2 * states * 128), bf16),
            pltpu.VMEM((lanes, 2 * states * 128), bf16), pltpu.VMEM((span * SEGS, lanes), f32),
        ],
        compiler_params=pltpu.CompilerParams(vmem_limit_bytes=ROOM),
        cost_estimate=about(22 * total * chans / 262144),
        name="scan_backward",
    )(proj, values, cut, dy, delta, dt_weight, dt_weight_t, dt_bias, a_log_t, skip, hist)


def tree_sum(parts):
    parts = [p.astype(f32) for p in parts]
    while len(parts) > 1:
        parts = [parts[i] + parts[i + 1] for i in range(0, len(parts), 2)]
    return parts[0]


def swap(value, axis, mask):
    return lax.ppermute(value, axis, [(i, i ^ mask) for i in range(lax.axis_size(axis))])


def pick(blocks, index, dim=0):
    return lax.dynamic_index_in_dim(blocks, index, dim, keepdims=False)


def collected(pieces, me):
    out = jnp.zeros((len(pieces),) + pieces[0].shape, pieces[0].dtype)
    for d, piece in enumerate(pieces):
        out = lax.dynamic_update_index_in_dim(out, piece, me ^ d, 0)
    return out


def owned_parts(blocks, axis):
    return [blocks[0]] + [swap(block, axis, d) for d, block in enumerate(blocks) if d]


def by_distance(blocks, axis):
    me = lax.axis_index(axis)
    return [pick(blocks, jnp.bitwise_xor(me, d)) for d in range(blocks.shape[0])]


def collect(value, axis):
    me = lax.axis_index(axis)
    return collected([value] + [swap(value, axis, d) for d in range(1, lax.axis_size(axis))], me)


def sum_over_peers(mine, other, beside=()):
    peers = lax.axis_size("ch")
    if peers != 8:
        part = jnp.concatenate([mine, other], axis=0).reshape(peers, -1, mine.shape[2])
        got = lax.all_to_all(part, "ch", split_axis=0, concat_axis=0, tiled=True)
        part = lax.all_gather(got.astype(f32).sum(axis=0).astype(bf16), "ch", axis=0, tiled=True).reshape(part.shape)
        return part[: peers // 2], part[peers // 2 :], beside
    half = tree_sum([mine, swap(other, "ch", 1)]).astype(bf16)
    pieces = [half[0]] + [swap(half[d], "ch", 2 * d) for d in range(1, peers // 2)]
    own = tree_sum(pieces).astype(bf16)
    pieces = [own] + [swap(own, "ch", 2 * d) for d in range(1, peers // 2)]
    pieces, beside = lax.optimization_barrier((pieces, beside))
    half = jnp.stack(pieces)
    return half, swap(half, "ch", 1), beside


def in_order(mine, other, place):
    chips = jnp.bitwise_xor(jnp.arange(mine.shape[0]), place[1])
    halves = jnp.stack([mine[chips], other[chips]])
    return halves[jnp.bitwise_xor(jnp.arange(2), place[0])].reshape(-1, mine.shape[2])


def by_place(part, peers, place):
    halves = part.reshape(2, peers // 2, -1, part.shape[1])[jnp.bitwise_xor(jnp.arange(2), place[0])]
    halves = halves[:, jnp.bitwise_xor(jnp.arange(peers // 2), place[1])]
    return halves[0], halves[1]


def to_peers(blocks):
    return lax.all_to_all(blocks, "ch", split_axis=0, concat_axis=0, tiled=True)


def finish_kernel(
    parts, me_ref, *refs,
):
    n = parts
    late, outs, (cross_ref, branch_ref, dn_ref, hid_ref, grad_ref, gain_ref) = refs[:n], refs[n : 2 * n], refs[2 * n : 2 * n + 6]
    (out_ref, dh_ref, dgain_ref, din_ref, dcw_ref, dcb_ref, dxw_ref, ddtw_ref, ddtb_ref, dalog_ref, dskip_ref,
     dout_ref, s_small) = refs[2 * n + 6 :]
    chans = dcb_ref.shape[1]
    inner = din_ref.shape[1] // 2
    share = din_ref.shape[0] // n
    peers = inner // chans
    low_cols, rank, states, taps = dxw_ref.shape[0], ddtw_ref.shape[0], dalog_ref.shape[0], dcw_ref.shape[0]
    for d in range(n):
        who = jnp.bitwise_xor(me_ref[0], d)
        rows = block_rows(who, share)
        sides = dout_ref.shape[1] // chans
        out_share = dout_ref.shape[0] // n
        for p in range(peers):
            here = slice(p * share, (p + 1) * share)
            din_ref[rows, p * chans : (p + 1) * chans] = late[d][here, :].astype(f32)
            here = slice(sides * out_share + p * share, sides * out_share + (p + 1) * share)
            din_ref[rows, inner + p * chans : inner + (p + 1) * chans] = outs[d][here, :].astype(f32)
        small = late[d][share * peers :, :].astype(f32)
        s_small[block_rows(who, small.shape[0]), :] = small
        for i in range(sides):
            part = outs[d][i * out_share : (i + 1) * out_share, :].astype(f32)
            dout_ref[block_rows(who, out_share), i * chans : (i + 1) * chans] = part
    gain = jnp.sum(cross_ref[:, share:, :].astype(f32), axis=0)
    dgain_ref[...] = gain[:1, : dgain_ref.shape[1]]
    at = low_cols + rank
    ddtw_ref[...] = s_small[low_cols:at, :]
    dxw_ref[...] = s_small[:low_cols, :]
    tail = s_small[at:, :]
    dalog_ref[...] = tail[:states]
    dcw_ref[...] = tail[states : states + taps]
    at = states + taps
    dcb_ref[...] = tail[at : at + 1]
    ddtb_ref[...] = tail[at + 1 : at + 2]
    dskip_ref[...] = tail[at + 2 : at + 3]
    hidden = hid_ref[...].astype(f32)
    out_ref[...] = (hidden + branch_ref[...].astype(f32)).astype(bf16)
    scale = lax.rsqrt(jnp.mean(hidden * hidden, axis=1, keepdims=True) + eps)
    unit = hidden * scale
    d_unit = dn_ref[...].astype(f32) * gain_ref[...]
    mean = jnp.mean(d_unit * unit, axis=1, keepdims=True)
    dh_ref[...] = (grad_ref[...].astype(f32) + scale * (d_unit - unit * mean)).astype(bf16)


def run_finish(late, outs, cross, branch, d_normed, hidden, grad, gain, sizes, me):
    rows, width = hidden.shape
    low_cols, rank, states, taps, small_rows = sizes
    packs = len(late)
    chans = late[0].shape[1]
    in_rows = width // cross.shape[0]
    inner = chans * cross.shape[0]
    wide = [*late, *outs, cross, branch, d_normed, hidden, grad, gain]
    shapes = [
        like(rows, width, dtype=bf16), like(rows, width, dtype=bf16), like(1, in_rows), like(in_rows, 2 * inner),
        like(taps, chans), like(1, chans), like(low_cols, chans), like(rank, chans), like(1, chans),
        like(states, chans), like(1, chans), like(chans, width),
    ]
    return pl.pallas_call(
        functools.partial(finish_kernel, packs),
        grid=(1,),
        in_specs=[SCALARS] + [whole(*a.shape) for a in wide],
        out_specs=[whole(*a.shape) for a in shapes],
        out_shape=shapes,
        scratch_shapes=[pltpu.VMEM((small_rows, chans), f32)],
        compiler_params=pltpu.CompilerParams(vmem_limit_bytes=20 * MIB),
        cost_estimate=about(4),
        name="finish",
    )(me[None], *wide)


def finish_plain(late, outs, cross, branch, d_normed, hidden, grad, gain, sizes, me):
    low_cols, rank, states, taps, small_rows = sizes
    packs, peers, chans = len(late), cross.shape[0], late[0].shape[1]
    share = hidden.shape[1] // (peers * packs)
    late = collected(late, me).astype(f32)
    outs = collected(outs, me).astype(f32)
    sides = hidden.shape[1] // chans
    out_share = chans // packs
    halves = [late[:, : share * peers], outs[:, sides * out_share :]]
    halves = jnp.stack(halves).reshape(2, packs, peers, share, chans)
    d_in = jnp.transpose(halves, (1, 3, 0, 2, 4)).reshape(packs * share, 2 * peers * chans)
    d_out = outs[:, : sides * out_share].reshape(packs, sides, out_share, chans)
    d_out = jnp.moveaxis(d_out, 1, 2).reshape(chans, sides * chans)
    small = late[:, share * peers :].reshape(small_rows, chans)
    parts = []
    at = 0
    for count in (low_cols, rank, states, taps, 1, 1, 1):
        parts.append(small[at : at + count])
        at += count
    d_xw, d_dtw, d_alog, d_cw, d_cb, d_dtb, d_skip = parts
    d_gain = cross[:, share:].astype(f32).sum(axis=0).reshape(1, -1)[:, : share * packs]
    hidden = hidden.astype(f32)
    output = (hidden + branch.astype(f32)).astype(bf16)
    scale = lax.rsqrt(jnp.mean(hidden * hidden, axis=1, keepdims=True) + eps)
    unit = hidden * scale
    d_unit = d_normed.astype(f32) * gain
    mean = jnp.mean(d_unit * unit, axis=1, keepdims=True)
    d_hidden = (grad.astype(f32) + scale * (d_unit - unit * mean)).astype(bf16)
    return output, d_hidden, d_gain, d_in, d_cw, d_cb, d_xw, d_dtw, d_dtb, d_alog, d_skip, d_out


def on_device(
    hidden_in, norm_gain, in_weight, conv_weight, conv_bias, x_weight, dt_weight, dt_bias, a_log, skip, out_weight,
    lengths, resets, out_grad,
):
    peers = lax.axis_size("ch")
    packs = lax.axis_size("ctx")
    me = lax.axis_index("ch")
    rows, width = hidden_in.shape
    chans = out_weight.shape[0]
    taps = conv_weight.shape[1]
    rank, states = dt_weight.shape[0], a_log.shape[1]
    total = rows * peers

    hidden_all = lax.all_gather(hidden_in, "ch", axis=0, tiled=True)
    in_rows = in_weight.shape[0]
    share = in_rows // packs
    my_share = lax.dynamic_slice_in_dim(in_weight, lax.axis_index("ctx") * share, share, 0)
    got = to_peers(jnp.moveaxis(my_share.reshape(share, 2, peers, chans), 2, 0))
    grad_all = lax.all_gather(out_grad, "ch", axis=0, tiled=True)

    steps = total // SEGS
    span = scan_span(steps)
    low_cols = rank + 2 * states
    lanes = -(-low_cols // 128) * 128
    sizes = lengths[0]
    offsets = jnp.cumsum(sizes) - sizes
    where_in = context_place(offsets, jnp.arange(total, dtype=jnp.int32))
    cut = ((where_in == 0) | (resets == 1)).astype(bf16).reshape(SEGS, steps).T.reshape(total, 1)
    cut = jnp.broadcast_to(cut, (total, lane_groups(chans)[1]))
    starts = offsets[None, :]
    conv_w = lax.dynamic_slice_in_dim(conv_weight, me * chans, chans, 0).T
    conv_b = lax.dynamic_slice_in_dim(conv_bias, me * chans, chans, 0)[None, :]
    x_w = lax.dynamic_slice_in_dim(x_weight, me * chans, chans, 0)
    x_w = jnp.pad(x_w, ((0, 0), (0, lanes - low_cols)))

    near = peers == 8
    place = jnp.stack([me % 2 if near else 0 * me, me // 2 if near else 0 * me, lax.axis_index("ctx")])
    dt_w_t = jnp.pad(dt_weight.T, ((0, 0), (0, lanes - rank)))
    got, cut, dt_w_t, conv_w, conv_b, x_w, starts = lax.optimization_barrier(
        (got, cut, dt_w_t, conv_w, conv_b, x_w, starts)
    )
    shares = collect(got.reshape(peers, share, 2 * chans), "ctx")
    my_cols = jnp.moveaxis(shares, 0, 1).reshape(width, 2 * chans)

    normed, scale_all, x_in, gate, values, pre, *proj_part = run_entry(
        place, starts, hidden_all, my_cols, norm_gain[None, :], conv_w, conv_b, x_w, peers, span
    )
    mine, other, _ = sum_over_peers(*proj_part)

    a_log_t = a_log.T
    dt_b, skip_row = dt_bias[None, :], skip[None, :]
    if total * chans * states <= 1 << 22 and chans % 128 == 0:
        (
            branch_part, gated, d_gate, d_mine, d_other, value_part, d_dt_weight, d_dt_bias, d_a_log_t, d_skip,
        ) = run_scan(
            place, mine, other, values, gate, cut, grad_all, out_weight, dt_weight, dt_w_t, dt_b, a_log_t, skip_row,
            states, span,
        )
    else:
        proj = in_order(mine, other, place)
        y, hist, delta = run_forward(proj, values, cut, dt_weight, dt_b, a_log_t, states, span)
        branch_part, gated, dy, d_gate, d_skip = run_gate(grad_all, out_weight, gate, values, y, skip_row, span)
        d_part, value_part, d_dt_weight, d_dt_bias, d_a_log_t = run_backward(
            proj, values, cut, dy, delta, dt_weight, dt_w_t, dt_b, a_log_t, skip_row, hist, states, span
        )
        d_mine, d_other = by_place(d_part, peers, place)
    branch = lax.psum_scatter(branch_part, "ch", scatter_dimension=0, tiled=True)
    sides = width // chans
    out_share = chans // packs
    d_out = dot(gated, grad_all, (0, 0)).astype(bf16).reshape(packs, out_share, sides, chans)
    d_out = jnp.moveaxis(d_out, 2, 1).reshape(packs, out_share * sides, chans)
    d_in_gate = dot(normed.reshape(total, width), d_gate, (0, 0)).astype(bf16)

    def by_pack(d_in):
        return jnp.moveaxis(d_in.reshape(peers, packs, share, chans), 1, 0).reshape(packs, peers * share, chans)

    early = owned_parts(by_distance(jnp.concatenate([d_out, by_pack(d_in_gate)], axis=1), "ctx"), "ctx")

    mine, other, early = sum_over_peers(d_mine, d_other, early)
    early = tree_sum(early).astype(bf16)
    counts = (low_cols, rank, states, taps)
    small_rows = -(-(sum(counts) + 3) // (16 * packs)) * 16 * packs
    d_normed_part, late = run_exit(
        place, starts, mine, other, value_part, pre, x_in, values, conv_w, x_w, d_gate, my_cols, hidden_all, scale_all,
        norm_gain[None, :], d_dt_weight, d_a_log_t, d_dt_bias, d_skip, low_cols, small_rows, packs, peers, span,
    )
    d_normed = lax.psum_scatter(d_normed_part, "ch", scatter_dimension=0, tiled=True)

    late = tree_sum(owned_parts(late, "ctx")).astype(bf16)
    own_rows = peers * share
    gain_rows = late[own_rows + small_rows // packs :][:sides].reshape(peers, in_rows)
    pad_rows = -(-in_rows // chans)
    gain_rows = jnp.pad(gain_rows, ((0, 0), (0, pad_rows * chans - in_rows))).reshape(peers, pad_rows, chans)
    gain_rows = jnp.pad(gain_rows, ((0, 0), (0, -pad_rows % 16), (0, 0)))
    early_in = to_peers(early[out_share * sides :].reshape(peers, share, chans)).reshape(own_rows, chans)
    early = jnp.concatenate([early[: out_share * sides], early_in], axis=0)
    cross = jnp.concatenate([late[:own_rows].reshape(peers, share, chans), gain_rows], axis=1)
    early, _ = lax.optimization_barrier((early, cross))
    cross = to_peers(cross)
    outs = [early] + [swap(early, "ctx", d) for d in range(1, packs)]
    own = [cross[:, :share].reshape(own_rows, chans), late[own_rows : own_rows + small_rows // packs]]
    own = jnp.concatenate(own, axis=0)
    late = [own] + [swap(own, "ctx", d) for d in range(1, packs)]
    finish = run_finish if share % 16 == 0 and chans % 128 == 0 else finish_plain
    (
        output, d_hidden, gain_sum, in_sum, conv_w_sum, conv_b_sum, x_w_sum, dt_w_sum, dt_b_sum, a_log_sum, skip_sum,
        out_sum,
    ) = finish(
        late, outs, cross, branch, d_normed, hidden_in, out_grad, norm_gain[None, :], (*counts, small_rows),
        lax.axis_index("ctx"),
    )
    return (
        output, d_hidden, gain_sum[0], in_sum, conv_w_sum.T, conv_b_sum[0], x_w_sum.T, dt_w_sum, dt_b_sum[0],
        a_log_sum.T, skip_sum[0], out_sum,
    )


def solution(mesh):
    return jax.shard_map(
        on_device,
        mesh=mesh,
        in_specs=(
            P(("ctx", "ch"), None), P(), P("ch", None), P(), P(), P(), P(None, "ch"), P("ch"), P("ch", None),
            P("ch"), P("ch", None), P("ctx", None), P("ctx"), P(("ctx", "ch"), None),
        ),
        out_specs=(
            P(("ctx", "ch"), None), P(("ctx", "ch"), None), P("ch"), P("ch", None), P("ch", None), P("ch"),
            P("ch", None), P(None, "ch"), P("ch"), P("ch", None), P("ch"), P("ch", None),
        ),
        check_vma=False,
    )
```

```python
import functools
import math

import jax
import jax.numpy as jnp
from jax import lax
from jax.experimental import pallas as pl
from jax.experimental.pallas import tpu as pltpu
from jax.sharding import PartitionSpec as P

f32 = jnp.float32
bf16 = jnp.bfloat16
eps = 1e-05
LOG2E = 1.4426950408889634
CUT = 1e30
SEGS = 8
BATCH = 4
TOGETHER = 4
MIB = 1 << 20
ROOM = 56 * MIB


def silu(v):
    return v * jax.nn.sigmoid(v)


def silu_slope(v):
    sig = jax.nn.sigmoid(v)
    return sig * (1.0 + v * (1.0 - sig))


def context_place(offsets, places):
    begins = jnp.max(jnp.where(offsets[:, None] <= places[None, :], offsets[:, None], 0), axis=0)
    return places - begins


def dot(a, b, dims, precision=None):
    return lax.dot_general(a, b, ((dims[:1], dims[1:]), ((), ())), precision=precision, preferred_element_type=f32)


def lane_groups(chans):
    width = 128 if chans % 128 == 0 else chans
    return chans // width, width


def softplus(v):
    small = jnp.exp(-jnp.abs(v))
    series = small * (1.0 - small * (0.5 - small * (1.0 / 3.0)))
    return jnp.maximum(v, 0.0) + jnp.where(small < 0.01, series, jnp.log(1.0 + small))


def mixing(span, back):
    size = span * SEGS
    row = lax.broadcasted_iota(jnp.int32, (size, size), 0)
    column = lax.broadcasted_iota(jnp.int32, (size, size), 1)
    if back:
        hit = (row % span) * SEGS + row // span == column
    else:
        hit = (row % SEGS) * span + row // SEGS == column
    return hit.astype(f32).astype(bf16)


def context_positions(starts_ref, first_row, rows, steps, lanes):
    row = lax.broadcasted_iota(jnp.int32, (rows, lanes), 0) + first_row
    token = jnp.bitwise_and(row, SEGS - 1) * steps + jnp.right_shift(row, SEGS.bit_length() - 1)
    begin = jnp.zeros((rows, lanes), jnp.int32)
    for c in range(starts_ref.shape[1]):
        begin = jnp.where(starts_ref[0, c] <= token, starts_ref[0, c], begin)
    return token - begin


def split_dot(wide, narrow, dims, swapped=False):
    high = wide.astype(bf16)
    low = (wide - high.astype(f32)).astype(bf16)
    if swapped:
        return dot(narrow, high, dims) + dot(narrow, low, dims)
    return dot(high, narrow, dims) + dot(low, narrow, dims)


def put(ref, rows, value, groups, width):
    for g in range(groups):
        ref[g, rows, :] = value[:, g * width : (g + 1) * width]


def take(ref, rows, groups):
    return jnp.concatenate([ref[g, rows, :] for g in range(groups)], axis=1) if groups > 1 else ref[0, rows, :]


def piece_rows(me_ref, core, apart, chips, rows):
    place = jnp.bitwise_xor(me_ref[0], core) * chips + jnp.bitwise_xor(me_ref[1], apart)
    return pl.ds(pl.multiple_of(place * rows, rows), rows)


def put_pieces(me_ref, refs, source_ref):
    for core, ref in enumerate(refs):
        for apart in range(ref.shape[0]):
            ref[apart] = source_ref[piece_rows(me_ref, core, apart, ref.shape[0], ref.shape[1]), :]


def take_pieces(me_ref, refs, target_ref):
    for core, ref in enumerate(refs):
        for apart in range(ref.shape[0]):
            target_ref[piece_rows(me_ref, core, apart, ref.shape[0], ref.shape[1]), :] = ref[apart]


def block_rows(t, size):
    return pl.ds(pl.multiple_of(t * size, size), size)


def entry_kernel(
    span, taps, me_ref, starts_ref, hid_ref, w_ref, gain_ref, cw_ref, cb_ref, xw_ref,
    normed_ref, scale_ref, x_ref, gate_ref, val_ref, pre_ref, mine_ref, other_ref, s_x, s_mixing, s_proj,
):
    turn = pl.program_id(0)
    turns = pl.num_programs(0) - 1
    chans = x_ref.shape[1]
    size = span * SEGS
    steps = span * turns
    halo = (taps - 1) * SEGS
    groups, width = lane_groups(chans)

    @pl.when(turn == 0)
    def _():
        s_mixing[...] = mixing(span, False)

    @pl.when(turn < turns)
    def _():
        wide = hid_ref[...].astype(f32).reshape(size, hid_ref.shape[2])
        scale = lax.rsqrt(jnp.mean(wide * wide, axis=1, keepdims=True) + eps)
        normed = (wide * scale * gain_ref[...]).astype(bf16)
        normed_ref[...] = normed.reshape(normed_ref.shape)
        scale_ref[...] = jnp.broadcast_to(scale, (size, 128)).reshape(scale_ref.shape)
        mixed = dot(normed, w_ref[...], (1, 0)).astype(bf16)
        mixed = dot(s_mixing[...], mixed, (1, 0))
        x_ref[...] = mixed[:, :chans].astype(bf16)
        gate_ref[...] = mixed[:, chans:].astype(bf16)
        s_x[pl.ds(pl.multiple_of(turn * size + halo, SEGS), size), :] = mixed[:, :chans]

    @pl.when(turn == turns)
    def _():
        first = lax.broadcasted_iota(jnp.int32, (SEGS, chans), 0) == 0
        for j in range(taps - 1):
            last = s_x[pl.ds(pl.multiple_of(steps * SEGS + j * SEGS, SEGS), SEGS), :]
            s_x[j * SEGS : (j + 1) * SEGS, :] = jnp.where(first, 0.0, pltpu.roll(last, 1, 0))

    @pl.when(turn > 0)
    def _():
        t = jnp.where(turn == turns, 0, turn)
        place = jnp.concatenate([context_positions(starts_ref, t * size, size, steps, width)] * groups, axis=1)
        pre = cb_ref[...] + jnp.zeros((size, chans), f32)
        for k in range(taps):
            lag = taps - 1 - k
            at = pl.ds(pl.multiple_of(t * size + halo - lag * SEGS, SEGS), size)
            pre = pre + cw_ref[k : k + 1, :] * jnp.where(place >= lag, s_x[at, :], 0.0)
        pre_ref[...] = pre
        values = silu(pre).astype(bf16)
        val_ref[...] = values
        s_proj[block_rows(t, size), :] = dot(values, xw_ref[...], (1, 0)).astype(bf16)

    @pl.when(turn == turns)
    def _():
        put_pieces(me_ref, (mine_ref, other_ref), s_proj)


def gate_kernel(
    span, grad_ref, w_ref, gate_ref, val_ref, y_ref, skip_ref,
    branch_ref, gated_ref, dy_ref, dgate_ref, dskip_ref, s_in, s_out,
):
    turn = pl.program_id(0)
    size = span * SEGS

    @pl.when(turn == 0)
    def _():
        s_in[...] = mixing(span, False)
        s_out[...] = mixing(span, True)
        dskip_ref[...] = jnp.zeros_like(dskip_ref)

    vals = val_ref[...].astype(f32)
    gate = gate_ref[...].astype(f32)
    sig = jax.nn.sigmoid(gate)
    act = gate * sig
    scanned = y_ref[...] + skip_ref[...] * vals
    gated = dot(s_out[...], (scanned * act).astype(bf16), (1, 0)).astype(bf16)
    gated_ref[...] = gated.reshape(gated_ref.shape)
    branch_ref[...] = dot(gated, w_ref[...], (1, 0)).astype(bf16).reshape(branch_ref.shape)
    grad = grad_ref[...].reshape(size, grad_ref.shape[2])
    d_gated = dot(s_in[...], dot(grad, w_ref[...], (1, 1)).astype(bf16), (1, 0))
    dy = d_gated * act
    dy_ref[...] = dy
    d_gate = (d_gated * scanned * (sig * (1.0 + gate * (1.0 - sig)))).astype(bf16)
    d_gate = dot(s_out[...], d_gate, (1, 0)).astype(bf16)
    dgate_ref[...] = d_gate.reshape(dgate_ref.shape)
    dskip_ref[...] += jnp.sum(dy * vals, axis=0, keepdims=True)


def exit_kernel(
    span, taps, low_cols, packs, peers, me_ref, starts_ref, mine_ref, other_ref, part_ref, pre_ref, x_ref, val_ref, cw_ref, xw_ref, dgate_ref, w_ref,
    hid_ref, scale_ref, gain_ref, ddtw_ref, dalog_ref, ddtb_ref, dskip_ref,
    dn_ref, *refs,
):
    *out_refs, s_pre, s_dx, s_din, s_place, s_small, dgain_ref, dproj_ref = refs
    total, chans = x_ref.shape
    size = span * SEGS
    steps = total // SEGS
    turns = steps // span
    halo = (taps - 1) * SEGS
    groups, width = lane_groups(chans)
    turn = pl.program_id(0)

    @pl.when(turn == 0)
    def _():
        take_pieces(me_ref, (mine_ref, other_ref), dproj_ref)

        def first(t, carry):
            rows = block_rows(t, size)
            d_proj = dproj_ref[rows, :]
            d_values = part_ref[rows, :] + dot(d_proj, xw_ref[...], (1, 1))
            d_pre = d_values * silu_slope(pre_ref[rows, :])
            s_pre[rows, :] = d_pre
            s_place[rows, :] = context_positions(starts_ref, t * size, size, steps, width)
            d_bias, d_xw = carry
            return d_bias + jnp.sum(d_pre, axis=0, keepdims=True), d_xw + dot(d_proj, val_ref[rows, :], (0, 0))

        begin = (jnp.zeros((1, chans), f32), jnp.zeros((dproj_ref.shape[1], chans), f32))
        d_bias, d_xw = lax.fori_loop(0, turns, first, begin)
        s_place[total : total + halo, :] = context_positions(starts_ref, total, halo, steps, width)
        last = lax.broadcasted_iota(jnp.int32, (SEGS, chans), 0) == SEGS - 1
        for j in range(taps - 1):
            head = s_pre[j * SEGS : (j + 1) * SEGS, :]
            s_pre[total + j * SEGS : total + (j + 1) * SEGS, :] = jnp.where(last, 0.0, pltpu.roll(head, SEGS - 1, 0))
        back = mixing(span, True)

        def second(t, sums):
            rows = block_rows(t, size)
            x = x_ref[rows, :].astype(f32)
            d_x = jnp.zeros((size, chans), f32)
            out = []
            for k in range(taps):
                lag = taps - 1 - k
                at = pl.ds(pl.multiple_of(t * size + lag * SEGS, SEGS), size)
                valid = jnp.concatenate([s_place[at, :]] * groups, axis=1) >= lag
                later = jnp.where(valid, s_pre[at, :], 0.0)
                d_x = d_x + cw_ref[k : k + 1, :] * later
                out.append(sums[k] + jnp.sum(later * x, axis=0, keepdims=True))
            natural = dot(back, d_x.astype(bf16), (1, 0)).astype(bf16).reshape(SEGS, span, chans)
            s_dx[:, block_rows(t, span), :] = natural
            return tuple(out)

        sums = lax.fori_loop(0, turns, second, (jnp.zeros((1, chans), f32),) * taps)
        s_din[...] = jnp.zeros_like(s_din)
        dgain_ref[...] = jnp.zeros_like(dgain_ref)
        rest = [*sums, d_bias, ddtb_ref[...], dskip_ref[...]]
        small = [d_xw[:low_cols], ddtw_ref[...], dalog_ref[...], *rest]
        pad = s_small.shape[0] - sum(a.shape[0] for a in small)
        s_small[...] = jnp.concatenate([*small, jnp.zeros((pad, chans), f32)], axis=0)

    @pl.when(turn > 0)
    def _():
        rows = hid_ref.shape[0]
        per_segment = steps // rows if rows <= steps else 1
        if rows <= steps:
            here = pl.ds(pl.multiple_of((turn - 1) % per_segment * rows, rows), rows)
            d_x = s_dx[(turn - 1) // per_segment, here, :]
        else:
            d_x = s_dx[pl.ds((turn - 1) * (rows // steps), rows // steps)].reshape(rows, chans)
        both = jnp.concatenate([d_x, dgate_ref[...]], axis=1)
        d_normed = dot(both, w_ref[...], (1, 1)).astype(bf16)
        dn_ref[...] = d_normed
        unit = hid_ref[...].astype(f32) * jnp.concatenate([scale_ref[...]] * (hid_ref.shape[1] // 128), axis=1)
        dgain_ref[...] += jnp.sum(d_normed.astype(f32) * unit, axis=0, keepdims=True)
        s_din[...] += dot(d_x, (unit * gain_ref[...]).astype(bf16), (0, 0))

    @pl.when(turn == pl.num_programs(0) - 1)
    def _():
        d_in = s_din[...].T
        if len(out_refs) < packs:
            out_refs[0][...] = d_in.astype(bf16)
            out_refs[1][...] = s_small[...].astype(bf16)
            out_refs[2][...] = dgain_ref[...]
            return
        each = s_small.shape[0] // packs
        share = d_in.shape[0] // (peers * packs)
        sides = d_in.shape[0] // chans
        gain = [dgain_ref[:, i * chans : (i + 1) * chans] for i in range(sides)]
        gain = jnp.concatenate([*gain, jnp.zeros((16 - sides, chans), f32)], axis=0).astype(bf16)
        for d, ref in enumerate(out_refs):
            who = jnp.bitwise_xor(me_ref[2], d)
            ref[peers * share : peers * share + each, :] = s_small[block_rows(who, each), :].astype(bf16)
            ref[peers * share + each :, :] = gain
            for p in range(packs):

                @pl.when(who == p)
                def _():
                    for q in range(peers):
                        at = (q * packs + p) * share
                        ref[q * share : (q + 1) * share, :] = d_in[at : at + share].astype(bf16)


def prepare_spread(hot_ref, rank, states):
    hot_ref[...] = jnp.zeros_like(hot_ref)
    row = lax.broadcasted_iota(jnp.int32, (16, 128), 0)
    for n in range(2 * states):
        first = (rank + n) // 16 * 16
        hot_ref[first : first + 16, n * 128 : (n + 1) * 128] = (row + first == rank + n).astype(f32).astype(bf16)


def spread_pair(out_ref, slot, hot_ref, proj_ref, rows, first, pair):
    at = first * 128 + pair * 256
    both = dot(proj_ref[rows, :], hot_ref[:, pl.ds(at if isinstance(at, int) else pl.multiple_of(at, 256), 256)], (1, 0))
    out_ref[slot, 2 * pair] = both[:, :128]
    out_ref[slot, 2 * pair + 1] = both[:, 128:]


def sum_lanes(mix_ref, hot_ref):
    return dot(hot_ref[...], mix_ref[...], (1, 1)).T


def forward_kernel(
    rank, states, span, proj_ref, val_ref, cut_ref, dtw_ref, dtb_ref, alog_ref,
    y_ref, hist_ref, delta_ref, s_cut, s_dx, s_rate, s_state, s_sum, s_b, s_c, s_hot,
):
    total, chans = val_ref.shape
    steps = total // SEGS
    size = span * SEGS
    groups, width = lane_groups(chans)
    turn = pl.program_id(0)
    turns = steps // span
    slots = s_b.shape[0]
    half = states // 2
    count = span // BATCH

    def rate(n, g):
        return s_rate[n : n + 1, g * width : (g + 1) * width]

    @pl.when(turn == 0)
    def _():
        s_rate[...] = -jnp.exp(alog_ref[...]) * LOG2E
        prepare_spread(s_hot, rank, states)
        s_state[...] = jnp.zeros_like(s_state)
        s_sum[...] = jnp.zeros_like(s_sum)
        def block(t, carry):
            rows = block_rows(t, size)
            slot = t if slots > 1 else 0
            for pair in range(half):
                spread_pair(s_b, slot, s_hot, proj_ref, rows, 0, pair)
                spread_pair(s_c, slot, s_hot, proj_ref, rows, states, pair)
            delta = softplus(dot(proj_ref[rows, :rank], dtw_ref[...], (1, 0)) + dtb_ref[...])
            put(delta_ref, rows, delta, groups, width)
            cut = cut_ref[rows, :].astype(f32) * CUT
            put(s_cut, rows, delta + jnp.concatenate([cut] * groups, axis=1), groups, width)
            put(s_dx, rows, delta * val_ref[rows, :].astype(f32), groups, width)

            def sweep(q, carry):
                at = [block_rows(t * span + q * BATCH + j, SEGS) for j in range(BATCH)]
                here = [block_rows(q * BATCH + j, SEGS) for j in range(BATCH)]
                for g in range(groups):
                    cuts = [s_cut[g, at[j], :] for j in range(BATCH)]
                    dxs = [s_dx[g, at[j], :] for j in range(BATCH)]
                    s_sum[g] = s_sum[g] + sum(cuts)
                    for n in range(states):
                        held = s_state[n * groups + g]
                        for j in range(BATCH):
                            push = dxs[j] * s_b[slot, n, here[j], :width]
                            held = jnp.exp2(cuts[j] * rate(n, g)) * held + push
                        s_state[n * groups + g] = held
                return carry

            return lax.fori_loop(0, count, sweep, carry)

        lax.fori_loop(0, turns, block, 0)
        first = lax.broadcasted_iota(jnp.int32, (SEGS, width), 0) == 0
        for n in range(states):
            for g in range(groups):
                gain = jnp.exp2(s_sum[g] * rate(n, g))
                end = s_state[n * groups + g]
                start = jnp.zeros((SEGS, width), f32)
                for _ in range(SEGS - 1):
                    start = jnp.where(first, 0.0, pltpu.roll(gain * start + end, 1, 0))
                s_state[n * groups + g] = start

    slot = turn if slots > 1 else 0
    if slots == 1:
        for pair in range(half):
            spread_pair(s_b, 0, s_hot, proj_ref, block_rows(turn, size), 0, pair)
            spread_pair(s_c, 0, s_hot, proj_ref, block_rows(turn, size), states, pair)

    def sweep(q, carry):
        at = [block_rows(turn * span + q * BATCH + j, SEGS) for j in range(BATCH)]
        here = [block_rows(q * BATCH + j, SEGS) for j in range(BATCH)]
        for g in range(groups):
            cuts = [s_cut[g, at[j], :] for j in range(BATCH)]
            dxs = [s_dx[g, at[j], :] for j in range(BATCH)]
            ys = [None] * BATCH
            for n in range(states):
                i = n * groups + g
                held = s_state[i]
                for j in range(BATCH):
                    hist_ref[0, q * BATCH + j, i] = held
                    push = dxs[j] * s_b[slot, n, here[j], :width]
                    held = jnp.exp2(cuts[j] * rate(n, g)) * held + push
                    term = held * s_c[slot, n, here[j], :width]
                    ys[j] = term if n == 0 else ys[j] + term
                s_state[i] = held
            for j in range(BATCH):
                y_ref[at[j], g * width : (g + 1) * width] = ys[j]
        return carry

    lax.fori_loop(0, count, sweep, 0)
    hist_ref[0, span] = s_state[...]


def backward_kernel(
    rank, states, span, proj_ref, val_ref, cut_ref, dy_ref, delta_ref, dtw_ref, dtwt_ref, dtb_ref, alog_ref, skip_ref,
    hist_ref, part_ref, dval_ref, ddtw_ref, ddtb_ref, dalog_ref,
    s_cut, s_val, s_dd, s_rate, s_state, s_sum, s_drate, s_b, s_c, s_mix, s_hot, s_bc,
):
    total, chans = val_ref.shape
    steps = total // SEGS
    size = span * SEGS
    groups, width = lane_groups(chans)
    turns = steps // span
    turn = pl.program_id(0)
    place = turns - 1 - turn
    slots = s_b.shape[0]
    half = states // 2
    count = span // BATCH
    lane = [slice(g * width, (g + 1) * width) for g in range(groups)]

    def rate(n, g):
        return s_rate[n : n + 1, lane[g]]

    @pl.when(turn == 0)
    def _():
        s_rate[...] = -jnp.exp(alog_ref[...]) * LOG2E
        s_drate[...] = jnp.zeros_like(s_drate)
        s_state[...] = jnp.zeros_like(s_state)
        s_sum[...] = jnp.zeros_like(s_sum)
        if width < 128:
            s_mix[...] = jnp.zeros_like(s_mix)
        prepare_spread(s_hot, rank, states)
        def block(turned, carry):
            t = turns - 1 - turned
            rows = block_rows(t, size)
            slot = t if slots > 1 else 0
            for pair in range(half):
                spread_pair(s_b, slot, s_hot, proj_ref, rows, 0, pair)
                spread_pair(s_c, slot, s_hot, proj_ref, rows, states, pair)
            cut = cut_ref[rows, :].astype(f32) * CUT
            delta = take(delta_ref, rows, groups)
            put(s_cut, rows, delta + jnp.concatenate([cut] * groups, axis=1), groups, width)
            put(s_val, rows, val_ref[rows, :].astype(f32), groups, width)

            def sweep(q, carry):
                k = span - BATCH - q * BATCH
                at = [block_rows(t * span + k + j, SEGS) for j in range(BATCH)]
                here = [block_rows(k + j, SEGS) for j in range(BATCH)]
                for g in range(groups):
                    cuts = [s_cut[g, at[j], :] for j in range(BATCH)]
                    dys = [dy_ref[at[j], lane[g]] for j in range(BATCH)]
                    s_sum[g] = s_sum[g] + sum(cuts)
                    for n in range(states):
                        held = s_state[n * groups + g]
                        for j in reversed(range(BATCH)):
                            held = dys[j] * s_c[slot, n, here[j], :width] + held
                            held = jnp.exp2(cuts[j] * rate(n, g)) * held
                        s_state[n * groups + g] = held
                return carry

            return lax.fori_loop(0, count, sweep, carry)

        lax.fori_loop(0, turns, block, 0)
        last = lax.broadcasted_iota(jnp.int32, (SEGS, width), 0) == SEGS - 1
        for n in range(states):
            for g in range(groups):
                gain = jnp.exp2(s_sum[g] * rate(n, g))
                end = s_state[n * groups + g]
                start = jnp.zeros((SEGS, width), f32)
                for _ in range(SEGS - 1):
                    start = jnp.where(last, 0.0, pltpu.roll(gain * start + end, SEGS - 1, 0))
                s_state[n * groups + g] = start

    slot = place if slots > 1 else 0
    if slots == 1:
        for pair in range(half):
            spread_pair(s_b, 0, s_hot, proj_ref, block_rows(place, size), 0, pair)
            spread_pair(s_c, 0, s_hot, proj_ref, block_rows(place, size), states, pair)

    def sweep(q, carry):
        k = span - BATCH - q * BATCH
        at = [block_rows(place * span + k + j, SEGS) for j in range(BATCH)]
        here = [block_rows(k + j, SEGS) for j in range(BATCH)]
        each = [(j, g) for j in range(BATCH) for g in range(groups)]
        cuts = {(j, g): s_cut[g, at[j], :] for j, g in each}
        deltas = {(j, g): delta_ref[g, at[j], :] for j, g in each}
        vals = {(j, g): s_val[g, at[j], :] for j, g in each}
        dys = {(j, g): dy_ref[at[j], lane[g]] for j, g in each}
        dxs = {e: deltas[e] * vals[e] for e in each}
        by_rate, by_b = {}, {}
        for first in range(0, states, TOGETHER):
            some = [(n, g) for n in range(first, first + TOGETHER) for g in range(groups)]
            held = {(n, g): s_state[n * groups + g] for n, g in some}
            d_rate = {(n, g): s_drate[n * groups + g] for n, g in some}
            after = {(n, g): hist_ref[0, k + BATCH, n * groups + g] for n, g in some}
            mix = {}
            for j in reversed(range(BATCH)):
                for n, g in some:
                    e, i = (j, g), (n, g)
                    b_n = s_b[slot, n, here[j], :width]
                    c_n = s_c[slot, n, here[j], :width]
                    before = hist_ref[0, k + j, n * groups + g]
                    lam = dys[e] * c_n + held[i]
                    held[i] = jnp.exp2(cuts[e] * rate(n, g)) * lam
                    through = held[i] * before
                    d_rate[i] = d_rate[i] + through * deltas[e]
                    terms = (through * rate(n, g), lam * b_n, lam * dxs[e], dys[e] * after[i])
                    by_rate[e] = by_rate[e] + terms[0] if e in by_rate else terms[0]
                    by_b[e] = by_b[e] + terms[1] if e in by_b else terms[1]
                    for m, term in ((n, terms[2]), (states + n, terms[3])):
                        mix[j, m] = mix[j, m] + term if (j, m) in mix else term
                    after[i] = before
                if j % 2 == 0:
                    two = pl.ds(pl.multiple_of((k + j) * SEGS, 2 * SEGS), 2 * SEGS)
                    for n in range(first, first + TOGETHER):
                        for m in (n, states + n):
                            value = jnp.concatenate([mix[j, m], mix[j + 1, m]], axis=0).astype(bf16)
                            s_mix[two, m * 128 : m * 128 + width] = value
            for n, g in some:
                s_state[n * groups + g] = held[n, g]
                s_drate[n * groups + g] = d_rate[n, g]
        for j, g in each:
            e = (j, g)
            s_dd[g, at[j], :] = by_rate[e] * (1.0 / LOG2E) + by_b[e] * vals[e]
            dval_ref[at[j], lane[g]] = by_b[e] * deltas[e] + dys[e] * skip_ref[:, lane[g]]
        return carry

    lax.fori_loop(0, count, sweep, 0)
    rows = block_rows(place, size)
    s_bc[...] = sum_lanes(s_mix, s_hot)
    pre = dot(proj_ref[rows, :rank], dtw_ref[...], (1, 0)) + dtb_ref[...]
    d_pre = take(s_dd, rows, groups) * jax.nn.sigmoid(pre)
    d_bias = jnp.sum(d_pre, axis=0, keepdims=True)
    d_dtw = split_dot(d_pre, proj_ref[rows, :rank], (0, 0), swapped=True)
    part = split_dot(d_pre, dtwt_ref[...], (1, 0))
    part_ref[rows, :] = (part + s_bc[...]).astype(bf16)

    @pl.when(turn == 0)
    def _():
        ddtb_ref[...] = d_bias
        ddtw_ref[...] = d_dtw

    @pl.when(turn > 0)
    def _():
        ddtb_ref[...] += d_bias
        ddtw_ref[...] += d_dtw

    @pl.when(turn == turns - 1)
    def _():
        sums = [jnp.sum(s_drate[i], axis=0, keepdims=True) for i in range(states * groups)]
        rows = [jnp.concatenate(sums[n * groups : (n + 1) * groups], axis=1) for n in range(states)]
        dalog_ref[...] = jnp.concatenate(rows, axis=0) * s_rate[...] * (1.0 / LOG2E)


def scan_kernel(
    rank, states, span, me_ref, mine_ref, other_ref, val_ref, gate_ref, cut_ref, grad_ref, w_ref, dtw_ref, dtwt_ref, dtb_ref, alog_ref,
    skip_ref, branch_ref, gated_ref, dgate_ref, pmine_ref, pother_ref, dval_ref, ddtw_ref, ddtb_ref, dalog_ref, dskip_ref,
    s_cut, s_delta, s_val, s_dy, s_hist, s_b, s_c, s_y, s_rate, s_state, s_drate, s_mix, s_hot, s_in, s_out, s_even, proj_ref, part_ref,
):
    total, chans = val_ref.shape
    steps = total // SEGS
    size = span * SEGS
    groups, width = lane_groups(chans)
    pairs = [(n, g) for n in range(states) for g in range(groups)]
    every = range(groups)
    lane = [slice(g * width, (g + 1) * width) for g in every]
    turns = steps // span
    turn = pl.program_id(0)
    zero = jnp.zeros((SEGS, width), f32)
    sublane = lax.broadcasted_iota(jnp.int32, (SEGS, width), 0)

    def decay(cut, n, g):
        return jnp.exp2(cut * s_rate[n : n + 1, lane[g]])

    def chained(ends, sums, edge, shift):
        for n, g in pairs:
            gain = decay(sums[g], n, g)
            end = ends[n * groups + g]
            start = zero
            for _ in range(SEGS - 1):
                start = jnp.where(sublane == edge, 0.0, pltpu.roll(gain * start + end, shift, 0))
            s_state[n * groups + g] = start

    @pl.when(turn == 0)
    def _():
        s_rate[...] = -jnp.exp(alog_ref[...]) * LOG2E
        s_drate[...] = jnp.zeros_like(s_drate)
        dskip_ref[...] = jnp.zeros_like(dskip_ref)
        s_in[...] = mixing(span, False)
        s_out[...] = mixing(span, True)
        prepare_spread(s_hot, rank, states)
        take_pieces(me_ref, (mine_ref, other_ref), proj_ref)
        s_even[...] = jnp.concatenate([s_hot[:, n * 128 : (n + 1) * 128] for n in range(0, 2 * states, 2)], axis=1)

        def fill(t, carry):
            rows = block_rows(t, size)
            for n in range(0, states, 2):
                for ref, first in ((s_b, n), (s_c, states + n)):
                    both = dot(proj_ref[rows, :], s_hot[:, first * 128 : (first + 2) * 128], (1, 0))
                    ref[n, rows, :] = both[:, :128]
                    ref[n + 1, rows, :] = both[:, 128:]
            delta = softplus(dot(proj_ref[rows, :rank], dtw_ref[...], (1, 0)) + dtb_ref[...])
            cut = cut_ref[rows, :].astype(f32) * CUT
            put(s_delta, rows, delta, groups, width)
            put(s_cut, rows, delta + jnp.concatenate([cut] * groups, axis=1), groups, width)
            put(s_val, rows, val_ref[rows, :].astype(f32), groups, width)
            return carry

        lax.fori_loop(0, turns, fill, 0)

        def sweep(i, carry):
            held, sums = carry
            at = block_rows(i, SEGS)
            cuts = [s_cut[g, at, :] for g in every]
            dxs = [s_delta[g, at, :] * s_val[g, at, :] for g in every]
            out = [decay(cuts[g], n, g) * held[n * groups + g] + dxs[g] * s_b[n, at, :width] for n, g in pairs]
            return tuple(out), tuple(sums[g] + cuts[g] for g in every)

        begin = ((zero,) * len(pairs), (zero,) * groups)
        chained(*lax.fori_loop(0, steps, sweep, begin, unroll=16), 0, 1)

    @pl.when(turn < turns)
    def _():

        def sweep(k, held):
            i = turn * span + k
            at = block_rows(i, SEGS)
            cuts = [s_cut[g, at, :] for g in every]
            dxs = [s_delta[g, at, :] * s_val[g, at, :] for g in every]
            ys = [zero] * groups
            out = []
            for n in range(states):
                b_n = s_b[n, at, :width]
                c_n = s_c[n, at, :width]
                for g in every:
                    old = held[n * groups + g]
                    s_hist[i, n * groups + g] = old
                    new = decay(cuts[g], n, g) * old + dxs[g] * b_n
                    out.append(new)
                    ys[g] = ys[g] + new * c_n
            for g in every:
                s_y[block_rows(k, SEGS), lane[g]] = ys[g]
            return tuple(out)

        held = lax.fori_loop(0, span, sweep, tuple(s_state[j] for j in range(len(pairs))), unroll=16)
        for j in range(len(pairs)):
            s_state[j] = held[j]

        @pl.when(turn == turns - 1)
        def _():
            s_hist[steps] = s_state[...]

        rows = block_rows(turn, size)
        vals = val_ref[rows, :].astype(f32)
        gate = gate_ref[...].astype(f32)
        sig = jax.nn.sigmoid(gate)
        act = gate * sig
        scanned = s_y[...] + skip_ref[...] * vals
        grad = grad_ref[...].reshape(size, grad_ref.shape[2])
        d_gated = dot(s_in[...], dot(grad, w_ref[...], (1, 1)).astype(bf16), (1, 0))
        dy = d_gated * act
        put(s_dy, rows, dy, groups, width)
        d_gate = d_gated * scanned * (sig * (1.0 + gate * (1.0 - sig)))
        both = jnp.concatenate([(scanned * act).astype(bf16), d_gate.astype(bf16)], axis=1)
        both = dot(s_out[...], both, (1, 0)).astype(bf16)
        gated_ref[...] = both[:, :chans].reshape(gated_ref.shape)
        dgate_ref[...] = both[:, chans:].reshape(dgate_ref.shape)
        branch_ref[...] = dot(both[:, :chans], w_ref[...], (1, 0)).astype(bf16).reshape(branch_ref.shape)
        dskip_ref[...] += jnp.sum(dy * vals, axis=0, keepdims=True)

    @pl.when(turn == turns)
    def _():
        ddtb_ref[...] = jnp.zeros_like(ddtb_ref)
        ddtw_ref[...] = jnp.zeros_like(ddtw_ref)

        def sweep(back, carry):
            held, sums = carry
            at = block_rows(steps - 1 - back, SEGS)
            cuts = [s_cut[g, at, :] for g in every]
            dys = [s_dy[g, at, :] for g in every]
            out = []
            for n, g in pairs:
                lam = dys[g] * s_c[n, at, :width] + held[n * groups + g]
                out.append(decay(cuts[g], n, g) * lam)
            return tuple(out), tuple(sums[g] + cuts[g] for g in every)

        begin = ((zero,) * len(pairs), (zero,) * groups)
        chained(*lax.fori_loop(0, steps, sweep, begin, unroll=16), SEGS - 1, SEGS - 1)

    @pl.when(turn >= turns)
    def _():
        place = 2 * turns - 1 - turn

        def sweep(back, held):
            k = span - 1 - back
            i = place * span + k
            at = block_rows(i, SEGS)
            cuts = [s_cut[g, at, :] for g in every]
            deltas = [s_delta[g, at, :] for g in every]
            vals = [s_val[g, at, :] for g in every]
            dys = [s_dy[g, at, :] for g in every]
            dxs = [deltas[g] * vals[g] for g in every]
            by_rate = [zero] * groups
            by_b = [zero] * groups
            out = []
            mixes = {}
            for n in range(states):
                b_n = s_b[n, at, :width]
                c_n = s_c[n, at, :width]
                mix = mix_c = None
                for g in every:
                    j = n * groups + g
                    lam = dys[g] * c_n + held[j]
                    onward = decay(cuts[g], n, g) * lam
                    out.append(onward)
                    through = onward * s_hist[i, j]
                    by_rate[g] = by_rate[g] + through * s_rate[n : n + 1, lane[g]]
                    by_b[g] = by_b[g] + lam * b_n
                    s_drate[j] = s_drate[j] + through * deltas[g]
                    term, term_c = lam * dxs[g], dys[g] * s_hist[i + 1, j]
                    mix = term if mix is None else mix + term
                    mix_c = term_c if mix_c is None else mix_c + term_c
                mixes[n], mixes[states + n] = mix, mix_c
                if n % 2:
                    for first in (n - 1, states + n - 1):
                        two = jnp.concatenate([mixes[first], mixes[first + 1]], axis=0).astype(bf16)
                        s_mix[block_rows(k, 2 * SEGS), first * 64 : first * 64 + width] = two
            for g in every:
                s_cut[g, at, :] = by_rate[g] * (1.0 / LOG2E) + by_b[g] * vals[g]
                dval_ref[block_rows(k, SEGS), lane[g]] = by_b[g] * deltas[g] + dys[g] * skip_ref[:, lane[g]]
            return tuple(out)

        held = lax.fori_loop(0, span, sweep, tuple(s_state[j] for j in range(len(pairs))), unroll=16)
        for j in range(len(pairs)):
            s_state[j] = held[j]
        rows = block_rows(place, size)
        pre = dot(proj_ref[rows, :rank], dtw_ref[...], (1, 0)) + dtb_ref[...]
        d_pre = take(s_cut, rows, groups) * jax.nn.sigmoid(pre)
        ddtb_ref[...] += jnp.sum(d_pre, axis=0, keepdims=True)
        ddtw_ref[...] += split_dot(d_pre, proj_ref[rows, :rank], (0, 0), swapped=True)
        part = split_dot(d_pre, dtwt_ref[...], (1, 0))
        found = dot(s_mix[...], s_even[...], (1, 1)).reshape(span, 2, SEGS, part_ref.shape[1])
        odd = pltpu.roll(found[:, 1].reshape(size, part_ref.shape[1]), 1, 1)
        part_ref[rows, :] = (part + found[:, 0].reshape(size, part_ref.shape[1]) + odd).astype(bf16)

    @pl.when(turn == 2 * turns - 1)
    def _():
        put_pieces(me_ref, (pmine_ref, pother_ref), part_ref)
        sums = [jnp.sum(s_drate[i], axis=0, keepdims=True) for i in range(states * groups)]
        rows = [jnp.concatenate(sums[n * groups : (n + 1) * groups], axis=1) for n in range(states)]
        dalog_ref[...] = jnp.concatenate(rows, axis=0) * s_rate[...] * (1.0 / LOG2E)


def scan_span(steps):
    return math.gcd(steps, 32)


def wide_slots(steps, span, states):
    turns = steps // span
    return turns if turns * 2 * states * span * SEGS * 128 * 4 <= 16 * MIB else 1


def whole(*shape):
    return pl.BlockSpec(shape, lambda *t: (0,) * len(shape))


def like(*shape, dtype=f32):
    return jax.ShapeDtypeStruct(shape, dtype)


def about(micros):
    return pl.CostEstimate(flops=int(micros * 1.1e9), bytes_accessed=1 << 20, transcendentals=0)


SCALARS = pl.BlockSpec(memory_space=pltpu.SMEM)


def run_entry(me, starts, hidden_all, weight, gain, conv_w, conv_b, x_w, peers, span):
    total, width = hidden_all.shape
    taps, chans = conv_w.shape
    lanes = x_w.shape[1]
    steps = total // SEGS
    turns = steps // span
    size = span * SEGS
    piece = (peers // 2, total // peers, lanes)

    def segments(lanes):
        return pl.BlockSpec((SEGS, span, lanes), lambda t: (0, jnp.minimum(t, turns - 1), 0))

    mixed = pl.BlockSpec((size, chans), lambda t: (jnp.minimum(t, turns - 1), 0))

    def late(lanes):
        return pl.BlockSpec((size, lanes), lambda t: (jnp.where(t == turns, 0, jnp.maximum(t, min(1, turns - 1))), 0))

    normed, scale, *rest = pl.pallas_call(
        functools.partial(entry_kernel, span, taps),
        grid=(turns + 1,),
        in_specs=[
            SCALARS, SCALARS, segments(width), whole(width, 2 * chans), whole(1, width), whole(taps, chans), whole(1, chans),
            whole(chans, lanes),
        ],
        out_specs=[segments(width), segments(128), mixed, mixed, late(chans), late(chans)]
        + [whole(*piece)] * 2,
        out_shape=[like(SEGS, steps, width, dtype=bf16), like(SEGS, steps, 128)] + [like(total, chans, dtype=bf16)] * 3
        + [like(total, chans)] + [like(*piece, dtype=bf16)] * 2,
        scratch_shapes=[
            pltpu.VMEM((total + (taps - 1) * SEGS, chans), f32), pltpu.VMEM((size, size), bf16),
            pltpu.VMEM((total, lanes), bf16),
        ],
        compiler_params=pltpu.CompilerParams(vmem_limit_bytes=ROOM),
        cost_estimate=about(6 * total * chans / 262144),
        name="entry",
    )(me, starts, hidden_all.reshape(SEGS, steps, width), weight, gain, conv_w, conv_b, x_w)
    return (normed, scale.reshape(total, 128), *rest)


def run_gate(grad_all, out_w, gate, values, y, skip, span):
    total, width = grad_all.shape
    chans = gate.shape[1]
    steps = total // SEGS
    rows = pl.BlockSpec((span * SEGS, chans), lambda t: (t, 0))
    part = pl.BlockSpec((SEGS, span, chans), lambda t: (0, t, 0))
    full = pl.BlockSpec((SEGS, span, width), lambda t: (0, t, 0))
    natural = like(SEGS, steps, chans, dtype=bf16)
    branch, gated, dy, d_gate, d_skip = pl.pallas_call(
        functools.partial(gate_kernel, span),
        grid=(steps // span,),
        in_specs=[full, whole(chans, width), rows, rows, rows, whole(1, chans)],
        out_specs=[full, part, rows, part, whole(1, chans)],
        out_shape=[like(SEGS, steps, width, dtype=bf16), natural, like(total, chans), natural, like(1, chans)],
        scratch_shapes=[pltpu.VMEM((span * SEGS, span * SEGS), bf16)] * 2,
        compiler_params=pltpu.CompilerParams(vmem_limit_bytes=ROOM),
        cost_estimate=about(6 * total * chans / 262144),
        name="gate",
    )(grad_all.reshape(SEGS, steps, width), out_w, gate, values, y, skip)
    return branch.reshape(total, width), gated.reshape(total, chans), dy, d_gate.reshape(total, chans), d_skip


def run_scan(me, mine, other, values, gate, cut, grad_all, out_w, dt_weight, dt_weight_t, dt_bias, a_log_t, skip, states, span):
    total, chans = values.shape
    width_all = grad_all.shape[1]
    rank = dt_weight.shape[0]
    steps = total // SEGS
    groups, width = lane_groups(chans)
    count = states * groups
    lanes = mine.shape[2]
    turns = steps // span
    size = span * SEGS
    by_group = pltpu.VMEM((groups, total, width), f32)
    spread = pltpu.VMEM((states, total, 128), f32)
    held = pltpu.VMEM((count, SEGS, width), f32)
    order = pltpu.VMEM((size, size), bf16)
    part = pl.BlockSpec((SEGS, span, chans), lambda t: (0, jnp.minimum(t, turns - 1), 0))
    full = pl.BlockSpec((SEGS, span, width_all), lambda t: (0, jnp.minimum(t, turns - 1), 0))
    ahead = pl.BlockSpec((size, chans), lambda t: (jnp.minimum(t, turns - 1), 0))

    def behind(lanes):
        return pl.BlockSpec((size, lanes), lambda t: (jnp.minimum(turns, 2 * turns - t) - 1, 0))

    natural = like(SEGS, steps, chans, dtype=bf16)
    branch, gated, d_gate, *rest = pl.pallas_call(
        functools.partial(scan_kernel, rank, states, span),
        grid=(2 * turns,),
        in_specs=[
            SCALARS, whole(*mine.shape), whole(*mine.shape), whole(total, chans), ahead, whole(total, width), full,
            whole(chans, width_all), whole(rank, chans), whole(chans, lanes), whole(1, chans), whole(states, chans),
            whole(1, chans),
        ],
        out_specs=[
            full, part, part, whole(*mine.shape), whole(*mine.shape), behind(chans), whole(rank, chans), whole(1, chans),
            whole(states, chans), whole(1, chans),
        ],
        out_shape=[
            like(SEGS, steps, width_all, dtype=bf16), natural, natural, like(*mine.shape, dtype=bf16),
            like(*mine.shape, dtype=bf16), like(total, chans), like(rank, chans), like(1, chans), like(states, chans), like(1, chans),
        ],
        scratch_shapes=[
            by_group, by_group, by_group, by_group, pltpu.VMEM((steps + 1, count, SEGS, width), f32), spread, spread,
            pltpu.VMEM((size, chans), f32), pltpu.VMEM((states, chans), f32), held, held,
            pltpu.VMEM((2 * size, states * 128), bf16), pltpu.VMEM((lanes, 2 * states * 128), bf16), order, order,
            pltpu.VMEM((lanes, states * 128), bf16), pltpu.VMEM((total, lanes), bf16), pltpu.VMEM((total, lanes), bf16),
        ],
        compiler_params=pltpu.CompilerParams(vmem_limit_bytes=ROOM),
        cost_estimate=about(38),
        name="scan",
    )(me, mine, other, values, gate, cut, grad_all.reshape(SEGS, steps, width_all), out_w, dt_weight, dt_weight_t, dt_bias, a_log_t, skip)
    return (branch.reshape(total, width_all), gated.reshape(total, chans), d_gate.reshape(total, chans), *rest)


def run_exit(
    me, starts, mine, other, value_part, pre, x_in, values, conv_w, x_w, d_gate, weight, hidden_all, scale, gain,
    d_dtw, d_alog_t, d_dtb, d_skip, low_cols, small_rows, packs, peers,
    span,
):
    total, chans = x_in.shape
    taps = conv_w.shape[0]
    lanes = x_w.shape[1]
    width = hidden_all.shape[1]
    steps = total // SEGS
    size = math.gcd(total, 512)

    def rows(lanes):
        return pl.BlockSpec((size, lanes), lambda t: (jnp.maximum(t - 1, 0), 0))

    sides = width // chans
    packed = width // (peers * packs) % 16 == 0 and sides <= 16
    if packed:
        shapes = [like((width + small_rows) // packs + 16, chans, dtype=bf16)] * packs
    else:
        shapes = [like(width, chans, dtype=bf16), like(small_rows, chans, dtype=bf16), like(1, width)]
    d_normed, *out = pl.pallas_call(
        functools.partial(exit_kernel, span, taps, low_cols, packs, peers),
        grid=(1 + total // size,),
        in_specs=[SCALARS, SCALARS, whole(*mine.shape), whole(*mine.shape)] + [whole(total, chans)] * 4 + [
            whole(taps, chans), whole(chans, lanes), rows(chans), whole(width, 2 * chans), rows(width), rows(128),
            whole(1, width), whole(*d_dtw.shape), whole(*d_alog_t.shape), whole(1, chans), whole(1, chans),
        ],
        out_specs=[rows(width)] + [whole(*a.shape) for a in shapes],
        out_shape=[like(total, width, dtype=bf16), *shapes],
        scratch_shapes=[
            pltpu.VMEM((total + (taps - 1) * SEGS, chans), f32), pltpu.VMEM((SEGS, steps, chans), bf16),
            pltpu.VMEM((chans, width), f32), pltpu.VMEM((total + (taps - 1) * SEGS, lane_groups(chans)[1]), jnp.int32),
            pltpu.VMEM((small_rows, chans), f32), pltpu.VMEM((1, width), f32), pltpu.VMEM((total, lanes), bf16),
        ],
        compiler_params=pltpu.CompilerParams(vmem_limit_bytes=ROOM),
        cost_estimate=about(10 * total * chans / 262144),
        name="exit",
    )(
        me, starts, mine, other, value_part, pre, x_in, values, conv_w, x_w, d_gate, weight, hidden_all, scale, gain,
        d_dtw, d_alog_t, d_dtb, d_skip,
    )
    if packed:
        return d_normed, out
    late = jnp.moveaxis(out[0].reshape(peers, packs, -1, chans), 1, 0).reshape(packs, -1, chans)
    gain = jnp.pad(out[2].astype(bf16).reshape(sides, chans), ((0, -sides % 16), (0, 0)))
    late = [late, out[1].reshape(packs, -1, chans), jnp.broadcast_to(gain, (packs,) + gain.shape)]
    late = jnp.concatenate(late, axis=1)
    return d_normed, [pick(late, jnp.bitwise_xor(me[2], d)) for d in range(packs)]


def run_forward(proj, values, cut, dt_weight, dt_bias, a_log_t, states, span):
    total, chans = values.shape
    rank = dt_weight.shape[0]
    steps = total // SEGS
    groups, width = lane_groups(chans)
    count = states * groups
    lanes = proj.shape[1]
    slots = wide_slots(steps, span, states)
    by_group = pltpu.VMEM((groups, total, width), f32)
    return pl.pallas_call(
        functools.partial(forward_kernel, rank, states, span),
        grid=(steps // span,),
        in_specs=[
            whole(total, lanes), whole(total, chans), whole(total, width), whole(rank, chans), whole(1, chans),
            whole(states, chans),
        ],
        out_specs=[
            whole(total, chans), pl.BlockSpec((1, span + 1, count, SEGS, width), lambda t: (t, 0, 0, 0, 0)),
            whole(groups, total, width),
        ],
        out_shape=[
            like(total, chans), like(steps // span, span + 1, count, SEGS, width), like(groups, total, width),
        ],
        scratch_shapes=[
            by_group, by_group, pltpu.VMEM((states, chans), f32), pltpu.VMEM((count, SEGS, width), f32),
            pltpu.VMEM((groups, SEGS, width), f32),
            pltpu.VMEM((slots, states, span * SEGS, 128), f32),
            pltpu.VMEM((slots, states, span * SEGS, 128), f32), pltpu.VMEM((lanes, 2 * states * 128), bf16),
        ],
        compiler_params=pltpu.CompilerParams(vmem_limit_bytes=ROOM),
        cost_estimate=about(18 * total * chans / 262144),
        name="scan_forward",
    )(proj, values, cut, dt_weight, dt_bias, a_log_t)


def run_backward(proj, values, cut, dy, delta, dt_weight, dt_weight_t, dt_bias, a_log_t, skip, hist, states, span):
    total, chans = values.shape
    rank = dt_weight.shape[0]
    steps = total // SEGS
    groups, width = lane_groups(chans)
    count = states * groups
    lanes = proj.shape[1]
    turns = steps // span
    slots = wide_slots(steps, span, states)
    by_group = pltpu.VMEM((groups, total, width), f32)
    return pl.pallas_call(
        functools.partial(backward_kernel, rank, states, span),
        grid=(turns,),
        in_specs=[
            whole(total, lanes), whole(total, chans), whole(total, width), whole(total, chans), whole(groups, total, width),
            whole(rank, chans), whole(chans, lanes), whole(1, chans), whole(states, chans), whole(1, chans),
            pl.BlockSpec((1, span + 1, count, SEGS, width), lambda t: (turns - 1 - t, 0, 0, 0, 0)),
        ],
        out_specs=[
            whole(total, lanes), whole(total, chans), whole(rank, chans), whole(1, chans), whole(states, chans),
        ],
        out_shape=[
            like(total, lanes, dtype=bf16), like(total, chans), like(rank, chans), like(1, chans), like(states, chans),
        ],
        scratch_shapes=[
            by_group, by_group, by_group, pltpu.VMEM((states, chans), f32),
            pltpu.VMEM((count, SEGS, width), f32), pltpu.VMEM((groups, SEGS, width), f32),
            pltpu.VMEM((count, SEGS, width), f32),
            pltpu.VMEM((slots, states, span * SEGS, 128), f32),
            pltpu.VMEM((slots, states, span * SEGS, 128), f32), pltpu.VMEM((span * SEGS, 2 * states * 128), bf16),
            pltpu.VMEM((lanes, 2 * states * 128), bf16), pltpu.VMEM((span * SEGS, lanes), f32),
        ],
        compiler_params=pltpu.CompilerParams(vmem_limit_bytes=ROOM),
        cost_estimate=about(22 * total * chans / 262144),
        name="scan_backward",
    )(proj, values, cut, dy, delta, dt_weight, dt_weight_t, dt_bias, a_log_t, skip, hist)


def tree_sum(parts):
    parts = [p.astype(f32) for p in parts]
    while len(parts) > 1:
        parts = [parts[i] + parts[i + 1] for i in range(0, len(parts), 2)]
    return parts[0]


def swap(value, axis, mask):
    return lax.ppermute(value, axis, [(i, i ^ mask) for i in range(lax.axis_size(axis))])


def pick(blocks, index, dim=0):
    return lax.dynamic_index_in_dim(blocks, index, dim, keepdims=False)


def collected(pieces, me):
    out = jnp.zeros((len(pieces),) + pieces[0].shape, pieces[0].dtype)
    for d, piece in enumerate(pieces):
        out = lax.dynamic_update_index_in_dim(out, piece, me ^ d, 0)
    return out


def owned_parts(blocks, axis):
    got = {d: swap(blocks[d], axis, d) for d in reversed(range(1, len(blocks)))}
    return [blocks[0]] + [got[d] for d in range(1, len(blocks))]


def by_distance(blocks, axis):
    me = lax.axis_index(axis)
    return [pick(blocks, jnp.bitwise_xor(me, d)) for d in range(blocks.shape[0])]


def collect(value, axis):
    me = lax.axis_index(axis)
    return collected([value] + [swap(value, axis, d) for d in range(1, lax.axis_size(axis))], me)


def sum_over_peers(mine, other, beside=()):
    peers = lax.axis_size("ch")
    if peers != 8:
        part = jnp.concatenate([mine, other], axis=0).reshape(peers, -1, mine.shape[2])
        got = lax.all_to_all(part, "ch", split_axis=0, concat_axis=0, tiled=True)
        part = lax.all_gather(got.astype(f32).sum(axis=0).astype(bf16), "ch", axis=0, tiled=True).reshape(part.shape)
        return part[: peers // 2], part[peers // 2 :], beside
    half = tree_sum([mine, swap(other, "ch", 1)]).astype(bf16)
    pieces = [half[0]] + [swap(half[d], "ch", 2 * d) for d in range(1, peers // 2)]
    own = tree_sum(pieces).astype(bf16)
    pieces = [own] + [swap(own, "ch", 2 * d) for d in range(1, peers // 2)]
    pieces, beside = lax.optimization_barrier((pieces, beside))
    half = jnp.stack(pieces)
    return half, swap(half, "ch", 1), beside


def in_order(mine, other, place):
    chips = jnp.bitwise_xor(jnp.arange(mine.shape[0]), place[1])
    halves = jnp.stack([mine[chips], other[chips]])
    return halves[jnp.bitwise_xor(jnp.arange(2), place[0])].reshape(-1, mine.shape[2])


def by_place(part, peers, place):
    halves = part.reshape(2, peers // 2, -1, part.shape[1])[jnp.bitwise_xor(jnp.arange(2), place[0])]
    halves = halves[:, jnp.bitwise_xor(jnp.arange(peers // 2), place[1])]
    return halves[0], halves[1]


def to_peers(blocks):
    return lax.all_to_all(blocks, "ch", split_axis=0, concat_axis=0, tiled=True)


def finish_kernel(
    parts, me_ref, *refs,
):
    n = parts
    late, outs, (cross_ref, branch_ref, dn_ref, hid_ref, grad_ref, gain_ref) = refs[:n], refs[n : 2 * n], refs[2 * n : 2 * n + 6]
    (out_ref, dh_ref, dgain_ref, din_ref, dcw_ref, dcb_ref, dxw_ref, ddtw_ref, ddtb_ref, dalog_ref, dskip_ref,
     dout_ref, s_small) = refs[2 * n + 6 :]
    chans = dcb_ref.shape[1]
    inner = din_ref.shape[1] // 2
    share = din_ref.shape[0] // n
    peers = inner // chans
    low_cols, rank, states, taps = dxw_ref.shape[0], ddtw_ref.shape[0], dalog_ref.shape[0], dcw_ref.shape[0]
    for d in range(n):
        who = jnp.bitwise_xor(me_ref[0], d)
        rows = block_rows(who, share)
        sides = dout_ref.shape[1] // chans
        out_share = dout_ref.shape[0] // n
        for p in range(peers):
            here = slice(p * share, (p + 1) * share)
            din_ref[rows, p * chans : (p + 1) * chans] = late[d][here, :].astype(f32)
            here = slice(sides * out_share + p * share, sides * out_share + (p + 1) * share)
            din_ref[rows, inner + p * chans : inner + (p + 1) * chans] = outs[d][here, :].astype(f32)
        small = late[d][share * peers :, :].astype(f32)
        s_small[block_rows(who, small.shape[0]), :] = small
        for i in range(sides):
            part = outs[d][i * out_share : (i + 1) * out_share, :].astype(f32)
            dout_ref[block_rows(who, out_share), i * chans : (i + 1) * chans] = part
    gain = jnp.sum(cross_ref[:, share:, :].astype(f32), axis=0)
    dgain_ref[...] = gain[:1, : dgain_ref.shape[1]]
    at = low_cols + rank
    ddtw_ref[...] = s_small[low_cols:at, :]
    dxw_ref[...] = s_small[:low_cols, :]
    tail = s_small[at:, :]
    dalog_ref[...] = tail[:states]
    dcw_ref[...] = tail[states : states + taps]
    at = states + taps
    dcb_ref[...] = tail[at : at + 1]
    ddtb_ref[...] = tail[at + 1 : at + 2]
    dskip_ref[...] = tail[at + 2 : at + 3]
    hidden = hid_ref[...].astype(f32)
    out_ref[...] = (hidden + branch_ref[...].astype(f32)).astype(bf16)
    scale = lax.rsqrt(jnp.mean(hidden * hidden, axis=1, keepdims=True) + eps)
    unit = hidden * scale
    d_unit = dn_ref[...].astype(f32) * gain_ref[...]
    mean = jnp.mean(d_unit * unit, axis=1, keepdims=True)
    dh_ref[...] = (grad_ref[...].astype(f32) + scale * (d_unit - unit * mean)).astype(bf16)


def run_finish(late, outs, cross, branch, d_normed, hidden, grad, gain, sizes, me):
    rows, width = hidden.shape
    low_cols, rank, states, taps, small_rows = sizes
    packs = len(late)
    chans = late[0].shape[1]
    in_rows = width // cross.shape[0]
    inner = chans * cross.shape[0]
    wide = [*late, *outs, cross, branch, d_normed, hidden, grad, gain]
    shapes = [
        like(rows, width, dtype=bf16), like(rows, width, dtype=bf16), like(1, in_rows), like(in_rows, 2 * inner),
        like(taps, chans), like(1, chans), like(low_cols, chans), like(rank, chans), like(1, chans),
        like(states, chans), like(1, chans), like(chans, width),
    ]
    return pl.pallas_call(
        functools.partial(finish_kernel, packs),
        grid=(1,),
        in_specs=[SCALARS] + [whole(*a.shape) for a in wide],
        out_specs=[whole(*a.shape) for a in shapes],
        out_shape=shapes,
        scratch_shapes=[pltpu.VMEM((small_rows, chans), f32)],
        compiler_params=pltpu.CompilerParams(vmem_limit_bytes=20 * MIB),
        cost_estimate=about(4),
        name="finish",
    )(me[None], *wide)


def finish_plain(late, outs, cross, branch, d_normed, hidden, grad, gain, sizes, me):
    low_cols, rank, states, taps, small_rows = sizes
    packs, peers, chans = len(late), cross.shape[0], late[0].shape[1]
    share = hidden.shape[1] // (peers * packs)
    late = collected(late, me).astype(f32)
    outs = collected(outs, me).astype(f32)
    sides = hidden.shape[1] // chans
    out_share = chans // packs
    halves = [late[:, : share * peers], outs[:, sides * out_share :]]
    halves = jnp.stack(halves).reshape(2, packs, peers, share, chans)
    d_in = jnp.transpose(halves, (1, 3, 0, 2, 4)).reshape(packs * share, 2 * peers * chans)
    d_out = outs[:, : sides * out_share].reshape(packs, sides, out_share, chans)
    d_out = jnp.moveaxis(d_out, 1, 2).reshape(chans, sides * chans)
    small = late[:, share * peers :].reshape(small_rows, chans)
    parts = []
    at = 0
    for count in (low_cols, rank, states, taps, 1, 1, 1):
        parts.append(small[at : at + count])
        at += count
    d_xw, d_dtw, d_alog, d_cw, d_cb, d_dtb, d_skip = parts
    d_gain = cross[:, share:].astype(f32).sum(axis=0).reshape(1, -1)[:, : share * packs]
    hidden = hidden.astype(f32)
    output = (hidden + branch.astype(f32)).astype(bf16)
    scale = lax.rsqrt(jnp.mean(hidden * hidden, axis=1, keepdims=True) + eps)
    unit = hidden * scale
    d_unit = d_normed.astype(f32) * gain
    mean = jnp.mean(d_unit * unit, axis=1, keepdims=True)
    d_hidden = (grad.astype(f32) + scale * (d_unit - unit * mean)).astype(bf16)
    return output, d_hidden, d_gain, d_in, d_cw, d_cb, d_xw, d_dtw, d_dtb, d_alog, d_skip, d_out


def on_device(
    hidden_in, norm_gain, in_weight, conv_weight, conv_bias, x_weight, dt_weight, dt_bias, a_log, skip, out_weight,
    lengths, resets, out_grad,
):
    peers = lax.axis_size("ch")
    packs = lax.axis_size("ctx")
    me = lax.axis_index("ch")
    rows, width = hidden_in.shape
    chans = out_weight.shape[0]
    taps = conv_weight.shape[1]
    rank, states = dt_weight.shape[0], a_log.shape[1]
    total = rows * peers

    hidden_all = lax.all_gather(hidden_in, "ch", axis=0, tiled=True)
    in_rows = in_weight.shape[0]
    share = in_rows // packs
    my_share = lax.dynamic_slice_in_dim(in_weight, lax.axis_index("ctx") * share, share, 0)
    got = to_peers(jnp.moveaxis(my_share.reshape(share, 2, peers, chans), 2, 0))
    grad_all = lax.all_gather(out_grad, "ch", axis=0, tiled=True)

    steps = total // SEGS
    span = scan_span(steps)
    low_cols = rank + 2 * states
    lanes = -(-low_cols // 128) * 128
    sizes = lengths[0]
    offsets = jnp.cumsum(sizes) - sizes
    where_in = context_place(offsets, jnp.arange(total, dtype=jnp.int32))
    cut = ((where_in == 0) | (resets == 1)).astype(bf16).reshape(SEGS, steps).T.reshape(total, 1)
    cut = jnp.broadcast_to(cut, (total, lane_groups(chans)[1]))
    starts = offsets[None, :]
    conv_w = lax.dynamic_slice_in_dim(conv_weight, me * chans, chans, 0).T
    conv_b = lax.dynamic_slice_in_dim(conv_bias, me * chans, chans, 0)[None, :]
    x_w = lax.dynamic_slice_in_dim(x_weight, me * chans, chans, 0)
    x_w = jnp.pad(x_w, ((0, 0), (0, lanes - low_cols)))

    near = peers == 8
    place = jnp.stack([me % 2 if near else 0 * me, me // 2 if near else 0 * me, lax.axis_index("ctx")])
    dt_w_t = jnp.pad(dt_weight.T, ((0, 0), (0, lanes - rank)))
    got, cut, dt_w_t, conv_w, conv_b, x_w, starts = lax.optimization_barrier(
        (got, cut, dt_w_t, conv_w, conv_b, x_w, starts)
    )
    shares = collect(got.reshape(peers, share, 2 * chans), "ctx")
    my_cols = jnp.moveaxis(shares, 0, 1).reshape(width, 2 * chans)

    normed, scale_all, x_in, gate, values, pre, *proj_part = run_entry(
        place, starts, hidden_all, my_cols, norm_gain[None, :], conv_w, conv_b, x_w, peers, span
    )
    mine, other, _ = sum_over_peers(*proj_part)

    a_log_t = a_log.T
    dt_b, skip_row = dt_bias[None, :], skip[None, :]
    if total * chans * states <= 1 << 22 and chans % 128 == 0:
        (
            branch_part, gated, d_gate, d_mine, d_other, value_part, d_dt_weight, d_dt_bias, d_a_log_t, d_skip,
        ) = run_scan(
            place, mine, other, values, gate, cut, grad_all, out_weight, dt_weight, dt_w_t, dt_b, a_log_t, skip_row,
            states, span,
        )
    else:
        proj = in_order(mine, other, place)
        y, hist, delta = run_forward(proj, values, cut, dt_weight, dt_b, a_log_t, states, span)
        branch_part, gated, dy, d_gate, d_skip = run_gate(grad_all, out_weight, gate, values, y, skip_row, span)
        d_part, value_part, d_dt_weight, d_dt_bias, d_a_log_t = run_backward(
            proj, values, cut, dy, delta, dt_weight, dt_w_t, dt_b, a_log_t, skip_row, hist, states, span
        )
        d_mine, d_other = by_place(d_part, peers, place)
    branch = lax.psum_scatter(branch_part, "ch", scatter_dimension=0, tiled=True)
    sides = width // chans
    out_share = chans // packs
    d_out = dot(gated, grad_all, (0, 0)).astype(bf16).reshape(packs, out_share, sides, chans)
    d_out = jnp.moveaxis(d_out, 2, 1).reshape(packs, out_share * sides, chans)
    d_in_gate = dot(normed.reshape(total, width), d_gate, (0, 0)).astype(bf16)

    def by_pack(d_in):
        return jnp.moveaxis(d_in.reshape(peers, packs, share, chans), 1, 0).reshape(packs, peers * share, chans)

    early = owned_parts(by_distance(jnp.concatenate([d_out, by_pack(d_in_gate)], axis=1), "ctx"), "ctx")

    mine, other, early = sum_over_peers(d_mine, d_other, early)
    early = tree_sum(early).astype(bf16)
    counts = (low_cols, rank, states, taps)
    small_rows = -(-(sum(counts) + 3) // (16 * packs)) * 16 * packs
    d_normed_part, late = run_exit(
        place, starts, mine, other, value_part, pre, x_in, values, conv_w, x_w, d_gate, my_cols, hidden_all, scale_all,
        norm_gain[None, :], d_dt_weight, d_a_log_t, d_dt_bias, d_skip, low_cols, small_rows, packs, peers, span,
    )
    d_normed = lax.psum_scatter(d_normed_part, "ch", scatter_dimension=0, tiled=True)

    late = tree_sum(owned_parts(late, "ctx")).astype(bf16)
    own_rows = peers * share
    gain_rows = late[own_rows + small_rows // packs :][:sides].reshape(peers, in_rows)
    pad_rows = -(-in_rows // chans)
    gain_rows = jnp.pad(gain_rows, ((0, 0), (0, pad_rows * chans - in_rows))).reshape(peers, pad_rows, chans)
    gain_rows = jnp.pad(gain_rows, ((0, 0), (0, -pad_rows % 16), (0, 0)))
    early_in = to_peers(early[out_share * sides :].reshape(peers, share, chans)).reshape(own_rows, chans)
    early = jnp.concatenate([early[: out_share * sides], early_in], axis=0)
    cross = jnp.concatenate([late[:own_rows].reshape(peers, share, chans), gain_rows], axis=1)
    early, _ = lax.optimization_barrier((early, cross))
    cross = to_peers(cross)
    outs = [early] + [swap(early, "ctx", d) for d in range(1, packs)]
    own = [cross[:, :share].reshape(own_rows, chans), late[own_rows : own_rows + small_rows // packs]]
    own = jnp.concatenate(own, axis=0)
    late = [own] + [swap(own, "ctx", d) for d in range(1, packs)]
    finish = run_finish if share % 16 == 0 and chans % 128 == 0 else finish_plain
    (
        output, d_hidden, gain_sum, in_sum, conv_w_sum, conv_b_sum, x_w_sum, dt_w_sum, dt_b_sum, a_log_sum, skip_sum,
        out_sum,
    ) = finish(
        late, outs, cross, branch, d_normed, hidden_in, out_grad, norm_gain[None, :], (*counts, small_rows),
        lax.axis_index("ctx"),
    )
    return (
        output, d_hidden, gain_sum[0], in_sum, conv_w_sum.T, conv_b_sum[0], x_w_sum.T, dt_w_sum, dt_b_sum[0],
        a_log_sum.T, skip_sum[0], out_sum,
    )


def solution(mesh):
    return jax.shard_map(
        on_device,
        mesh=mesh,
        in_specs=(
            P(("ctx", "ch"), None), P(), P("ch", None), P(), P(), P(), P(None, "ch"), P("ch"), P("ch", None),
            P("ch"), P("ch", None), P("ctx", None), P("ctx"), P(("ctx", "ch"), None),
        ),
        out_specs=(
            P(("ctx", "ch"), None), P(("ctx", "ch"), None), P("ch"), P("ch", None), P("ch", None), P("ch"),
            P("ch", None), P(None, "ch"), P("ch"), P("ch", None), P("ch"), P("ch", None),
        ),
        check_vma=False,
    )
```
